32 devices in a mesh: seq: 8 (over y, x, core), head: 4 (over z).
Axes of the slice: x: 2, y: 2, z: 4, core: 2. Of those that a mesh axis runs over, the one named last changes fastest.
Arguments:
- query_rows: bfloat16 [2048, 8, 128], P('seq', 'head'), may hold values from -20 to 20
- key_rows: bfloat16 [2048, 8, 128], P('seq', 'head'), may hold values from -20 to 20
- value_rows: bfloat16 [2048, 8, 128], P('seq', 'head'), may hold values from -6 to 6
- cotangent: bfloat16 [2048, 8, 128], P('seq', 'head'), may hold values from -6 to 6
- norm_gain: float32 [8, 128], P('head'), may hold values from 0.5 to 2
- offsets: int32 [8], P('head'), may hold values from 0 to 31, as said below
Outputs:
- query_grad: bfloat16 [2048, 8, 128], P('seq', 'head')
- key_grad: bfloat16 [2048, 8, 128], P('seq', 'head')
- value_grad: bfloat16 [2048, 8, 128], P('seq', 'head')
The draws below stay inside these ranges and needn't reach their ends.
Inputs may be any that keep to these rules, and one draw needn't show every extreme that they name: The heads' offsets are distinct.
All inputs are finite; a program needn't handle non-finite values.
Results may differ from the reference program's by a relative error of at most 0.018.
Values may be sent and summed in bfloat16 or wider, within the bound.
A program may use at most 128 MiB of HBM per device.

```python
import math
import jax
import jax.numpy as jnp
from jax import lax

HD = 128
HEADS = 8
RATE2 = 4
RATE3 = 16
RATE4 = 32
TOKENS = 2048
SEL = 64


def paired_rows(key):
    full_shape = (TOKENS, HEADS, HD)
    queries = jnp.clip(jax.random.normal(jax.random.fold_in(key, 11), full_shape, jnp.float32), -6.0, 6.0)
    keyed = jnp.clip(jax.random.normal(jax.random.fold_in(key, 12), full_shape, jnp.float32), -6.0, 6.0)
    return (queries, keyed)


def draw_query_rows(key, part):
    return paired_rows(key)[0].astype(jnp.bfloat16)


def draw_key_rows(key, part):
    return paired_rows(key)[1].astype(jnp.bfloat16)


def draw_offsets(key, part):
    inner = jax.random.permutation(jax.random.fold_in(key, 21), 30).astype(jnp.int32) + 1
    chosen = jnp.concatenate([jnp.array([0, 31], dtype=jnp.int32), inner[:HEADS - 2]])
    return jax.random.permutation(jax.random.fold_in(key, 22), chosen).astype(jnp.int32)


def level_of(rng, extent, shards, least, largest):
    def one(axis_at, shards_of):
        draws = jax.random.uniform(jax.random.fold_in(jax.random.fold_in(rng, 6), axis_at), (shards_of,), jnp.float32, least / len(shards), largest / len(shards))
        return jnp.repeat(jnp.exp(draws), extent[axis_at] // shards_of).reshape((-1,) + (1,) * (len(extent) - axis_at - 1))

    factor_of = one(*shards[0])
    for cut in shards[1:]:
        factor_of = factor_of * one(*cut)
    return factor_of


def normal_values(own_key, extent, deviation, limit, pieces=(), held_as=jnp.bfloat16):
    values = jax.random.normal(own_key, extent, jnp.float32) * deviation
    if len(pieces) > 0:
        values = level_of(own_key, extent, pieces, -0.22, 0.18) * values
    return jnp.clip(values, min=-limit, max=limit).astype(held_as)


def setup_inputs(seed: int = 0) -> dict:
    streams_of = jax.random.split(jax.random.key(seed), 7)
    return {
        "query_rows": draw_query_rows(jax.random.fold_in(streams_of[6], 71), 0),
        "key_rows": draw_key_rows(jax.random.fold_in(streams_of[6], 71), 0),
        "value_rows": normal_values(streams_of[2], (TOKENS, HEADS, HD), 1.0, 6.0, ((0, 8), (1, 4))),
        "cotangent": normal_values(streams_of[3], (TOKENS, HEADS, HD), 1.0, 6.0, ((0, 8), (1, 4))),
        "norm_gain": jnp.clip(jnp.exp(math.log(2.0) - 1.3862944 * jax.random.uniform(streams_of[4], (HEADS, HD), jnp.float32) ** level_of(streams_of[4], (HEADS, HD), ((0, 4),), -0.2, 0.2)), 0.5, 2.0),
        "offsets": draw_offsets(jax.random.fold_in(streams_of[6], 71), 0),
    }


neg_fill = -1e+30
epsilon = 1e-05

def level_places(offsets, stride):
    seg_len = stride * SEL
    seg_total = TOKENS // seg_len
    starts = jnp.arange(seg_total, dtype=jnp.int32) * seg_len
    inside = stride * jnp.arange(SEL, dtype=jnp.int32)
    shifted = (offsets % stride).astype(jnp.int32)
    return starts[None, :, None] + inside[None, None, :] + shifted[:, None, None]

def reference(query_rows, key_rows, value_rows, cotangent, norm_gain, offsets):
    score_scale = HD ** (-0.5)
    lower = jnp.tril(jnp.ones((SEL, SEL), dtype=bool))
    level_rates = (1, RATE2, RATE3, RATE4)

    def group_scores(query_grp, key_grp):
        raw = jnp.dot(query_grp, key_grp.T, preferred_element_type=jnp.float32) * score_scale
        return jnp.where(lower, raw, neg_fill)

    def group_lse(members):
        scores = group_scores(members[0], members[1])
        row_peak = lax.optimization_barrier(jnp.max(scores, axis=1))
        return row_peak + jnp.log(lax.optimization_barrier(jnp.sum(jnp.exp(scores - row_peak[:, None]), axis=1)))

    def group_out(members):
        scores = group_scores(members[0], members[1])
        weights = jnp.exp(scores - members[3][:, None]).astype(jnp.bfloat16)
        return jnp.dot(weights, members[2], preferred_element_type=jnp.float32)

    def group_grads(members):
        query_grp, key_grp, value_grp, lse_grp, dout_grp, delta_grp = members
        scores = group_scores(query_grp, key_grp)
        weights = jnp.exp(scores - lse_grp[:, None])
        weights_low = weights.astype(jnp.bfloat16)
        value_part = jnp.dot(weights_low.T, dout_grp, preferred_element_type=jnp.float32)
        weight_grad = jnp.dot(dout_grp, value_grp.T, preferred_element_type=jnp.float32)
        score_grad = (weights * (weight_grad - delta_grp[:, None])).astype(jnp.bfloat16)
        query_part = jnp.dot(score_grad, key_grp, preferred_element_type=jnp.float32) * score_scale
        key_part = jnp.dot(score_grad.T, query_grp, preferred_element_type=jnp.float32) * score_scale
        return (query_part, key_part, value_part)
    log_total = jnp.full((TOKENS, HEADS), neg_fill, jnp.float32)
    for stride in level_rates:
        places = level_places(offsets, stride)
        for head in range(HEADS):
            where_rows = places[head]
            flat_rows = where_rows.reshape(-1)
            query_grp = query_rows[:, head][where_rows]
            key_grp = key_rows[:, head][where_rows]
            level_lse = lax.map(group_lse, (query_grp, key_grp))
            log_total = log_total.at[flat_rows, head].set(jnp.logaddexp(log_total[flat_rows, head], level_lse.reshape(-1)))
    attended = jnp.zeros((TOKENS, HEADS, HD), jnp.float32)
    for stride in level_rates:
        places = level_places(offsets, stride)
        for head in range(HEADS):
            where_rows = places[head]
            flat_rows = where_rows.reshape(-1)
            members = (query_rows[:, head][where_rows], key_rows[:, head][where_rows], value_rows[:, head][where_rows], log_total[:, head][where_rows])
            outputs = lax.map(group_out, members)
            attended = attended.at[flat_rows, head].add(outputs.reshape(-1, HD))
    centre = lax.optimization_barrier(jnp.mean(attended, axis=(1, 2)))
    variance = lax.optimization_barrier(jnp.mean(attended * attended, axis=(1, 2))) - centre * centre
    inverse = lax.rsqrt(variance + epsilon)
    normed = (attended - centre[:, None, None]) * inverse[:, None, None]
    grad_in = cotangent.astype(jnp.float32) * norm_gain[None]
    first = lax.optimization_barrier(jnp.mean(grad_in, axis=(1, 2)))
    second = lax.optimization_barrier(jnp.mean(grad_in * normed, axis=(1, 2)))
    d_attended = (inverse[:, None, None] * (grad_in - first[:, None, None] - normed * second[:, None, None])).astype(jnp.bfloat16)
    row_delta = lax.optimization_barrier(jnp.sum(d_attended.astype(jnp.float32) * attended, axis=2))
    query_grad = jnp.zeros((TOKENS, HEADS, HD), jnp.float32)
    key_grad = jnp.zeros((TOKENS, HEADS, HD), jnp.float32)
    value_grad = jnp.zeros((TOKENS, HEADS, HD), jnp.float32)
    for stride in level_rates:
        places = level_places(offsets, stride)
        for head in range(HEADS):
            where_rows = places[head]
            flat_rows = where_rows.reshape(-1)
            members = (query_rows[:, head][where_rows], key_rows[:, head][where_rows], value_rows[:, head][where_rows], log_total[:, head][where_rows], d_attended[:, head][where_rows], row_delta[:, head][where_rows])
            query_part, key_part, value_part = lax.map(group_grads, members)
            query_grad = query_grad.at[flat_rows, head].add(query_part.reshape(-1, HD))
            key_grad = key_grad.at[flat_rows, head].add(key_part.reshape(-1, HD))
            value_grad = value_grad.at[flat_rows, head].add(value_part.reshape(-1, HD))
    return (query_grad.astype(jnp.bfloat16), key_grad.astype(jnp.bfloat16), value_grad.astype(jnp.bfloat16))
```

```python
import functools

import jax
import jax.numpy as jnp
from jax import lax
from jax.experimental import pallas as pl
from jax.experimental.pallas import tpu as pltpu
from jax.sharding import PartitionSpec as P

RATE2 = 4
RATE3 = 16
RATE4 = 32


neg_fill = -1e30
epsilon = 1e-05
block_width = 512


def passed_along(value, axis, steps):
    count = lax.axis_size(axis)
    leading, last = (max(0, -steps), min(count, count - steps))
    return lax.ppermute(value, axis, [(source, source + steps) for source in range(leading, last)])


def pick_rows(source, wanted, stride):
    row_count = source.shape[0] // stride
    shaped = source.reshape((row_count, stride) + source.shape[1:])
    trailing = (1,) * (source.ndim - 2)
    target = wanted.reshape((1, 1, -1) + trailing)
    column = jnp.arange(stride, dtype=jnp.int32).reshape((1, stride, 1) + trailing)
    zeroed = jnp.where(column == target, shaped, jnp.zeros((), source.dtype))
    return jnp.sum(zeroed, axis=1, dtype=source.dtype)


def put_rows(compact, wanted, stride, filler):
    trailing = (1,) * (compact.ndim - 2)
    target = wanted.reshape((1, 1, -1) + trailing)
    column = jnp.arange(stride, dtype=jnp.int32).reshape((1, stride, 1) + trailing)
    spread = jnp.where(column == target, compact[:, None], jnp.asarray(filler, compact.dtype))
    return spread.reshape((compact.shape[0] * stride,) + compact.shape[1:])


def row_places(device, slot_count, direction, row_count, stride, wanted, tok_dev):
    owners = device + direction * jnp.arange(slot_count, dtype=jnp.int32)
    within_dev = wanted[None, :] + stride * jnp.arange(row_count, dtype=jnp.int32)[:, None]
    places = owners[:, None, None] * tok_dev + within_dev[None]
    return places.reshape(slot_count * row_count, wanted.shape[0])


def masked_scores(query_blk, key_blk, query_pos, key_pos, seg_len, score_scale):
    raw = (
        jnp.einsum("qhd,khd->hqk", query_blk, key_blk, preferred_element_type=jnp.float32)
        * score_scale
    )
    query_at = query_pos.T[:, :, None]
    key_at = key_pos.T[:, None, :]
    linked = (query_at // seg_len == key_at // seg_len) & (key_at <= query_at)
    return jnp.where(linked, raw, neg_fill)


def flatten_slots(member):
    return member.reshape((member.shape[0] * member.shape[1],) + member.shape[2:])


def extend(buffers, target, sign, puller):
    while buffers[0].shape[0] < target:
        covered = buffers[0].shape[0]
        arrived = puller(buffers, sign * covered)
        buffers = tuple(
            (jnp.concatenate([held, current], axis=0) for held, current in zip(buffers, arrived))
        )
    return buffers


def pull_keys(buffers, offset):
    return passed_along((buffers[0], buffers[1]), "seq", offset)


def pull_queries(buffers, offset):
    moved = passed_along((buffers[0], buffers[1]), "seq", offset)
    stats = passed_along((buffers[2], buffers[3]), "seq", offset)
    return (moved[0], moved[1], stats[0], stats[1])


def feature_sums(first, second):
    return lax.psum((first, second), "head")


def shards(query_rows, key_rows, value_rows, cotangent, norm_gain, offsets):
    tok_dev, heads_dev, head_size = query_rows.shape
    seq_count = lax.axis_size("seq")
    device = lax.axis_index("seq")
    group_rows = tok_dev * seq_count // RATE4
    score_scale = head_size ** (-0.5)
    features = heads_dev * head_size * lax.axis_size("head")
    levels = []
    for stride in (1, RATE2, RATE3, RATE4):
        seg_len = stride * group_rows
        levels.append((stride, seg_len, max(1, seg_len // tok_dev), offsets % stride))
    key_sets = []
    for stride, seg_len, span_devices, wanted in levels:
        own_rows = (
            pick_rows(key_rows, wanted, stride)[None],
            pick_rows(value_rows, wanted, stride)[None],
        )
        key_sets.append(extend(own_rows, span_devices, 1, pull_keys))
    prepared = []
    for (stride, seg_len, span_devices, wanted), key_set in zip(levels, key_sets):
        row_count = tok_dev // stride
        key_flat = flatten_slots(key_set[0])
        value_flat = flatten_slots(key_set[1])
        key_places = row_places(device, key_set[0].shape[0], -1, row_count, stride, wanted, tok_dev)
        query_sel = pick_rows(query_rows, wanted, stride)
        query_places = row_places(device, 1, -1, row_count, stride, wanted, tok_dev)
        prepared.append(
            (
                stride,
                seg_len,
                span_devices,
                wanted,
                row_count,
                key_flat,
                value_flat,
                key_places,
                query_sel,
                query_places,
            )
        )
    lse_total = jnp.full((tok_dev, heads_dev), neg_fill, jnp.float32)
    for (
        stride,
        seg_len,
        span_devices,
        wanted,
        row_count,
        key_flat,
        value_flat,
        key_places,
        query_sel,
        query_places,
    ) in prepared:
        level_lse = jnp.full((row_count, heads_dev), neg_fill, jnp.float32)
        for first_row in range(0, key_flat.shape[0], block_width):
            scores = masked_scores(
                query_sel,
                key_flat[first_row : first_row + block_width],
                query_places,
                key_places[first_row : first_row + block_width],
                seg_len,
                score_scale,
            )
            row_peak = jnp.max(scores, axis=2)
            block_lse = row_peak + jnp.log(jnp.sum(jnp.exp(scores - row_peak[:, :, None]), axis=2))
            level_lse = jnp.logaddexp(level_lse, block_lse.T)
        lse_total = jnp.logaddexp(lse_total, put_rows(level_lse, wanted, stride, neg_fill))
    attended = jnp.zeros((tok_dev, heads_dev, head_size), jnp.float32)
    for (
        stride,
        seg_len,
        span_devices,
        wanted,
        row_count,
        key_flat,
        value_flat,
        key_places,
        query_sel,
        query_places,
    ) in prepared:
        lse_sel = pick_rows(lse_total, wanted, stride)
        out_sel = jnp.zeros((row_count, heads_dev, head_size), jnp.float32)
        for first_row in range(0, key_flat.shape[0], block_width):
            scores = masked_scores(
                query_sel,
                key_flat[first_row : first_row + block_width],
                query_places,
                key_places[first_row : first_row + block_width],
                seg_len,
                score_scale,
            )
            weights = jnp.exp(scores - lse_sel.T[:, :, None]).astype(jnp.bfloat16)
            out_sel = out_sel + jnp.einsum(
                "hqk,khd->qhd",
                weights,
                value_flat[first_row : first_row + block_width],
                preferred_element_type=jnp.float32,
            )
        attended = attended + put_rows(out_sel, wanted, stride, 0.0)
    totals = feature_sums(jnp.sum(attended, axis=(1, 2)), jnp.sum(attended * attended, axis=(1, 2)))
    centre = totals[0] / features
    variance = totals[1] / features - centre * centre
    inverse = lax.rsqrt(variance + epsilon)
    normed = (attended - centre[:, None, None]) * inverse[:, None, None]
    grad_in = cotangent.astype(jnp.float32) * norm_gain[None]
    moments = feature_sums(jnp.sum(grad_in, axis=(1, 2)), jnp.sum(grad_in * normed, axis=(1, 2)))
    first_mean = moments[0] / features
    second_mean = moments[1] / features
    d_attended = (
        inverse[:, None, None]
        * (grad_in - first_mean[:, None, None] - normed * second_mean[:, None, None])
    ).astype(jnp.bfloat16)
    row_delta = jnp.sum(d_attended.astype(jnp.float32) * attended, axis=2)
    query_grad = jnp.zeros((tok_dev, heads_dev, head_size), jnp.float32)
    for (
        stride,
        seg_len,
        span_devices,
        wanted,
        row_count,
        key_flat,
        value_flat,
        key_places,
        query_sel,
        query_places,
    ) in prepared:
        lse_sel = pick_rows(lse_total, wanted, stride)
        dout_sel = pick_rows(d_attended, wanted, stride)
        delta_sel = pick_rows(row_delta, wanted, stride)
        grad_sel = jnp.zeros((row_count, heads_dev, head_size), jnp.float32)
        for first_row in range(0, key_flat.shape[0], block_width):
            key_block = key_flat[first_row : first_row + block_width]
            scores = masked_scores(
                query_sel,
                key_block,
                query_places,
                key_places[first_row : first_row + block_width],
                seg_len,
                score_scale,
            )
            weights = jnp.exp(scores - lse_sel.T[:, :, None])
            weight_grad = jnp.einsum(
                "qhd,khd->hqk",
                dout_sel,
                value_flat[first_row : first_row + block_width],
                preferred_element_type=jnp.float32,
            )
            score_grad = (weights * (weight_grad - delta_sel.T[:, :, None])).astype(jnp.bfloat16)
            grad_sel = grad_sel + jnp.einsum(
                "hqk,khd->qhd", score_grad, key_block, preferred_element_type=jnp.float32
            )
        query_grad = query_grad + put_rows(grad_sel * score_scale, wanted, stride, 0.0)
    query_sets = []
    for stride, seg_len, span_devices, wanted in levels:
        own_rows = (
            pick_rows(query_rows, wanted, stride)[None],
            pick_rows(d_attended, wanted, stride)[None],
            pick_rows(lse_total, wanted, stride)[None],
            pick_rows(row_delta, wanted, stride)[None],
        )
        query_sets.append(extend(own_rows, span_devices, -1, pull_queries))
    key_grad = jnp.zeros((tok_dev, heads_dev, head_size), jnp.float32)
    value_grad = jnp.zeros((tok_dev, heads_dev, head_size), jnp.float32)
    for (
        stride,
        seg_len,
        span_devices,
        wanted,
        row_count,
        key_flat,
        value_flat,
        key_places,
        query_sel,
        query_places,
    ), query_set in zip(prepared, query_sets):
        query_flat = flatten_slots(query_set[0])
        dout_flat = flatten_slots(query_set[1])
        lse_flat = flatten_slots(query_set[2])
        delta_flat = flatten_slots(query_set[3])
        query_far = row_places(device, query_set[0].shape[0], 1, row_count, stride, wanted, tok_dev)
        key_sel = pick_rows(key_rows, wanted, stride)
        value_sel = pick_rows(value_rows, wanted, stride)
        key_grad_sel = jnp.zeros((row_count, heads_dev, head_size), jnp.float32)
        value_grad_sel = jnp.zeros((row_count, heads_dev, head_size), jnp.float32)
        for first_row in range(0, query_flat.shape[0], block_width):
            query_block = query_flat[first_row : first_row + block_width]
            dout_block = dout_flat[first_row : first_row + block_width]
            lse_block = lse_flat[first_row : first_row + block_width]
            delta_block = delta_flat[first_row : first_row + block_width]
            scores = masked_scores(
                query_block,
                key_sel,
                query_far[first_row : first_row + block_width],
                query_places,
                seg_len,
                score_scale,
            )
            weights = jnp.exp(scores - lse_block.T[:, :, None])
            value_grad_sel = value_grad_sel + jnp.einsum(
                "hqk,qhd->khd",
                weights.astype(jnp.bfloat16),
                dout_block,
                preferred_element_type=jnp.float32,
            )
            weight_grad = jnp.einsum(
                "qhd,khd->hqk", dout_block, value_sel, preferred_element_type=jnp.float32
            )
            score_grad = (weights * (weight_grad - delta_block.T[:, :, None])).astype(jnp.bfloat16)
            key_grad_sel = key_grad_sel + jnp.einsum(
                "hqk,qhd->khd", score_grad, query_block, preferred_element_type=jnp.float32
            )
        key_grad = key_grad + put_rows(key_grad_sel * score_scale, wanted, stride, 0.0)
        value_grad = value_grad + put_rows(value_grad_sel, wanted, stride, 0.0)
    return (
        query_grad.astype(jnp.bfloat16),
        key_grad.astype(jnp.bfloat16),
        value_grad.astype(jnp.bfloat16),
    )

MESH = pl.DeviceIdType.MESH
LOG2E = 1.4426950408889634
HIDDEN = -1e30
ROWS = 16


def dot_nn(a, b):
    return lax.dot_general(a, b, (((1,), (0,)), ((), ())), preferred_element_type=jnp.float32)


def dot_nt(a, b):
    return lax.dot_general(a, b, (((1,), (1,)), ((), ())), preferred_element_type=jnp.float32)


def dot_tn(a, b):
    return lax.dot_general(a, b, (((0,), (0,)), ((), ())), preferred_element_type=jnp.float32)


def iota(shape, axis):
    return lax.broadcasted_iota(jnp.int32, shape, axis)


def bias_of(count):
    return jnp.where(count > 0.5, jnp.log2(jnp.maximum(count, 1.0)), HIDDEN)


def fused(
    seqs,
    heads,
    seg1,
    features,
    off_ref,
    q_hbm,
    k_hbm,
    v_hbm,
    c_hbm,
    gain_ref,
    dq_ref,
    dk_ref,
    dv_ref,
    xin,
    wide,
    mats,
    grads,
    weights,
    far_weights,
    bias,
    far_bias,
    late_bias,
    kvsel,
    qsel,
    dosel,
    ssel,
    kvbuf,
    qbuf,
    dobuf,
    sbuf,
    hsend,
    hbuf,
    rows_ref,
    outwide,
    in_sem,
    kv_send,
    kv_recv,
    q_send,
    q_recv,
    do_send,
    do_recv,
    s_send,
    s_recv,
    h_send,
    h_recv,
):
    me = lax.axis_index("seq")
    mine = lax.axis_index("head")
    both, tok = mats.shape[1], mats.shape[2]
    size = mats.shape[3]
    far = seqs * ROWS
    quad = 16 * seg1 // tok
    scale = size ** (-0.5)
    scale2 = scale * LOG2E

    loads = []
    for at, source in enumerate((k_hbm, v_hbm, q_hbm, c_hbm)):
        copy = pltpu.make_async_copy(source, xin.at[at], in_sem.at[at])
        copy.start()
        loads.append(copy)
    kvbuf[...] = jnp.zeros_like(kvbuf)
    qbuf[...] = jnp.zeros_like(qbuf)
    dobuf[...] = jnp.zeros_like(dobuf)
    sbuf[...] = jnp.zeros_like(sbuf)
    hbuf[...] = jnp.zeros_like(hbuf)
    hsend[...] = jnp.zeros_like(hsend)
    rows_ref[...] = jnp.zeros_like(rows_ref)

    barrier = pltpu.get_barrier_semaphore()
    for step in range(1, seqs):
        pl.semaphore_signal(
            barrier, inc=1, device_id=(lax.rem(me + step, seqs), mine), device_id_type=MESH
        )
    for step in range(1, heads):
        pl.semaphore_signal(
            barrier, inc=1, device_id=(me, lax.rem(mine + step, heads)), device_id_type=MESH
        )

    def later_copy(source, target, send, recv, step):
        return pltpu.make_async_remote_copy(
            src_ref=source,
            dst_ref=target,
            send_sem=send.at[step - 1],
            recv_sem=recv.at[step - 1],
            device_id=(lax.rem(me + step, seqs), mine),
            device_id_type=MESH,
        )

    def earlier_copy(source, target, send, recv, step):
        return pltpu.make_async_remote_copy(
            src_ref=source,
            dst_ref=target,
            send_sem=send.at[step - 1],
            recv_sem=recv.at[step - 1],
            device_id=(lax.rem(me + seqs - step, seqs), mine),
            device_id_type=MESH,
        )

    def head_copy(step):
        return pltpu.make_async_remote_copy(
            src_ref=hsend,
            dst_ref=hbuf.at[mine],
            send_sem=h_send.at[step - 1],
            recv_sem=h_recv.at[step - 1],
            device_id=(me, lax.rem(mine + step, heads)),
            device_id_type=MESH,
        )

    kv_copies = [
        later_copy(kvsel, kvbuf.at[:, :, me], kv_send, kv_recv, step) for step in range(1, seqs)
    ]
    q_copies = [
        earlier_copy(qsel, qbuf.at[:, me], q_send, q_recv, step) for step in range(1, seqs)
    ]
    do_copies = [
        earlier_copy(dosel, dobuf.at[:, me], do_send, do_recv, step) for step in range(1, seqs)
    ]
    s_copies = [
        earlier_copy(ssel, sbuf.at[me], s_send, s_recv, step) for step in range(1, seqs)
    ]
    h_copies = [head_copy(step) for step in range(1, heads)]
    ahead = [me + step < seqs for step in range(1, seqs)]
    behind = [me >= step for step in range(1, seqs)]

    wanted = [off_ref[h] for h in range(both)]
    for at in range(3):
        loads[at].wait()
        wide[at] = xin[at].astype(jnp.float32)
        for h in range(both):
            start = both * (wanted[h] & (ROWS - 1)) + h
            rows = wide[at, pl.ds(start, ROWS, stride=both * ROWS), :].astype(jnp.bfloat16)
            if at < 2:
                kvsel[at, h] = rows
            else:
                qsel[h] = rows

    pl.semaphore_wait(barrier, seqs + heads - 2)
    for step in range(1, seqs):
        @pl.when(ahead[step - 1])
        def _(step=step):
            kv_copies[step - 1].start()
    for step in range(1, seqs):
        @pl.when(behind[step - 1])
        def _(step=step):
            q_copies[step - 1].start()

    for at in range(3):
        for h in range(both):
            mats[at, h] = wide[at, pl.ds(h, tok, stride=both), :].astype(jnp.bfloat16)

    lane = iota((tok, 128), 1)
    token = iota((tok, 128), 0)
    causal = iota((tok, tok), 0) <= iota((tok, tok), 1)
    for h in range(both):
        off = wanted[h]
        marks = (token // seg1) == lane
        marks = marks | ((lane == 64) & ((token & (RATE2 - 1)) == (off & (RATE2 - 1))))
        marks = marks | ((lane == 65) & ((token & (RATE3 - 1)) == (off & (RATE3 - 1))))
        marks = marks | ((lane == 66) & ((token & (RATE4 - 1)) == (off & (RATE4 - 1))))
        marked = jnp.where(marks, 1.0, 0.0).astype(jnp.bfloat16)
        count = dot_nt(marked, marked)
        bias[h] = bias_of(jnp.where(causal, count, 0.0))

    first_stats = []
    for h in range(both):
        score = dot_nt(mats[0, h], mats[2, h]) * scale2 + bias[h]
        peak = jnp.max(score, axis=0, keepdims=True)
        held = jnp.exp2(score - peak)
        weights[h] = held
        total = jnp.sum(held, axis=0, keepdims=True)
        out = dot_tn(mats[1, h], held.astype(jnp.bfloat16))
        first_stats.append((peak, total, out))

    loads[3].wait()
    wide[3] = xin[3].astype(jnp.float32)
    for h in range(both):
        grad = wide[3, pl.ds(h, tok, stride=both), :] * gain_ref[h : h + 1, :]
        grads[h] = grad.T

    for h in range(both):
        off = wanted[h]
        odd = (off // ROWS) & 1
        slot = iota((far, tok), 0) // ROWS
        query = iota((far, tok), 1)
        sel3 = (query & 15) == (off & 15)
        sel4 = (query & 31) == (off & 31)
        key4 = (iota((far, tok), 0) & 1) == odd
        near = (slot // quad) == (me // quad)
        count = jnp.where(near & sel3, 1.0, 0.0) + jnp.where(key4 & sel4, 1.0, 0.0)
        far_bias[h] = bias_of(jnp.where(slot < me, count, 0.0))
        slot = iota((tok, far), 1) // ROWS
        key = iota((tok, far), 0)
        sel3 = (key & 15) == (off & 15)
        sel4 = (key & 31) == (off & 31)
        query4 = (iota((tok, far), 1) & 1) == odd
        near = (slot // quad) == (me // quad)
        count = jnp.where(near & sel3, 1.0, 0.0) + jnp.where(query4 & sel4, 1.0, 0.0)
        late_bias[h] = bias_of(jnp.where(slot > me, count, 0.0))

    for step in range(1, seqs):
        @pl.when(behind[step - 1])
        def _(step=step):
            kv_copies[step - 1].wait_recv()

    sums = [jnp.zeros((1, tok), jnp.float32) for _ in range(4)]
    stats = []
    for h in range(both):
        peak, total, out = first_stats[h]
        far_keys = kvbuf[0, h].reshape(far, size)
        far_values = kvbuf[1, h].reshape(far, size)
        score = dot_nt(far_keys, mats[2, h]) * scale2 + far_bias[h]
        top = jnp.maximum(peak, jnp.max(score, axis=0, keepdims=True))
        shrink = jnp.exp2(peak - top)
        held = jnp.exp2(score - top)
        total = total * shrink + jnp.sum(held, axis=0, keepdims=True)
        ratio = 1.0 / total
        far_weights[h] = held * ratio
        out = (out * shrink + dot_tn(far_values, held.astype(jnp.bfloat16))) * ratio
        grad = grads[h]
        sums[0] = sums[0] + jnp.sum(out, axis=0, keepdims=True)
        sums[1] = sums[1] + jnp.sum(out * out, axis=0, keepdims=True)
        sums[2] = sums[2] + jnp.sum(grad, axis=0, keepdims=True)
        sums[3] = sums[3] + jnp.sum(grad * out, axis=0, keepdims=True)
        stats.append((out, shrink * ratio, top + jnp.log2(total)))
    for at in range(4):
        hsend[at : at + 1, :] = sums[at]
    for copy in h_copies:
        copy.start()
    for h in range(both):
        weights[h] = weights[h] * stats[h][1]
    for copy in h_copies:
        copy.wait_recv()

    full = hsend[...]
    for at in range(heads):
        full = full + hbuf[at]
    full = full * (1.0 / features)
    centre = full[0:1]
    inverse = lax.rsqrt(full[1:2] - centre * centre + epsilon)
    first = full[2:3]
    second = inverse * (full[3:4] - centre * first)

    douts = []
    for h in range(both):
        out, _, lse = stats[h]
        normed = (out - centre) * inverse
        dout = (inverse * (grads[h] - first - normed * second)).astype(jnp.bfloat16)
        delta = jnp.sum(dout.astype(jnp.float32) * out, axis=0, keepdims=True)
        off = wanted[h]
        picker = jnp.where(
            iota((ROWS, tok), 1) == (off & 15) + ROWS * iota((ROWS, tok), 0), 1.0, 0.0
        ).astype(jnp.bfloat16)
        dosel[h] = dot_nt(picker, dout).astype(jnp.bfloat16)
        rows_ref[h, 0:1, :] = lse
        rows_ref[h, 1:2, :] = delta
        placer = jnp.where(
            iota((tok, far), 0) + ROWS * ROWS * me == (off & 15) + ROWS * iota((tok, far), 1),
            1.0,
            0.0,
        ).astype(jnp.bfloat16)
        rest = rows_ref[h]
        moved = jnp.zeros((8, far), jnp.float32)
        for _ in range(3):
            part = rest.astype(jnp.bfloat16)
            rest = rest - part.astype(jnp.float32)
            moved = moved + dot_nn(part, placer)
        ssel[h] = moved
        douts.append((dout, delta))

    for step in range(1, seqs):
        @pl.when(behind[step - 1])
        def _(step=step):
            do_copies[step - 1].start()
            s_copies[step - 1].start()

    key_parts = []
    for h in range(both):
        dout, delta = douts[h]
        weight = weights[h]
        weight_grad = dot_nn(mats[1, h], dout)
        score_grad = (weight * (weight_grad - delta)).astype(jnp.bfloat16)
        value_part = dot_nt(weight.astype(jnp.bfloat16), dout)
        key_part = dot_nn(score_grad, mats[2, h])
        far_keys = kvbuf[0, h].reshape(far, size)
        far_values = kvbuf[1, h].reshape(far, size)
        far_grad = dot_nn(far_values, dout)
        far_score = (far_weights[h] * (far_grad - delta)).astype(jnp.bfloat16)
        query_part = dot_tn(mats[0, h], score_grad) + dot_tn(far_keys, far_score)
        outwide[0, pl.ds(h, tok, stride=both), :] = (query_part * scale).T
        key_parts.append((key_part, value_part))
    dq_ref[...] = outwide[0].astype(jnp.bfloat16)

    for step in range(1, seqs):
        @pl.when(ahead[step - 1])
        def _(step=step):
            q_copies[step - 1].wait_recv()
            do_copies[step - 1].wait_recv()
            s_copies[step - 1].wait_recv()

    for h in range(both):
        key_part, value_part = key_parts[h]
        late_queries = qbuf[h].reshape(far, size)
        late_douts = dobuf[h].reshape(far, size)
        held = sbuf[0, h]
        for at in range(1, seqs):
            held = held + sbuf[at, h]
        score = dot_nt(mats[0, h], late_queries) * scale2 + late_bias[h]
        weight = jnp.exp2(score - held[0:1])
        weight_grad = dot_nt(mats[1, h], late_douts)
        score_grad = (weight * (weight_grad - held[1:2])).astype(jnp.bfloat16)
        value_part = value_part + dot_nn(weight.astype(jnp.bfloat16), late_douts)
        key_part = key_part + dot_nn(score_grad, late_queries)
        outwide[1, pl.ds(h, tok, stride=both), :] = key_part * scale
        outwide[2, pl.ds(h, tok, stride=both), :] = value_part
    dk_ref[...] = outwide[1].astype(jnp.bfloat16)
    dv_ref[...] = outwide[2].astype(jnp.bfloat16)

    for step in range(1, seqs):
        @pl.when(ahead[step - 1])
        def _(step=step):
            kv_copies[step - 1].wait_send()

        @pl.when(behind[step - 1])
        def _(step=step):
            q_copies[step - 1].wait_send()
            do_copies[step - 1].wait_send()
            s_copies[step - 1].wait_send()
    for copy in h_copies:
        copy.wait_send()


def fused_shards(query_rows, key_rows, value_rows, cotangent, norm_gain, offsets):
    tok, both, size = query_rows.shape
    seqs = lax.axis_size("seq")
    heads = lax.axis_size("head")
    seg1 = tok * seqs // RATE4
    far = seqs * ROWS
    flat = (both * tok, size)
    low, full = jnp.bfloat16, jnp.float32
    vmem = pl.BlockSpec(memory_space=pltpu.VMEM)
    anywhere = pl.BlockSpec(memory_space=pl.ANY)
    outs = pl.pallas_call(
        functools.partial(fused, seqs, heads, seg1, both * size * heads),
        out_shape=[jax.ShapeDtypeStruct(flat, low)] * 3,
        in_specs=[pl.BlockSpec(memory_space=pltpu.SMEM)] + [anywhere] * 4 + [vmem],
        out_specs=[vmem] * 3,
        scratch_shapes=[
            pltpu.VMEM((4,) + flat, low),
            pltpu.VMEM((4,) + flat, full),
            pltpu.VMEM((3, both, tok, size), low),
            pltpu.VMEM((both, size, tok), full),
            pltpu.VMEM((both, tok, tok), full),
            pltpu.VMEM((both, far, tok), full),
            pltpu.VMEM((both, tok, tok), full),
            pltpu.VMEM((both, far, tok), full),
            pltpu.VMEM((both, tok, far), full),
            pltpu.VMEM((2, both, ROWS, size), low),
            pltpu.VMEM((both, ROWS, size), low),
            pltpu.VMEM((both, ROWS, size), low),
            pltpu.VMEM((both, 8, far), full),
            pltpu.VMEM((2, both, seqs, ROWS, size), low),
            pltpu.VMEM((both, seqs, ROWS, size), low),
            pltpu.VMEM((both, seqs, ROWS, size), low),
            pltpu.VMEM((seqs, both, 8, far), full),
            pltpu.VMEM((8, tok), full),
            pltpu.VMEM((heads, 8, tok), full),
            pltpu.VMEM((both, 8, tok), full),
            pltpu.VMEM((3,) + flat, full),
            pltpu.SemaphoreType.DMA((4,)),
        ]
        + [pltpu.SemaphoreType.DMA((seqs - 1,))] * 8
        + [pltpu.SemaphoreType.DMA((heads - 1,))] * 2,
        compiler_params=pltpu.CompilerParams(
            collective_id=0, has_side_effects=True, vmem_limit_bytes=32 * 1024 * 1024
        ),
        name="fused_backward",
    )(
        offsets,
        query_rows.reshape(flat),
        key_rows.reshape(flat),
        value_rows.reshape(flat),
        cotangent.reshape(flat),
        norm_gain,
    )
    return tuple(out.reshape(query_rows.shape) for out in outs)


def fits(mesh, tok, both, size):
    seqs = mesh.shape["seq"]
    seg1 = tok * seqs // RATE4
    return (
        tok == ROWS * RATE3
        and size == 128
        and both == 2
        and seqs * ROWS == 128
        and tok % (RATE2 * seg1) == 0
        and (RATE3 * seg1) % tok == 0
        and tok // seg1 <= 64
    )


def solution(mesh):
    placed = (
        P("seq", "head", None),
        P("seq", "head", None),
        P("seq", "head", None),
        P("seq", "head", None),
        P("head", None),
        P("head"),
    )

    def run(query_rows, key_rows, value_rows, cotangent, norm_gain, offsets):
        tokens, heads, size = query_rows.shape
        small = fits(mesh, tokens // mesh.shape["seq"], heads // mesh.shape["head"], size)
        return jax.shard_map(
            fused_shards if small else shards,
            mesh=mesh,
            in_specs=placed,
            out_specs=(P("seq", "head", None), P("seq", "head", None), P("seq", "head", None)),
            check_vma=False,
        )(query_rows, key_rows, value_rows, cotangent, norm_gain, offsets)

    return run
```

```python
import functools

import jax
import jax.numpy as jnp
from jax import lax
from jax.experimental import pallas as pl
from jax.experimental.pallas import tpu as pltpu
from jax.sharding import PartitionSpec as P

RATE2 = 4
RATE3 = 16
RATE4 = 32


neg_fill = -1e30
epsilon = 1e-05
block_width = 512


def passed_along(value, axis, steps):
    count = lax.axis_size(axis)
    leading, last = (max(0, -steps), min(count, count - steps))
    return lax.ppermute(value, axis, [(source, source + steps) for source in range(leading, last)])


def pick_rows(source, wanted, stride):
    row_count = source.shape[0] // stride
    shaped = source.reshape((row_count, stride) + source.shape[1:])
    trailing = (1,) * (source.ndim - 2)
    target = wanted.reshape((1, 1, -1) + trailing)
    column = jnp.arange(stride, dtype=jnp.int32).reshape((1, stride, 1) + trailing)
    zeroed = jnp.where(column == target, shaped, jnp.zeros((), source.dtype))
    return jnp.sum(zeroed, axis=1, dtype=source.dtype)


def put_rows(compact, wanted, stride, filler):
    trailing = (1,) * (compact.ndim - 2)
    target = wanted.reshape((1, 1, -1) + trailing)
    column = jnp.arange(stride, dtype=jnp.int32).reshape((1, stride, 1) + trailing)
    spread = jnp.where(column == target, compact[:, None], jnp.asarray(filler, compact.dtype))
    return spread.reshape((compact.shape[0] * stride,) + compact.shape[1:])


def row_places(device, slot_count, direction, row_count, stride, wanted, tok_dev):
    owners = device + direction * jnp.arange(slot_count, dtype=jnp.int32)
    within_dev = wanted[None, :] + stride * jnp.arange(row_count, dtype=jnp.int32)[:, None]
    places = owners[:, None, None] * tok_dev + within_dev[None]
    return places.reshape(slot_count * row_count, wanted.shape[0])


def masked_scores(query_blk, key_blk, query_pos, key_pos, seg_len, score_scale):
    raw = (
        jnp.einsum("qhd,khd->hqk", query_blk, key_blk, preferred_element_type=jnp.float32)
        * score_scale
    )
    query_at = query_pos.T[:, :, None]
    key_at = key_pos.T[:, None, :]
    linked = (query_at // seg_len == key_at // seg_len) & (key_at <= query_at)
    return jnp.where(linked, raw, neg_fill)


def flatten_slots(member):
    return member.reshape((member.shape[0] * member.shape[1],) + member.shape[2:])


def extend(buffers, target, sign, puller):
    while buffers[0].shape[0] < target:
        covered = buffers[0].shape[0]
        arrived = puller(buffers, sign * covered)
        buffers = tuple(
            (jnp.concatenate([held, current], axis=0) for held, current in zip(buffers, arrived))
        )
    return buffers


def pull_keys(buffers, offset):
    return passed_along((buffers[0], buffers[1]), "seq", offset)


def pull_queries(buffers, offset):
    moved = passed_along((buffers[0], buffers[1]), "seq", offset)
    stats = passed_along((buffers[2], buffers[3]), "seq", offset)
    return (moved[0], moved[1], stats[0], stats[1])


def feature_sums(first, second):
    return lax.psum((first, second), "head")


def shards(query_rows, key_rows, value_rows, cotangent, norm_gain, offsets):
    tok_dev, heads_dev, head_size = query_rows.shape
    seq_count = lax.axis_size("seq")
    device = lax.axis_index("seq")
    group_rows = tok_dev * seq_count // RATE4
    score_scale = head_size ** (-0.5)
    features = heads_dev * head_size * lax.axis_size("head")
    levels = []
    for stride in (1, RATE2, RATE3, RATE4):
        seg_len = stride * group_rows
        levels.append((stride, seg_len, max(1, seg_len // tok_dev), offsets % stride))
    key_sets = []
    for stride, seg_len, span_devices, wanted in levels:
        own_rows = (
            pick_rows(key_rows, wanted, stride)[None],
            pick_rows(value_rows, wanted, stride)[None],
        )
        key_sets.append(extend(own_rows, span_devices, 1, pull_keys))
    prepared = []
    for (stride, seg_len, span_devices, wanted), key_set in zip(levels, key_sets):
        row_count = tok_dev // stride
        key_flat = flatten_slots(key_set[0])
        value_flat = flatten_slots(key_set[1])
        key_places = row_places(device, key_set[0].shape[0], -1, row_count, stride, wanted, tok_dev)
        query_sel = pick_rows(query_rows, wanted, stride)
        query_places = row_places(device, 1, -1, row_count, stride, wanted, tok_dev)
        prepared.append(
            (
                stride,
                seg_len,
                span_devices,
                wanted,
                row_count,
                key_flat,
                value_flat,
                key_places,
                query_sel,
                query_places,
            )
        )
    lse_total = jnp.full((tok_dev, heads_dev), neg_fill, jnp.float32)
    for (
        stride,
        seg_len,
        span_devices,
        wanted,
        row_count,
        key_flat,
        value_flat,
        key_places,
        query_sel,
        query_places,
    ) in prepared:
        level_lse = jnp.full((row_count, heads_dev), neg_fill, jnp.float32)
        for first_row in range(0, key_flat.shape[0], block_width):
            scores = masked_scores(
                query_sel,
                key_flat[first_row : first_row + block_width],
                query_places,
                key_places[first_row : first_row + block_width],
                seg_len,
                score_scale,
            )
            row_peak = jnp.max(scores, axis=2)
            block_lse = row_peak + jnp.log(jnp.sum(jnp.exp(scores - row_peak[:, :, None]), axis=2))
            level_lse = jnp.logaddexp(level_lse, block_lse.T)
        lse_total = jnp.logaddexp(lse_total, put_rows(level_lse, wanted, stride, neg_fill))
    attended = jnp.zeros((tok_dev, heads_dev, head_size), jnp.float32)
    for (
        stride,
        seg_len,
        span_devices,
        wanted,
        row_count,
        key_flat,
        value_flat,
        key_places,
        query_sel,
        query_places,
    ) in prepared:
        lse_sel = pick_rows(lse_total, wanted, stride)
        out_sel = jnp.zeros((row_count, heads_dev, head_size), jnp.float32)
        for first_row in range(0, key_flat.shape[0], block_width):
            scores = masked_scores(
                query_sel,
                key_flat[first_row : first_row + block_width],
                query_places,
                key_places[first_row : first_row + block_width],
                seg_len,
                score_scale,
            )
            weights = jnp.exp(scores - lse_sel.T[:, :, None]).astype(jnp.bfloat16)
            out_sel = out_sel + jnp.einsum(
                "hqk,khd->qhd",
                weights,
                value_flat[first_row : first_row + block_width],
                preferred_element_type=jnp.float32,
            )
        attended = attended + put_rows(out_sel, wanted, stride, 0.0)
    totals = feature_sums(jnp.sum(attended, axis=(1, 2)), jnp.sum(attended * attended, axis=(1, 2)))
    centre = totals[0] / features
    variance = totals[1] / features - centre * centre
    inverse = lax.rsqrt(variance + epsilon)
    normed = (attended - centre[:, None, None]) * inverse[:, None, None]
    grad_in = cotangent.astype(jnp.float32) * norm_gain[None]
    moments = feature_sums(jnp.sum(grad_in, axis=(1, 2)), jnp.sum(grad_in * normed, axis=(1, 2)))
    first_mean = moments[0] / features
    second_mean = moments[1] / features
    d_attended = (
        inverse[:, None, None]
        * (grad_in - first_mean[:, None, None] - normed * second_mean[:, None, None])
    ).astype(jnp.bfloat16)
    row_delta = jnp.sum(d_attended.astype(jnp.float32) * attended, axis=2)
    query_grad = jnp.zeros((tok_dev, heads_dev, head_size), jnp.float32)
    for (
        stride,
        seg_len,
        span_devices,
        wanted,
        row_count,
        key_flat,
        value_flat,
        key_places,
        query_sel,
        query_places,
    ) in prepared:
        lse_sel = pick_rows(lse_total, wanted, stride)
        dout_sel = pick_rows(d_attended, wanted, stride)
        delta_sel = pick_rows(row_delta, wanted, stride)
        grad_sel = jnp.zeros((row_count, heads_dev, head_size), jnp.float32)
        for first_row in range(0, key_flat.shape[0], block_width):
            key_block = key_flat[first_row : first_row + block_width]
            scores = masked_scores(
                query_sel,
                key_block,
                query_places,
                key_places[first_row : first_row + block_width],
                seg_len,
                score_scale,
            )
            weights = jnp.exp(scores - lse_sel.T[:, :, None])
            weight_grad = jnp.einsum(
                "qhd,khd->hqk",
                dout_sel,
                value_flat[first_row : first_row + block_width],
                preferred_element_type=jnp.float32,
            )
            score_grad = (weights * (weight_grad - delta_sel.T[:, :, None])).astype(jnp.bfloat16)
            grad_sel = grad_sel + jnp.einsum(
                "hqk,khd->qhd", score_grad, key_block, preferred_element_type=jnp.float32
            )
        query_grad = query_grad + put_rows(grad_sel * score_scale, wanted, stride, 0.0)
    query_sets = []
    for stride, seg_len, span_devices, wanted in levels:
        own_rows = (
            pick_rows(query_rows, wanted, stride)[None],
            pick_rows(d_attended, wanted, stride)[None],
            pick_rows(lse_total, wanted, stride)[None],
            pick_rows(row_delta, wanted, stride)[None],
        )
        query_sets.append(extend(own_rows, span_devices, -1, pull_queries))
    key_grad = jnp.zeros((tok_dev, heads_dev, head_size), jnp.float32)
    value_grad = jnp.zeros((tok_dev, heads_dev, head_size), jnp.float32)
    for (
        stride,
        seg_len,
        span_devices,
        wanted,
        row_count,
        key_flat,
        value_flat,
        key_places,
        query_sel,
        query_places,
    ), query_set in zip(prepared, query_sets):
        query_flat = flatten_slots(query_set[0])
        dout_flat = flatten_slots(query_set[1])
        lse_flat = flatten_slots(query_set[2])
        delta_flat = flatten_slots(query_set[3])
        query_far = row_places(device, query_set[0].shape[0], 1, row_count, stride, wanted, tok_dev)
        key_sel = pick_rows(key_rows, wanted, stride)
        value_sel = pick_rows(value_rows, wanted, stride)
        key_grad_sel = jnp.zeros((row_count, heads_dev, head_size), jnp.float32)
        value_grad_sel = jnp.zeros((row_count, heads_dev, head_size), jnp.float32)
        for first_row in range(0, query_flat.shape[0], block_width):
            query_block = query_flat[first_row : first_row + block_width]
            dout_block = dout_flat[first_row : first_row + block_width]
            lse_block = lse_flat[first_row : first_row + block_width]
            delta_block = delta_flat[first_row : first_row + block_width]
            scores = masked_scores(
                query_block,
                key_sel,
                query_far[first_row : first_row + block_width],
                query_places,
                seg_len,
                score_scale,
            )
            weights = jnp.exp(scores - lse_block.T[:, :, None])
            value_grad_sel = value_grad_sel + jnp.einsum(
                "hqk,qhd->khd",
                weights.astype(jnp.bfloat16),
                dout_block,
                preferred_element_type=jnp.float32,
            )
            weight_grad = jnp.einsum(
                "qhd,khd->hqk", dout_block, value_sel, preferred_element_type=jnp.float32
            )
            score_grad = (weights * (weight_grad - delta_block.T[:, :, None])).astype(jnp.bfloat16)
            key_grad_sel = key_grad_sel + jnp.einsum(
                "hqk,qhd->khd", score_grad, query_block, preferred_element_type=jnp.float32
            )
        key_grad = key_grad + put_rows(key_grad_sel * score_scale, wanted, stride, 0.0)
        value_grad = value_grad + put_rows(value_grad_sel, wanted, stride, 0.0)
    return (
        query_grad.astype(jnp.bfloat16),
        key_grad.astype(jnp.bfloat16),
        value_grad.astype(jnp.bfloat16),
    )

MESH = pl.DeviceIdType.MESH
LOG2E = 1.4426950408889634
HIDDEN = -1e30
ROWS = 16
VMEM_BYTES = 64 * 1024 * 1024


def dot_nn(a, b):
    return lax.dot_general(a, b, (((1,), (0,)), ((), ())), preferred_element_type=jnp.float32)


def dot_nt(a, b):
    return lax.dot_general(a, b, (((1,), (1,)), ((), ())), preferred_element_type=jnp.float32)


def dot_tn(a, b):
    return lax.dot_general(a, b, (((0,), (0,)), ((), ())), preferred_element_type=jnp.float32)


def iota(shape, axis):
    return lax.broadcasted_iota(jnp.int32, shape, axis)


def bias_of(count):
    return jnp.where(count > 0.5, jnp.log2(jnp.maximum(count, 1.0)), HIDDEN)


def fused(
    seqs,
    heads,
    seg1,
    features,
    off_hbm,
    q_hbm,
    k_hbm,
    v_hbm,
    c_hbm,
    gain_hbm,
    dq_hbm,
    dk_hbm,
    dv_hbm,
    off_ref,
    gain_ref,
    xin,
    wide,
    mats,
    grads,
    weights,
    far_weights,
    bias,
    far_bias,
    late_score,
    picker,
    placer,
    kvsel,
    qsel,
    dosel,
    kvbuf,
    qbuf,
    dobuf,
    hsend,
    hbuf,
    rows_ref,
    outwide,
    outlow,
    in_sem,
    out_sem,
    kv_send,
    kv_recv,
    q_send,
    q_recv,
    do_send,
    do_recv,
    h_send,
    h_recv,
):
    me = lax.axis_index("seq")
    mine = lax.axis_index("head")
    both, tok = mats.shape[1], mats.shape[2]
    size = mats.shape[3]
    far = seqs * ROWS
    half = ROWS // 2
    quad = RATE3 * seg1 // tok
    scale = size ** (-0.5)
    scale2 = scale * LOG2E

    loads = []
    for at, (source, target) in enumerate(
        (
            (off_hbm, off_ref),
            (k_hbm, xin.at[0]),
            (v_hbm, xin.at[1]),
            (q_hbm, xin.at[2]),
            (c_hbm, xin.at[3]),
            (gain_hbm, gain_ref),
        )
    ):
        copy = pltpu.make_async_copy(source, target, in_sem.at[at])
        copy.start()
        loads.append(copy)
    kvbuf[...] = jnp.zeros_like(kvbuf)
    qbuf[...] = jnp.zeros_like(qbuf)
    dobuf[...] = jnp.zeros_like(dobuf)
    hbuf[...] = jnp.zeros_like(hbuf)

    barrier = pltpu.get_barrier_semaphore()
    for step in range(1, seqs):
        pl.semaphore_signal(
            barrier, inc=1, device_id=(lax.rem(me + step, seqs), mine), device_id_type=MESH
        )
    for step in range(1, heads):
        pl.semaphore_signal(
            barrier, inc=1, device_id=(me, lax.rem(mine + step, heads)), device_id_type=MESH
        )
    rows_ref[...] = jnp.zeros_like(rows_ref)
    stores = [
        pltpu.make_async_copy(outlow.at[at], target, out_sem.at[at])
        for at, target in enumerate((dq_hbm, dk_hbm, dv_hbm))
    ]

    def remote(source, target, send, recv, step, owner):
        return pltpu.make_async_remote_copy(
            src_ref=source,
            dst_ref=target,
            send_sem=send.at[step - 1],
            recv_sem=recv.at[step - 1],
            device_id=owner,
            device_id_type=MESH,
        )

    steps = range(1, seqs)
    later, earlier, kv_copies, q_copies, do_copies = {}, {}, {}, {}, {}
    for step in steps:
        up = (lax.rem(me + step, seqs), mine)
        down = (lax.rem(me + seqs - step, seqs), mine)
        later[step] = (
            (me + step < seqs) & ((me + step) // quad == me // quad),
            (me + step < seqs) & ((me + step) // quad != me // quad),
        )
        earlier[step] = (
            (me >= step) & ((me + seqs - step) // quad == (me + seqs) // quad),
            (me >= step) & ((me + seqs - step) // quad != (me + seqs) // quad),
        )
        top = pl.ds(0, ROWS)
        kv_copies[step] = (
            remote(kvsel, kvbuf.at[:, me], kv_send, kv_recv, step, up),
            remote(kvsel.at[:, top], kvbuf.at[:, me, top], kv_send, kv_recv, step, up),
        )
        q_copies[step] = (
            remote(qsel, qbuf.at[me], q_send, q_recv, step, down),
            remote(qsel.at[top], qbuf.at[me, top], q_send, q_recv, step, down),
        )
        top = pl.ds(0, 2 * ROWS)
        do_copies[step] = (
            remote(dosel, dobuf.at[me], do_send, do_recv, step, down),
            remote(dosel.at[top], dobuf.at[me, top], do_send, do_recv, step, down),
        )
    h_copies = [
        remote(hsend, hbuf.at[mine], h_send, h_recv, step, (me, lax.rem(mine + step, heads)))
        for step in range(1, heads)
    ]

    def each(side, copies, action):
        for step in steps:
            for which in range(2):
                if step >= quad and which == 0:
                    continue

                @pl.when(side[step][which])
                def _(step=step, which=which):
                    getattr(copies[step][which], action)()

    def per_head(mixed, h):
        groups = mixed.astype(jnp.float32).reshape(seqs, 2, both, half, size)
        return groups[:, :, h].reshape(far, size).astype(jnp.bfloat16)

    def select(at, g):
        rows = []
        for h in range(both):
            start = both * ((wanted[h] & (RATE4 - 1)) ^ (RATE3 * g)) + h
            rows.append(wide[at, pl.ds(start, half, stride=both * RATE4), :])
        return jnp.concatenate(rows, axis=0).astype(jnp.bfloat16)

    loads[0].wait()
    wanted = [off_ref[h] for h in range(both)]
    for at in range(2):
        loads[1 + at].wait()
        wide[at] = xin[at].astype(jnp.float32)
        for g in range(2):
            kvsel[at, pl.ds(g * ROWS, ROWS), :] = select(at, g)
    pl.semaphore_wait(barrier, seqs + heads - 2)
    each(later, kv_copies, "start")

    loads[3].wait()
    wide[2] = xin[2].astype(jnp.float32)
    for g in range(2):
        qsel[pl.ds(g * ROWS, ROWS), :] = select(2, g)
    each(earlier, q_copies, "start")

    for at in range(3):
        for h in range(both):
            mats[at, h] = wide[at, pl.ds(h, tok, stride=both), :].astype(jnp.bfloat16)

    lane = iota((tok, 128), 1)
    token = iota((tok, 128), 0)
    causal = iota((tok, tok), 0) <= iota((tok, tok), 1)
    for h in range(both):
        off = wanted[h]
        marks = (token // seg1) == lane
        marks = marks | ((lane == 64) & ((token & (RATE2 - 1)) == (off & (RATE2 - 1))))
        marks = marks | ((lane == 65) & ((token & (RATE3 - 1)) == (off & (RATE3 - 1))))
        marks = marks | ((lane == 66) & ((token & (RATE4 - 1)) == (off & (RATE4 - 1))))
        marked = jnp.where(marks, 1.0, 0.0).astype(jnp.bfloat16)
        count = dot_nt(marked, marked)
        bias[h] = bias_of(jnp.where(causal, count, 0.0))

    first_stats = []
    for h in range(both):
        score = dot_nt(mats[0, h], mats[2, h]) * scale2 + bias[h]
        peak = jnp.max(score, axis=0, keepdims=True)
        held = jnp.exp2(score - peak)
        weights[h] = held
        total = jnp.sum(held, axis=0, keepdims=True)
        out = dot_tn(mats[1, h], held.astype(jnp.bfloat16))
        first_stats.append((peak, total, out))

    loads[4].wait()
    loads[5].wait()
    wide[3] = xin[3].astype(jnp.float32)
    for h in range(both):
        grad = wide[3, pl.ds(h, tok, stride=both), :] * gain_ref[h : h + 1, :]
        grads[h] = grad.T

    for h in range(both):
        off = wanted[h]
        slot = iota((far, tok), 0) // ROWS
        query = iota((far, tok), 1)
        sel3 = (query & (RATE3 - 1)) == (off & (RATE3 - 1))
        sel4 = (query & (RATE4 - 1)) == (off & (RATE4 - 1))
        key4 = (iota((far, tok), 0) & half) == 0
        near = (slot // quad) == (me // quad)
        count = jnp.where(near & sel3, 1.0, 0.0) + jnp.where(key4 & sel4, 1.0, 0.0)
        far_bias[h] = bias_of(jnp.where(slot < me, count, 0.0))

    each(earlier, kv_copies, "wait_recv")

    sums = [jnp.zeros((1, tok), jnp.float32) for _ in range(4)]
    stats = []
    far_keys = [per_head(kvbuf[0], h) for h in range(both)]
    far_values = [per_head(kvbuf[1], h) for h in range(both)]
    for h in range(both):
        peak, total, out = first_stats[h]
        score = dot_nt(far_keys[h], mats[2, h]) * scale2 + far_bias[h]
        top = jnp.maximum(peak, jnp.max(score, axis=0, keepdims=True))
        shrink = jnp.exp2(peak - top)
        held = jnp.exp2(score - top)
        total = total * shrink + jnp.sum(held, axis=0, keepdims=True)
        ratio = 1.0 / total
        far_weights[h] = held * ratio
        out = (out * shrink + dot_tn(far_values[h], held.astype(jnp.bfloat16))) * ratio
        grad = grads[h]
        sums[0] = sums[0] + jnp.sum(out, axis=0, keepdims=True)
        sums[1] = sums[1] + jnp.sum(out * out, axis=0, keepdims=True)
        sums[2] = sums[2] + jnp.sum(grad, axis=0, keepdims=True)
        sums[3] = sums[3] + jnp.sum(grad * out, axis=0, keepdims=True)
        stats.append((out, shrink * ratio, top + jnp.log2(total)))
    for at in range(4):
        hsend[at : at + 1, :] = sums[at]
    for copy in h_copies:
        copy.start()

    for h in range(both):
        weights[h] = weights[h] * stats[h][1]
    row = iota((2 * ROWS, both * tok), 0)
    column = iota((2 * ROWS, both * tok), 1)
    head_of = (row // half) & 1
    start = jnp.where(head_of == 0, wanted[0], wanted[1]) & (RATE4 - 1)
    place = (start ^ (RATE3 * (row // ROWS))) + RATE4 * (row & (half - 1)) + tok * head_of
    picker[...] = jnp.where(column == place, 1.0, 0.0).astype(jnp.bfloat16)
    for h in range(both):
        token = iota((tok, far), 0)
        column = iota((tok, far), 1)
        start = (wanted[h] & (RATE4 - 1)) ^ (2 * (column & half))
        hit = (token == start + RATE4 * (column & (half - 1))) & (column // ROWS == me)
        placer[:, pl.ds(h * far, far)] = jnp.where(hit, 1.0, 0.0).astype(jnp.bfloat16)

    each(later, q_copies, "wait_recv")
    late_queries = [per_head(qbuf[...], h) for h in range(both)]
    for h in range(both):
        off = wanted[h]
        slot = iota((tok, far), 1) // ROWS
        key = iota((tok, far), 0)
        sel3 = (key & (RATE3 - 1)) == (off & (RATE3 - 1))
        sel4 = (key & (RATE4 - 1)) == (off & (RATE4 - 1))
        query4 = (iota((tok, far), 1) & half) == 0
        near = (slot // quad) == (me // quad)
        count = jnp.where(near & sel3, 1.0, 0.0) + jnp.where(query4 & sel4, 1.0, 0.0)
        late_bias = bias_of(jnp.where(slot > me, count, 0.0))
        late_score[h] = dot_nt(mats[0, h], late_queries[h]) * scale2 + late_bias

    for copy in h_copies:
        copy.wait_recv()
    full = hsend[...]
    for at in range(heads):
        full = full + hbuf[at]
    full = full * (1.0 / features)
    centre = full[0:1]
    inverse = lax.rsqrt(full[1:2] - centre * centre + epsilon)
    first = full[2:3]
    second = inverse * (full[3:4] - centre * first)

    douts = []
    for h in range(both):
        out, _, lse = stats[h]
        normed = (out - centre) * inverse
        dout = (inverse * (grads[h] - first - normed * second)).astype(jnp.bfloat16)
        delta = jnp.sum(dout.astype(jnp.float32) * out, axis=0, keepdims=True)
        for at, rest in enumerate((lse, delta)):
            for piece in range(3):
                part = rest.astype(jnp.bfloat16).astype(jnp.float32)
                rest = rest - part
                line = 8 * h + 2 * piece + at
                rows_ref[line : line + 1, :] = part
        douts.append((dout, delta))
    chosen = dot_nt(picker[...], jnp.concatenate([item[0] for item in douts], axis=1))
    moved = dot_nn(rows_ref[...].astype(jnp.bfloat16), placer[...])
    moved = jnp.concatenate([moved[0:8, 0:far], moved[8:16, far : 2 * far]], axis=0)
    dosel[0:ROWS, :] = chosen[0:ROWS].astype(jnp.bfloat16)
    dosel[ROWS : 2 * ROWS, :] = moved.astype(jnp.bfloat16)
    dosel[2 * ROWS : 3 * ROWS, :] = chosen[ROWS : 2 * ROWS].astype(jnp.bfloat16)
    each(earlier, do_copies, "start")

    key_parts = []
    for h in range(both):
        dout, delta = douts[h]
        weight = weights[h]
        weight_grad = dot_nn(mats[1, h], dout)
        score_grad = (weight * (weight_grad - delta)).astype(jnp.bfloat16)
        value_part = dot_nt(weight.astype(jnp.bfloat16), dout)
        key_part = dot_nn(score_grad, mats[2, h])
        far_grad = dot_nn(far_values[h], dout)
        far_score = (far_weights[h] * (far_grad - delta)).astype(jnp.bfloat16)
        query_part = dot_tn(mats[0, h], score_grad) + dot_tn(far_keys[h], far_score)
        outwide[0, pl.ds(h, tok, stride=both), :] = (query_part * scale).T
        key_parts.append((key_part, value_part))
    outlow[0] = outwide[0].astype(jnp.bfloat16)
    stores[0].start()

    each(later, do_copies, "wait_recv")

    arrived = dobuf[...].astype(jnp.float32)
    mixed = jnp.stack([arrived[:, 0:ROWS], arrived[:, 2 * ROWS : 3 * ROWS]], axis=1)
    lines = arrived[0, ROWS : 2 * ROWS]
    for at in range(1, seqs):
        lines = lines + arrived[at, ROWS : 2 * ROWS]
    for h in range(both):
        key_part, value_part = key_parts[h]
        late_douts = per_head(mixed, h)
        at = 8 * h
        lse = lines[at : at + 1] + lines[at + 2 : at + 3] + lines[at + 4 : at + 5]
        delta = lines[at + 1 : at + 2] + lines[at + 3 : at + 4] + lines[at + 5 : at + 6]
        weight = jnp.exp2(late_score[h] - lse)
        weight_grad = dot_nt(mats[1, h], late_douts)
        score_grad = (weight * (weight_grad - delta)).astype(jnp.bfloat16)
        value_part = value_part + dot_nn(weight.astype(jnp.bfloat16), late_douts)
        key_part = key_part + dot_nn(score_grad, late_queries[h])
        outwide[1, pl.ds(h, tok, stride=both), :] = key_part * scale
        outwide[2, pl.ds(h, tok, stride=both), :] = value_part
    for at in range(1, 3):
        outlow[at] = outwide[at].astype(jnp.bfloat16)
        stores[at].start()

    each(later, kv_copies, "wait_send")
    each(earlier, q_copies, "wait_send")
    each(earlier, do_copies, "wait_send")
    for copy in h_copies:
        copy.wait_send()
    for copy in stores:
        copy.wait()


def place_outputs(dq_ref, dk_ref, dv_ref, dq_hbm, dk_hbm, dv_hbm, sem):
    copies = [
        pltpu.make_async_copy(source, target, sem.at[at])
        for at, (source, target) in enumerate(
            ((dq_ref, dq_hbm), (dk_ref, dk_hbm), (dv_ref, dv_hbm))
        )
    ]
    for copy in copies:
        copy.start()
    for copy in copies:
        copy.wait()


def fused_shards(query_rows, key_rows, value_rows, cotangent, norm_gain, offsets):
    tok, both, size = query_rows.shape
    seqs = lax.axis_size("seq")
    heads = lax.axis_size("head")
    seg1 = tok * seqs // RATE4
    far = seqs * ROWS
    flat = (both * tok, size)
    low, full = jnp.bfloat16, jnp.float32
    hbm = pl.BlockSpec(memory_space=pltpu.HBM)
    outs = pl.pallas_call(
        functools.partial(fused, seqs, heads, seg1, both * size * heads),
        out_shape=[jax.ShapeDtypeStruct(flat, low)] * 3,
        in_specs=[hbm] * 6,
        out_specs=[hbm] * 3,
        scratch_shapes=[
            pltpu.SMEM((both,), jnp.int32),
            pltpu.VMEM((both, size), full),
            pltpu.VMEM((4,) + flat, low),
            pltpu.VMEM((4,) + flat, full),
            pltpu.VMEM((3, both, tok, size), low),
            pltpu.VMEM((both, size, tok), full),
            pltpu.VMEM((both, tok, tok), full),
            pltpu.VMEM((both, far, tok), full),
            pltpu.VMEM((both, tok, tok), full),
            pltpu.VMEM((both, far, tok), full),
            pltpu.VMEM((both, tok, far), full),
            pltpu.VMEM((2 * ROWS, both * tok), low),
            pltpu.VMEM((tok, both * far), low),
            pltpu.VMEM((2, 2 * ROWS, size), low),
            pltpu.VMEM((2 * ROWS, size), low),
            pltpu.VMEM((3 * ROWS, size), low),
            pltpu.VMEM((2, seqs, 2 * ROWS, size), low),
            pltpu.VMEM((seqs, 2 * ROWS, size), low),
            pltpu.VMEM((seqs, 3 * ROWS, size), low),
            pltpu.VMEM((4, tok), full),
            pltpu.VMEM((heads, 4, tok), full),
            pltpu.VMEM((8 * both, tok), full),
            pltpu.VMEM((3,) + flat, full),
            pltpu.VMEM((3,) + flat, low),
            pltpu.SemaphoreType.DMA((6,)),
            pltpu.SemaphoreType.DMA((3,)),
        ]
        + [pltpu.SemaphoreType.DMA((seqs - 1,))] * 6
        + [pltpu.SemaphoreType.DMA((heads - 1,))] * 2,
        compiler_params=pltpu.CompilerParams(
            collective_id=0, has_side_effects=True, vmem_limit_bytes=VMEM_BYTES
        ),
        name="fused_backward",
    )(
        offsets,
        query_rows.reshape(flat),
        key_rows.reshape(flat),
        value_rows.reshape(flat),
        cotangent.reshape(flat),
        norm_gain,
    )
    outs = pl.pallas_call(
        place_outputs,
        out_shape=[jax.ShapeDtypeStruct(flat, low)] * 3,
        in_specs=[hbm] * 3,
        out_specs=[hbm] * 3,
        scratch_shapes=[pltpu.SemaphoreType.DMA((3,))],
        compiler_params=pltpu.CompilerParams(vmem_limit_bytes=VMEM_BYTES),
        name="place_outputs",
    )(*outs)
    return tuple(out.reshape(query_rows.shape) for out in outs)


def fits(mesh, tok, both, size):
    seqs = mesh.shape["seq"]
    seg1 = tok * seqs // RATE4
    return (
        tok == ROWS * RATE3
        and size == 128
        and both == 2
        and seqs * ROWS == 128
        and tok % (RATE2 * seg1) == 0
        and (RATE3 * seg1) % tok == 0
        and tok // seg1 <= 64
    )


def solution(mesh):
    placed = (
        P("seq", "head", None),
        P("seq", "head", None),
        P("seq", "head", None),
        P("seq", "head", None),
        P("head", None),
        P("head"),
    )

    def run(query_rows, key_rows, value_rows, cotangent, norm_gain, offsets):
        tokens, heads, size = query_rows.shape
        small = fits(mesh, tokens // mesh.shape["seq"], heads // mesh.shape["head"], size)
        return jax.shard_map(
            fused_shards if small else shards,
            mesh=mesh,
            in_specs=placed,
            out_specs=(P("seq", "head", None), P("seq", "head", None), P("seq", "head", None)),
            check_vma=False,
        )(query_rows, key_rows, value_rows, cotangent, norm_gain, offsets)

    return run
```

```python
import functools

import jax
import jax.numpy as jnp
from jax import lax
from jax.experimental import pallas as pl
from jax.experimental.pallas import tpu as pltpu
from jax.sharding import PartitionSpec as P

RATE2 = 4
RATE3 = 16
RATE4 = 32


neg_fill = -1e30
epsilon = 1e-05
block_width = 512


def passed_along(value, axis, steps):
    count = lax.axis_size(axis)
    leading, last = (max(0, -steps), min(count, count - steps))
    return lax.ppermute(value, axis, [(source, source + steps) for source in range(leading, last)])


def pick_rows(source, wanted, stride):
    row_count = source.shape[0] // stride
    shaped = source.reshape((row_count, stride) + source.shape[1:])
    trailing = (1,) * (source.ndim - 2)
    target = wanted.reshape((1, 1, -1) + trailing)
    column = jnp.arange(stride, dtype=jnp.int32).reshape((1, stride, 1) + trailing)
    zeroed = jnp.where(column == target, shaped, jnp.zeros((), source.dtype))
    return jnp.sum(zeroed, axis=1, dtype=source.dtype)


def put_rows(compact, wanted, stride, filler):
    trailing = (1,) * (compact.ndim - 2)
    target = wanted.reshape((1, 1, -1) + trailing)
    column = jnp.arange(stride, dtype=jnp.int32).reshape((1, stride, 1) + trailing)
    spread = jnp.where(column == target, compact[:, None], jnp.asarray(filler, compact.dtype))
    return spread.reshape((compact.shape[0] * stride,) + compact.shape[1:])


def row_places(device, slot_count, direction, row_count, stride, wanted, tok_dev):
    owners = device + direction * jnp.arange(slot_count, dtype=jnp.int32)
    within_dev = wanted[None, :] + stride * jnp.arange(row_count, dtype=jnp.int32)[:, None]
    places = owners[:, None, None] * tok_dev + within_dev[None]
    return places.reshape(slot_count * row_count, wanted.shape[0])


def masked_scores(query_blk, key_blk, query_pos, key_pos, seg_len, score_scale):
    raw = (
        jnp.einsum("qhd,khd->hqk", query_blk, key_blk, preferred_element_type=jnp.float32)
        * score_scale
    )
    query_at = query_pos.T[:, :, None]
    key_at = key_pos.T[:, None, :]
    linked = (query_at // seg_len == key_at // seg_len) & (key_at <= query_at)
    return jnp.where(linked, raw, neg_fill)


def flatten_slots(member):
    return member.reshape((member.shape[0] * member.shape[1],) + member.shape[2:])


def extend(buffers, target, sign, puller):
    while buffers[0].shape[0] < target:
        covered = buffers[0].shape[0]
        arrived = puller(buffers, sign * covered)
        buffers = tuple(
            (jnp.concatenate([held, current], axis=0) for held, current in zip(buffers, arrived))
        )
    return buffers


def pull_keys(buffers, offset):
    return passed_along((buffers[0], buffers[1]), "seq", offset)


def pull_queries(buffers, offset):
    moved = passed_along((buffers[0], buffers[1]), "seq", offset)
    stats = passed_along((buffers[2], buffers[3]), "seq", offset)
    return (moved[0], moved[1], stats[0], stats[1])


def feature_sums(first, second):
    return lax.psum((first, second), "head")


def shards(query_rows, key_rows, value_rows, cotangent, norm_gain, offsets):
    tok_dev, heads_dev, head_size = query_rows.shape
    seq_count = lax.axis_size("seq")
    device = lax.axis_index("seq")
    group_rows = tok_dev * seq_count // RATE4
    score_scale = head_size ** (-0.5)
    features = heads_dev * head_size * lax.axis_size("head")
    levels = []
    for stride in (1, RATE2, RATE3, RATE4):
        seg_len = stride * group_rows
        levels.append((stride, seg_len, max(1, seg_len // tok_dev), offsets % stride))
    key_sets = []
    for stride, seg_len, span_devices, wanted in levels:
        own_rows = (
            pick_rows(key_rows, wanted, stride)[None],
            pick_rows(value_rows, wanted, stride)[None],
        )
        key_sets.append(extend(own_rows, span_devices, 1, pull_keys))
    prepared = []
    for (stride, seg_len, span_devices, wanted), key_set in zip(levels, key_sets):
        row_count = tok_dev // stride
        key_flat = flatten_slots(key_set[0])
        value_flat = flatten_slots(key_set[1])
        key_places = row_places(device, key_set[0].shape[0], -1, row_count, stride, wanted, tok_dev)
        query_sel = pick_rows(query_rows, wanted, stride)
        query_places = row_places(device, 1, -1, row_count, stride, wanted, tok_dev)
        prepared.append(
            (
                stride,
                seg_len,
                span_devices,
                wanted,
                row_count,
                key_flat,
                value_flat,
                key_places,
                query_sel,
                query_places,
            )
        )
    lse_total = jnp.full((tok_dev, heads_dev), neg_fill, jnp.float32)
    for (
        stride,
        seg_len,
        span_devices,
        wanted,
        row_count,
        key_flat,
        value_flat,
        key_places,
        query_sel,
        query_places,
    ) in prepared:
        level_lse = jnp.full((row_count, heads_dev), neg_fill, jnp.float32)
        for first_row in range(0, key_flat.shape[0], block_width):
            scores = masked_scores(
                query_sel,
                key_flat[first_row : first_row + block_width],
                query_places,
                key_places[first_row : first_row + block_width],
                seg_len,
                score_scale,
            )
            row_peak = jnp.max(scores, axis=2)
            block_lse = row_peak + jnp.log(jnp.sum(jnp.exp(scores - row_peak[:, :, None]), axis=2))
            level_lse = jnp.logaddexp(level_lse, block_lse.T)
        lse_total = jnp.logaddexp(lse_total, put_rows(level_lse, wanted, stride, neg_fill))
    attended = jnp.zeros((tok_dev, heads_dev, head_size), jnp.float32)
    for (
        stride,
        seg_len,
        span_devices,
        wanted,
        row_count,
        key_flat,
        value_flat,
        key_places,
        query_sel,
        query_places,
    ) in prepared:
        lse_sel = pick_rows(lse_total, wanted, stride)
        out_sel = jnp.zeros((row_count, heads_dev, head_size), jnp.float32)
        for first_row in range(0, key_flat.shape[0], block_width):
            scores = masked_scores(
                query_sel,
                key_flat[first_row : first_row + block_width],
                query_places,
                key_places[first_row : first_row + block_width],
                seg_len,
                score_scale,
            )
            weights = jnp.exp(scores - lse_sel.T[:, :, None]).astype(jnp.bfloat16)
            out_sel = out_sel + jnp.einsum(
                "hqk,khd->qhd",
                weights,
                value_flat[first_row : first_row + block_width],
                preferred_element_type=jnp.float32,
            )
        attended = attended + put_rows(out_sel, wanted, stride, 0.0)
    totals = feature_sums(jnp.sum(attended, axis=(1, 2)), jnp.sum(attended * attended, axis=(1, 2)))
    centre = totals[0] / features
    variance = totals[1] / features - centre * centre
    inverse = lax.rsqrt(variance + epsilon)
    normed = (attended - centre[:, None, None]) * inverse[:, None, None]
    grad_in = cotangent.astype(jnp.float32) * norm_gain[None]
    moments = feature_sums(jnp.sum(grad_in, axis=(1, 2)), jnp.sum(grad_in * normed, axis=(1, 2)))
    first_mean = moments[0] / features
    second_mean = moments[1] / features
    d_attended = (
        inverse[:, None, None]
        * (grad_in - first_mean[:, None, None] - normed * second_mean[:, None, None])
    ).astype(jnp.bfloat16)
    row_delta = jnp.sum(d_attended.astype(jnp.float32) * attended, axis=2)
    query_grad = jnp.zeros((tok_dev, heads_dev, head_size), jnp.float32)
    for (
        stride,
        seg_len,
        span_devices,
        wanted,
        row_count,
        key_flat,
        value_flat,
        key_places,
        query_sel,
        query_places,
    ) in prepared:
        lse_sel = pick_rows(lse_total, wanted, stride)
        dout_sel = pick_rows(d_attended, wanted, stride)
        delta_sel = pick_rows(row_delta, wanted, stride)
        grad_sel = jnp.zeros((row_count, heads_dev, head_size), jnp.float32)
        for first_row in range(0, key_flat.shape[0], block_width):
            key_block = key_flat[first_row : first_row + block_width]
            scores = masked_scores(
                query_sel,
                key_block,
                query_places,
                key_places[first_row : first_row + block_width],
                seg_len,
                score_scale,
            )
            weights = jnp.exp(scores - lse_sel.T[:, :, None])
            weight_grad = jnp.einsum(
                "qhd,khd->hqk",
                dout_sel,
                value_flat[first_row : first_row + block_width],
                preferred_element_type=jnp.float32,
            )
            score_grad = (weights * (weight_grad - delta_sel.T[:, :, None])).astype(jnp.bfloat16)
            grad_sel = grad_sel + jnp.einsum(
                "hqk,khd->qhd", score_grad, key_block, preferred_element_type=jnp.float32
            )
        query_grad = query_grad + put_rows(grad_sel * score_scale, wanted, stride, 0.0)
    query_sets = []
    for stride, seg_len, span_devices, wanted in levels:
        own_rows = (
            pick_rows(query_rows, wanted, stride)[None],
            pick_rows(d_attended, wanted, stride)[None],
            pick_rows(lse_total, wanted, stride)[None],
            pick_rows(row_delta, wanted, stride)[None],
        )
        query_sets.append(extend(own_rows, span_devices, -1, pull_queries))
    key_grad = jnp.zeros((tok_dev, heads_dev, head_size), jnp.float32)
    value_grad = jnp.zeros((tok_dev, heads_dev, head_size), jnp.float32)
    for (
        stride,
        seg_len,
        span_devices,
        wanted,
        row_count,
        key_flat,
        value_flat,
        key_places,
        query_sel,
        query_places,
    ), query_set in zip(prepared, query_sets):
        query_flat = flatten_slots(query_set[0])
        dout_flat = flatten_slots(query_set[1])
        lse_flat = flatten_slots(query_set[2])
        delta_flat = flatten_slots(query_set[3])
        query_far = row_places(device, query_set[0].shape[0], 1, row_count, stride, wanted, tok_dev)
        key_sel = pick_rows(key_rows, wanted, stride)
        value_sel = pick_rows(value_rows, wanted, stride)
        key_grad_sel = jnp.zeros((row_count, heads_dev, head_size), jnp.float32)
        value_grad_sel = jnp.zeros((row_count, heads_dev, head_size), jnp.float32)
        for first_row in range(0, query_flat.shape[0], block_width):
            query_block = query_flat[first_row : first_row + block_width]
            dout_block = dout_flat[first_row : first_row + block_width]
            lse_block = lse_flat[first_row : first_row + block_width]
            delta_block = delta_flat[first_row : first_row + block_width]
            scores = masked_scores(
                query_block,
                key_sel,
                query_far[first_row : first_row + block_width],
                query_places,
                seg_len,
                score_scale,
            )
            weights = jnp.exp(scores - lse_block.T[:, :, None])
            value_grad_sel = value_grad_sel + jnp.einsum(
                "hqk,qhd->khd",
                weights.astype(jnp.bfloat16),
                dout_block,
                preferred_element_type=jnp.float32,
            )
            weight_grad = jnp.einsum(
                "qhd,khd->hqk", dout_block, value_sel, preferred_element_type=jnp.float32
            )
            score_grad = (weights * (weight_grad - delta_block.T[:, :, None])).astype(jnp.bfloat16)
            key_grad_sel = key_grad_sel + jnp.einsum(
                "hqk,qhd->khd", score_grad, query_block, preferred_element_type=jnp.float32
            )
        key_grad = key_grad + put_rows(key_grad_sel * score_scale, wanted, stride, 0.0)
        value_grad = value_grad + put_rows(value_grad_sel, wanted, stride, 0.0)
    return (
        query_grad.astype(jnp.bfloat16),
        key_grad.astype(jnp.bfloat16),
        value_grad.astype(jnp.bfloat16),
    )

MESH = pl.DeviceIdType.MESH
LOG2E = 1.4426950408889634
HIDDEN = -1e30
ROWS = 16
VMEM_BYTES = 54752 * 1024


def dot_nn(a, b):
    return lax.dot_general(a, b, (((1,), (0,)), ((), ())), preferred_element_type=jnp.float32)


def dot_nt(a, b):
    return lax.dot_general(a, b, (((1,), (1,)), ((), ())), preferred_element_type=jnp.float32)


def dot_tn(a, b):
    return lax.dot_general(a, b, (((0,), (0,)), ((), ())), preferred_element_type=jnp.float32)


def iota(shape, axis):
    return lax.broadcasted_iota(jnp.int32, shape, axis)


def bias_of(count):
    return jnp.where(count > 0.5, jnp.log2(jnp.maximum(count, 1.0)), HIDDEN)


def fused(
    seqs,
    heads,
    seg1,
    features,
    off_hbm,
    q_hbm,
    k_hbm,
    v_hbm,
    c_hbm,
    gain_hbm,
    dq_ref,
    dk_ref,
    dv_ref,
    off_ref,
    gain_ref,
    xin,
    wide,
    mats,
    grads,
    weights,
    far_weights,
    bias,
    far_bias,
    late_score,
    picker,
    placer,
    kvsel,
    qsel,
    dosel,
    kvbuf,
    qbuf,
    dobuf,
    hsend,
    hbuf,
    rows_ref,
    outwide,
    in_sem,
    kv_send,
    kv_recv,
    q_send,
    q_recv,
    do_send,
    do_recv,
    h_send,
    h_recv,
):
    me = lax.axis_index("seq")
    mine = lax.axis_index("head")
    both, tok = mats.shape[1], mats.shape[2]
    size = mats.shape[3]
    far = seqs * ROWS
    half = ROWS // 2
    quad = RATE3 * seg1 // tok
    scale = size ** (-0.5)
    scale2 = scale * LOG2E

    loads = []
    for at, (source, target) in enumerate(
        (
            (off_hbm, off_ref),
            (k_hbm, xin.at[0]),
            (v_hbm, xin.at[1]),
            (q_hbm, xin.at[2]),
            (c_hbm, xin.at[3]),
            (gain_hbm, gain_ref),
        )
    ):
        copy = pltpu.make_async_copy(source, target, in_sem.at[at])
        copy.start()
        loads.append(copy)
    kvbuf[...] = jnp.zeros_like(kvbuf)
    qbuf[...] = jnp.zeros_like(qbuf)
    dobuf[...] = jnp.zeros_like(dobuf)
    hbuf[...] = jnp.zeros_like(hbuf)

    barrier = pltpu.get_barrier_semaphore()
    for step in range(1, seqs):
        pl.semaphore_signal(
            barrier, inc=1, device_id=(lax.rem(me + step, seqs), mine), device_id_type=MESH
        )
    for step in range(1, heads):
        pl.semaphore_signal(
            barrier, inc=1, device_id=(me, lax.rem(mine + step, heads)), device_id_type=MESH
        )
    rows_ref[...] = jnp.zeros_like(rows_ref)

    def remote(source, target, send, recv, step, owner):
        return pltpu.make_async_remote_copy(
            src_ref=source,
            dst_ref=target,
            send_sem=send.at[step - 1],
            recv_sem=recv.at[step - 1],
            device_id=owner,
            device_id_type=MESH,
        )

    steps = range(1, seqs)
    later, earlier, kv_copies, q_copies, do_copies = {}, {}, {}, {}, {}
    for step in steps:
        up = (lax.rem(me + step, seqs), mine)
        down = (lax.rem(me + seqs - step, seqs), mine)
        later[step] = (
            (me + step < seqs) & ((me + step) // quad == me // quad),
            (me + step < seqs) & ((me + step) // quad != me // quad),
        )
        earlier[step] = (
            (me >= step) & ((me + seqs - step) // quad == (me + seqs) // quad),
            (me >= step) & ((me + seqs - step) // quad != (me + seqs) // quad),
        )
        top = pl.ds(0, ROWS)
        kv_copies[step] = (
            remote(kvsel, kvbuf.at[:, me], kv_send, kv_recv, step, up),
            remote(kvsel.at[:, top], kvbuf.at[:, me, top], kv_send, kv_recv, step, up),
        )
        q_copies[step] = (
            remote(qsel, qbuf.at[me], q_send, q_recv, step, down),
            remote(qsel.at[top], qbuf.at[me, top], q_send, q_recv, step, down),
        )
        top = pl.ds(0, 2 * ROWS)
        do_copies[step] = (
            remote(dosel, dobuf.at[me], do_send, do_recv, step, down),
            remote(dosel.at[top], dobuf.at[me, top], do_send, do_recv, step, down),
        )
    h_copies = [
        remote(hsend, hbuf.at[mine], h_send, h_recv, step, (me, lax.rem(mine + step, heads)))
        for step in range(1, heads)
    ]

    def each(side, copies, action):
        for step in reversed(steps):
            for which in range(2):
                if step >= quad and which == 0:
                    continue

                @pl.when(side[step][which])
                def _(step=step, which=which):
                    getattr(copies[step][which], action)()

    def per_head(mixed, h):
        groups = mixed.astype(jnp.float32).reshape(seqs, 2, both, half, size)
        return groups[:, :, h].reshape(far, size).astype(jnp.bfloat16)

    def select(at, g):
        rows = []
        for h in range(both):
            start = both * ((wanted[h] & (RATE4 - 1)) ^ (RATE3 * g)) + h
            rows.append(wide[at, pl.ds(start, half, stride=both * RATE4), :])
        return jnp.concatenate(rows, axis=0).astype(jnp.bfloat16)

    loads[0].wait()
    wanted = [off_ref[h] for h in range(both)]

    lane = iota((tok, 128), 1)
    token = iota((tok, 128), 0)
    causal = iota((tok, tok), 0) <= iota((tok, tok), 1)
    for h in range(both):
        off = wanted[h]
        marks = (token // seg1) == lane
        marks = marks | ((lane == 64) & ((token & (RATE2 - 1)) == (off & (RATE2 - 1))))
        marks = marks | ((lane == 65) & ((token & (RATE3 - 1)) == (off & (RATE3 - 1))))
        marks = marks | ((lane == 66) & ((token & (RATE4 - 1)) == (off & (RATE4 - 1))))
        marked = jnp.where(marks, 1.0, 0.0).astype(jnp.bfloat16)
        count = dot_nt(marked, marked)
        bias[h] = bias_of(jnp.where(causal, count, 0.0))

    for at in range(2):
        loads[1 + at].wait()
        wide[at] = xin[at].astype(jnp.float32)
        for g in range(2):
            kvsel[at, pl.ds(g * ROWS, ROWS), :] = select(at, g)
    pl.semaphore_wait(barrier, seqs + heads - 2)
    each(later, kv_copies, "start")

    loads[3].wait()
    wide[2] = xin[2].astype(jnp.float32)
    for g in range(2):
        qsel[pl.ds(g * ROWS, ROWS), :] = select(2, g)
    each(earlier, q_copies, "start")

    for at in range(3):
        for h in range(both):
            mats[at, h] = wide[at, pl.ds(h, tok, stride=both), :].astype(jnp.bfloat16)

    first_stats = []
    for h in range(both):
        score = dot_nt(mats[0, h], mats[2, h]) * scale2 + bias[h]
        peak = jnp.max(score, axis=0, keepdims=True)
        held = jnp.exp2(score - peak)
        weights[h] = held
        total = jnp.sum(held, axis=0, keepdims=True)
        out = dot_tn(mats[1, h], held.astype(jnp.bfloat16))
        first_stats.append((peak, total, out))

    loads[4].wait()
    loads[5].wait()
    wide[3] = xin[3].astype(jnp.float32)
    for h in range(both):
        grad = wide[3, pl.ds(h, tok, stride=both), :] * gain_ref[h : h + 1, :]
        grads[h] = grad.T

    for h in range(both):
        off = wanted[h]
        slot = iota((far, tok), 0) // ROWS
        query = iota((far, tok), 1)
        sel3 = (query & (RATE3 - 1)) == (off & (RATE3 - 1))
        sel4 = (query & (RATE4 - 1)) == (off & (RATE4 - 1))
        key4 = (iota((far, tok), 0) & half) == 0
        near = (slot // quad) == (me // quad)
        count = jnp.where(near & sel3, 1.0, 0.0) + jnp.where(key4 & sel4, 1.0, 0.0)
        far_bias[h] = bias_of(jnp.where(slot < me, count, 0.0))

    each(earlier, kv_copies, "wait_recv")

    sums = [jnp.zeros((1, tok), jnp.float32) for _ in range(4)]
    stats = []
    far_keys = [per_head(kvbuf[0], h) for h in range(both)]
    far_values = [per_head(kvbuf[1], h) for h in range(both)]
    for h in range(both):
        peak, total, out = first_stats[h]
        score = dot_nt(far_keys[h], mats[2, h]) * scale2 + far_bias[h]
        top = jnp.maximum(peak, jnp.max(score, axis=0, keepdims=True))
        shrink = jnp.exp2(peak - top)
        held = jnp.exp2(score - top)
        total = total * shrink + jnp.sum(held, axis=0, keepdims=True)
        ratio = 1.0 / total
        far_weights[h] = held * ratio
        out = (out * shrink + dot_tn(far_values[h], held.astype(jnp.bfloat16))) * ratio
        grad = grads[h]
        sums[0] = sums[0] + jnp.sum(out, axis=0, keepdims=True)
        sums[1] = sums[1] + jnp.sum(out * out, axis=0, keepdims=True)
        sums[2] = sums[2] + jnp.sum(grad, axis=0, keepdims=True)
        sums[3] = sums[3] + jnp.sum(grad * out, axis=0, keepdims=True)
        stats.append((out, shrink * ratio, top + jnp.log2(total)))
    for at in range(4):
        hsend[at : at + 1, :] = sums[at]
    for copy in h_copies:
        copy.start()

    for h in range(both):
        weights[h] = weights[h] * stats[h][1]
    row = iota((2 * ROWS, both * tok), 0)
    column = iota((2 * ROWS, both * tok), 1)
    head_of = (row // half) & 1
    start = jnp.where(head_of == 0, wanted[0], wanted[1]) & (RATE4 - 1)
    place = (start ^ (RATE3 * (row // ROWS))) + RATE4 * (row & (half - 1)) + tok * head_of
    picker[...] = jnp.where(column == place, 1.0, 0.0).astype(jnp.bfloat16)
    for h in range(both):
        token = iota((tok, far), 0)
        column = iota((tok, far), 1)
        start = (wanted[h] & (RATE4 - 1)) ^ (2 * (column & half))
        hit = (token == start + RATE4 * (column & (half - 1))) & (column // ROWS == me)
        placer[:, pl.ds(h * far, far)] = jnp.where(hit, 1.0, 0.0).astype(jnp.bfloat16)

    each(later, q_copies, "wait_recv")
    late_queries = [per_head(qbuf[...], h) for h in range(both)]
    for h in range(both):
        off = wanted[h]
        slot = iota((tok, far), 1) // ROWS
        key = iota((tok, far), 0)
        sel3 = (key & (RATE3 - 1)) == (off & (RATE3 - 1))
        sel4 = (key & (RATE4 - 1)) == (off & (RATE4 - 1))
        query4 = (iota((tok, far), 1) & half) == 0
        near = (slot // quad) == (me // quad)
        count = jnp.where(near & sel3, 1.0, 0.0) + jnp.where(query4 & sel4, 1.0, 0.0)
        late_bias = bias_of(jnp.where(slot > me, count, 0.0))
        late_score[h] = dot_nt(mats[0, h], late_queries[h]) * scale2 + late_bias

    for copy in h_copies:
        copy.wait_recv()
    full = hsend[...]
    for at in range(heads):
        full = full + hbuf[at]
    full = full * (1.0 / features)
    centre = full[0:1]
    inverse = lax.rsqrt(full[1:2] - centre * centre + epsilon)
    first = full[2:3]
    second = inverse * (full[3:4] - centre * first)

    douts = []
    for h in range(both):
        out, _, lse = stats[h]
        normed = (out - centre) * inverse
        dout = (inverse * (grads[h] - first - normed * second)).astype(jnp.bfloat16)
        delta = jnp.sum(dout.astype(jnp.float32) * out, axis=0, keepdims=True)
        for at, rest in enumerate((lse, delta)):
            for piece in range(3):
                part = rest.astype(jnp.bfloat16).astype(jnp.float32)
                rest = rest - part
                line = 8 * h + 2 * piece + at
                rows_ref[line : line + 1, :] = part
        douts.append((dout, delta))
    chosen = dot_nt(picker[...], jnp.concatenate([item[0] for item in douts], axis=1))
    moved = dot_nn(rows_ref[...].astype(jnp.bfloat16), placer[...])
    moved = jnp.concatenate([moved[0:8, 0:far], moved[8:16, far : 2 * far]], axis=0)
    dosel[0:ROWS, :] = chosen[0:ROWS].astype(jnp.bfloat16)
    dosel[ROWS : 2 * ROWS, :] = moved.astype(jnp.bfloat16)
    dosel[2 * ROWS : 3 * ROWS, :] = chosen[ROWS : 2 * ROWS].astype(jnp.bfloat16)
    each(earlier, do_copies, "start")

    key_parts = []
    for h in range(both):
        dout, delta = douts[h]
        weight = weights[h]
        weight_grad = dot_nn(mats[1, h], dout)
        score_grad = (weight * (weight_grad - delta)).astype(jnp.bfloat16)
        value_part = dot_nt(weight.astype(jnp.bfloat16), dout)
        key_part = dot_nn(score_grad, mats[2, h])
        far_grad = dot_nn(far_values[h], dout)
        far_score = (far_weights[h] * (far_grad - delta)).astype(jnp.bfloat16)
        query_part = dot_tn(mats[0, h], score_grad) + dot_tn(far_keys[h], far_score)
        outwide[0, pl.ds(h, tok, stride=both), :] = (query_part * scale).T
        key_parts.append((key_part, value_part))
    dq_ref[...] = outwide[0].astype(jnp.bfloat16)

    each(later, do_copies, "wait_recv")

    arrived = dobuf[...].astype(jnp.float32)
    mixed = jnp.stack([arrived[:, 0:ROWS], arrived[:, 2 * ROWS : 3 * ROWS]], axis=1)
    lines = arrived[0, ROWS : 2 * ROWS]
    for at in range(1, seqs):
        lines = lines + arrived[at, ROWS : 2 * ROWS]
    for h in range(both):
        key_part, value_part = key_parts[h]
        late_douts = per_head(mixed, h)
        at = 8 * h
        lse = lines[at : at + 1] + lines[at + 2 : at + 3] + lines[at + 4 : at + 5]
        delta = lines[at + 1 : at + 2] + lines[at + 3 : at + 4] + lines[at + 5 : at + 6]
        weight = jnp.exp2(late_score[h] - lse)
        weight_grad = dot_nt(mats[1, h], late_douts)
        score_grad = (weight * (weight_grad - delta)).astype(jnp.bfloat16)
        value_part = value_part + dot_nn(weight.astype(jnp.bfloat16), late_douts)
        key_part = key_part + dot_nn(score_grad, late_queries[h])
        outwide[1, pl.ds(h, tok, stride=both), :] = key_part * scale
        outwide[2, pl.ds(h, tok, stride=both), :] = value_part
    dk_ref[...] = outwide[1].astype(jnp.bfloat16)
    dv_ref[...] = outwide[2].astype(jnp.bfloat16)

    each(later, kv_copies, "wait_send")
    each(earlier, q_copies, "wait_send")
    each(earlier, do_copies, "wait_send")
    for copy in h_copies:
        copy.wait_send()


def place_outputs(dq_ref, dk_ref, dv_ref, dq_hbm, dk_hbm, dv_hbm, sem):
    copies = [
        pltpu.make_async_copy(source, target, sem.at[at])
        for at, (source, target) in enumerate(
            ((dq_ref, dq_hbm), (dk_ref, dk_hbm), (dv_ref, dv_hbm))
        )
    ]
    for copy in copies:
        copy.start()
    for copy in copies:
        copy.wait()


def fused_shards(query_rows, key_rows, value_rows, cotangent, norm_gain, offsets):
    tok, both, size = query_rows.shape
    seqs = lax.axis_size("seq")
    heads = lax.axis_size("head")
    seg1 = tok * seqs // RATE4
    far = seqs * ROWS
    flat = (both * tok, size)
    low, full = jnp.bfloat16, jnp.float32
    vmem = pl.BlockSpec(memory_space=pltpu.VMEM)
    hbm = pl.BlockSpec(memory_space=pltpu.HBM)
    outs = pl.pallas_call(
        functools.partial(fused, seqs, heads, seg1, both * size * heads),
        out_shape=[jax.ShapeDtypeStruct(flat, low)] * 3,
        in_specs=[hbm] * 6,
        out_specs=[vmem] * 3,
        scratch_shapes=[
            pltpu.SMEM((both,), jnp.int32),
            pltpu.VMEM((both, size), full),
            pltpu.VMEM((4,) + flat, low),
            pltpu.VMEM((4,) + flat, full),
            pltpu.VMEM((3, both, tok, size), low),
            pltpu.VMEM((both, size, tok), full),
            pltpu.VMEM((both, tok, tok), full),
            pltpu.VMEM((both, far, tok), full),
            pltpu.VMEM((both, tok, tok), full),
            pltpu.VMEM((both, far, tok), full),
            pltpu.VMEM((both, tok, far), full),
            pltpu.VMEM((2 * ROWS, both * tok), low),
            pltpu.VMEM((tok, both * far), low),
            pltpu.VMEM((2, 2 * ROWS, size), low),
            pltpu.VMEM((2 * ROWS, size), low),
            pltpu.VMEM((3 * ROWS, size), low),
            pltpu.VMEM((2, seqs, 2 * ROWS, size), low),
            pltpu.VMEM((seqs, 2 * ROWS, size), low),
            pltpu.VMEM((seqs, 3 * ROWS, size), low),
            pltpu.VMEM((4, tok), full),
            pltpu.VMEM((heads, 4, tok), full),
            pltpu.VMEM((8 * both, tok), full),
            pltpu.VMEM((3,) + flat, full),
            pltpu.SemaphoreType.DMA((6,)),
        ]
        + [pltpu.SemaphoreType.DMA((seqs - 1,))] * 6
        + [pltpu.SemaphoreType.DMA((heads - 1,))] * 2,
        compiler_params=pltpu.CompilerParams(
            collective_id=0, has_side_effects=True, vmem_limit_bytes=VMEM_BYTES
        ),
        name="fused_backward",
    )(
        offsets,
        query_rows.reshape(flat),
        key_rows.reshape(flat),
        value_rows.reshape(flat),
        cotangent.reshape(flat),
        norm_gain,
    )
    outs = pl.pallas_call(
        place_outputs,
        out_shape=[jax.ShapeDtypeStruct(flat, low)] * 3,
        in_specs=[vmem] * 3,
        out_specs=[hbm] * 3,
        scratch_shapes=[pltpu.SemaphoreType.DMA((3,))],
        name="place_outputs",
    )(*outs)
    return tuple(out.reshape(query_rows.shape) for out in outs)


def fits(mesh, tok, both, size):
    seqs = mesh.shape["seq"]
    seg1 = tok * seqs // RATE4
    return (
        tok == ROWS * RATE3
        and size == 128
        and both == 2
        and seqs * ROWS == 128
        and tok % (RATE2 * seg1) == 0
        and (RATE3 * seg1) % tok == 0
        and tok // seg1 <= 64
    )


def solution(mesh):
    placed = (
        P("seq", "head", None),
        P("seq", "head", None),
        P("seq", "head", None),
        P("seq", "head", None),
        P("head", None),
        P("head"),
    )

    def run(query_rows, key_rows, value_rows, cotangent, norm_gain, offsets):
        tokens, heads, size = query_rows.shape
        small = fits(mesh, tokens // mesh.shape["seq"], heads // mesh.shape["head"], size)
        return jax.shard_map(
            fused_shards if small else shards,
            mesh=mesh,
            in_specs=placed,
            out_specs=(P("seq", "head", None), P("seq", "head", None), P("seq", "head", None)),
            check_vma=False,
        )(query_rows, key_rows, value_rows, cotangent, norm_gain, offsets)

    return run
```

```python
import functools

import jax
import jax.numpy as jnp
from jax import lax
from jax.experimental import pallas as pl
from jax.experimental.pallas import tpu as pltpu
from jax.sharding import PartitionSpec as P

RATE2 = 4
RATE3 = 16
RATE4 = 32


neg_fill = -1e30
epsilon = 1e-05
block_width = 512


def passed_along(value, axis, steps):
    count = lax.axis_size(axis)
    leading, last = (max(0, -steps), min(count, count - steps))
    return lax.ppermute(value, axis, [(source, source + steps) for source in range(leading, last)])


def pick_rows(source, wanted, stride):
    row_count = source.shape[0] // stride
    shaped = source.reshape((row_count, stride) + source.shape[1:])
    trailing = (1,) * (source.ndim - 2)
    target = wanted.reshape((1, 1, -1) + trailing)
    column = jnp.arange(stride, dtype=jnp.int32).reshape((1, stride, 1) + trailing)
    zeroed = jnp.where(column == target, shaped, jnp.zeros((), source.dtype))
    return jnp.sum(zeroed, axis=1, dtype=source.dtype)


def put_rows(compact, wanted, stride, filler):
    trailing = (1,) * (compact.ndim - 2)
    target = wanted.reshape((1, 1, -1) + trailing)
    column = jnp.arange(stride, dtype=jnp.int32).reshape((1, stride, 1) + trailing)
    spread = jnp.where(column == target, compact[:, None], jnp.asarray(filler, compact.dtype))
    return spread.reshape((compact.shape[0] * stride,) + compact.shape[1:])


def row_places(device, slot_count, direction, row_count, stride, wanted, tok_dev):
    owners = device + direction * jnp.arange(slot_count, dtype=jnp.int32)
    within_dev = wanted[None, :] + stride * jnp.arange(row_count, dtype=jnp.int32)[:, None]
    places = owners[:, None, None] * tok_dev + within_dev[None]
    return places.reshape(slot_count * row_count, wanted.shape[0])


def masked_scores(query_blk, key_blk, query_pos, key_pos, seg_len, score_scale):
    raw = (
        jnp.einsum("qhd,khd->hqk", query_blk, key_blk, preferred_element_type=jnp.float32)
        * score_scale
    )
    query_at = query_pos.T[:, :, None]
    key_at = key_pos.T[:, None, :]
    linked = (query_at // seg_len == key_at // seg_len) & (key_at <= query_at)
    return jnp.where(linked, raw, neg_fill)


def flatten_slots(member):
    return member.reshape((member.shape[0] * member.shape[1],) + member.shape[2:])


def extend(buffers, target, sign, puller):
    while buffers[0].shape[0] < target:
        covered = buffers[0].shape[0]
        arrived = puller(buffers, sign * covered)
        buffers = tuple(
            (jnp.concatenate([held, current], axis=0) for held, current in zip(buffers, arrived))
        )
    return buffers


def pull_keys(buffers, offset):
    return passed_along((buffers[0], buffers[1]), "seq", offset)


def pull_queries(buffers, offset):
    moved = passed_along((buffers[0], buffers[1]), "seq", offset)
    stats = passed_along((buffers[2], buffers[3]), "seq", offset)
    return (moved[0], moved[1], stats[0], stats[1])


def feature_sums(first, second):
    return lax.psum((first, second), "head")


def shards(query_rows, key_rows, value_rows, cotangent, norm_gain, offsets):
    tok_dev, heads_dev, head_size = query_rows.shape
    seq_count = lax.axis_size("seq")
    device = lax.axis_index("seq")
    group_rows = tok_dev * seq_count // RATE4
    score_scale = head_size ** (-0.5)
    features = heads_dev * head_size * lax.axis_size("head")
    levels = []
    for stride in (1, RATE2, RATE3, RATE4):
        seg_len = stride * group_rows
        levels.append((stride, seg_len, max(1, seg_len // tok_dev), offsets % stride))
    key_sets = []
    for stride, seg_len, span_devices, wanted in levels:
        own_rows = (
            pick_rows(key_rows, wanted, stride)[None],
            pick_rows(value_rows, wanted, stride)[None],
        )
        key_sets.append(extend(own_rows, span_devices, 1, pull_keys))
    prepared = []
    for (stride, seg_len, span_devices, wanted), key_set in zip(levels, key_sets):
        row_count = tok_dev // stride
        key_flat = flatten_slots(key_set[0])
        value_flat = flatten_slots(key_set[1])
        key_places = row_places(device, key_set[0].shape[0], -1, row_count, stride, wanted, tok_dev)
        query_sel = pick_rows(query_rows, wanted, stride)
        query_places = row_places(device, 1, -1, row_count, stride, wanted, tok_dev)
        prepared.append(
            (
                stride,
                seg_len,
                span_devices,
                wanted,
                row_count,
                key_flat,
                value_flat,
                key_places,
                query_sel,
                query_places,
            )
        )
    lse_total = jnp.full((tok_dev, heads_dev), neg_fill, jnp.float32)
    for (
        stride,
        seg_len,
        span_devices,
        wanted,
        row_count,
        key_flat,
        value_flat,
        key_places,
        query_sel,
        query_places,
    ) in prepared:
        level_lse = jnp.full((row_count, heads_dev), neg_fill, jnp.float32)
        for first_row in range(0, key_flat.shape[0], block_width):
            scores = masked_scores(
                query_sel,
                key_flat[first_row : first_row + block_width],
                query_places,
                key_places[first_row : first_row + block_width],
                seg_len,
                score_scale,
            )
            row_peak = jnp.max(scores, axis=2)
            block_lse = row_peak + jnp.log(jnp.sum(jnp.exp(scores - row_peak[:, :, None]), axis=2))
            level_lse = jnp.logaddexp(level_lse, block_lse.T)
        lse_total = jnp.logaddexp(lse_total, put_rows(level_lse, wanted, stride, neg_fill))
    attended = jnp.zeros((tok_dev, heads_dev, head_size), jnp.float32)
    for (
        stride,
        seg_len,
        span_devices,
        wanted,
        row_count,
        key_flat,
        value_flat,
        key_places,
        query_sel,
        query_places,
    ) in prepared:
        lse_sel = pick_rows(lse_total, wanted, stride)
        out_sel = jnp.zeros((row_count, heads_dev, head_size), jnp.float32)
        for first_row in range(0, key_flat.shape[0], block_width):
            scores = masked_scores(
                query_sel,
                key_flat[first_row : first_row + block_width],
                query_places,
                key_places[first_row : first_row + block_width],
                seg_len,
                score_scale,
            )
            weights = jnp.exp(scores - lse_sel.T[:, :, None]).astype(jnp.bfloat16)
            out_sel = out_sel + jnp.einsum(
                "hqk,khd->qhd",
                weights,
                value_flat[first_row : first_row + block_width],
                preferred_element_type=jnp.float32,
            )
        attended = attended + put_rows(out_sel, wanted, stride, 0.0)
    totals = feature_sums(jnp.sum(attended, axis=(1, 2)), jnp.sum(attended * attended, axis=(1, 2)))
    centre = totals[0] / features
    variance = totals[1] / features - centre * centre
    inverse = lax.rsqrt(variance + epsilon)
    normed = (attended - centre[:, None, None]) * inverse[:, None, None]
    grad_in = cotangent.astype(jnp.float32) * norm_gain[None]
    moments = feature_sums(jnp.sum(grad_in, axis=(1, 2)), jnp.sum(grad_in * normed, axis=(1, 2)))
    first_mean = moments[0] / features
    second_mean = moments[1] / features
    d_attended = (
        inverse[:, None, None]
        * (grad_in - first_mean[:, None, None] - normed * second_mean[:, None, None])
    ).astype(jnp.bfloat16)
    row_delta = jnp.sum(d_attended.astype(jnp.float32) * attended, axis=2)
    query_grad = jnp.zeros((tok_dev, heads_dev, head_size), jnp.float32)
    for (
        stride,
        seg_len,
        span_devices,
        wanted,
        row_count,
        key_flat,
        value_flat,
        key_places,
        query_sel,
        query_places,
    ) in prepared:
        lse_sel = pick_rows(lse_total, wanted, stride)
        dout_sel = pick_rows(d_attended, wanted, stride)
        delta_sel = pick_rows(row_delta, wanted, stride)
        grad_sel = jnp.zeros((row_count, heads_dev, head_size), jnp.float32)
        for first_row in range(0, key_flat.shape[0], block_width):
            key_block = key_flat[first_row : first_row + block_width]
            scores = masked_scores(
                query_sel,
                key_block,
                query_places,
                key_places[first_row : first_row + block_width],
                seg_len,
                score_scale,
            )
            weights = jnp.exp(scores - lse_sel.T[:, :, None])
            weight_grad = jnp.einsum(
                "qhd,khd->hqk",
                dout_sel,
                value_flat[first_row : first_row + block_width],
                preferred_element_type=jnp.float32,
            )
            score_grad = (weights * (weight_grad - delta_sel.T[:, :, None])).astype(jnp.bfloat16)
            grad_sel = grad_sel + jnp.einsum(
                "hqk,khd->qhd", score_grad, key_block, preferred_element_type=jnp.float32
            )
        query_grad = query_grad + put_rows(grad_sel * score_scale, wanted, stride, 0.0)
    query_sets = []
    for stride, seg_len, span_devices, wanted in levels:
        own_rows = (
            pick_rows(query_rows, wanted, stride)[None],
            pick_rows(d_attended, wanted, stride)[None],
            pick_rows(lse_total, wanted, stride)[None],
            pick_rows(row_delta, wanted, stride)[None],
        )
        query_sets.append(extend(own_rows, span_devices, -1, pull_queries))
    key_grad = jnp.zeros((tok_dev, heads_dev, head_size), jnp.float32)
    value_grad = jnp.zeros((tok_dev, heads_dev, head_size), jnp.float32)
    for (
        stride,
        seg_len,
        span_devices,
        wanted,
        row_count,
        key_flat,
        value_flat,
        key_places,
        query_sel,
        query_places,
    ), query_set in zip(prepared, query_sets):
        query_flat = flatten_slots(query_set[0])
        dout_flat = flatten_slots(query_set[1])
        lse_flat = flatten_slots(query_set[2])
        delta_flat = flatten_slots(query_set[3])
        query_far = row_places(device, query_set[0].shape[0], 1, row_count, stride, wanted, tok_dev)
        key_sel = pick_rows(key_rows, wanted, stride)
        value_sel = pick_rows(value_rows, wanted, stride)
        key_grad_sel = jnp.zeros((row_count, heads_dev, head_size), jnp.float32)
        value_grad_sel = jnp.zeros((row_count, heads_dev, head_size), jnp.float32)
        for first_row in range(0, query_flat.shape[0], block_width):
            query_block = query_flat[first_row : first_row + block_width]
            dout_block = dout_flat[first_row : first_row + block_width]
            lse_block = lse_flat[first_row : first_row + block_width]
            delta_block = delta_flat[first_row : first_row + block_width]
            scores = masked_scores(
                query_block,
                key_sel,
                query_far[first_row : first_row + block_width],
                query_places,
                seg_len,
                score_scale,
            )
            weights = jnp.exp(scores - lse_block.T[:, :, None])
            value_grad_sel = value_grad_sel + jnp.einsum(
                "hqk,qhd->khd",
                weights.astype(jnp.bfloat16),
                dout_block,
                preferred_element_type=jnp.float32,
            )
            weight_grad = jnp.einsum(
                "qhd,khd->hqk", dout_block, value_sel, preferred_element_type=jnp.float32
            )
            score_grad = (weights * (weight_grad - delta_block.T[:, :, None])).astype(jnp.bfloat16)
            key_grad_sel = key_grad_sel + jnp.einsum(
                "hqk,qhd->khd", score_grad, query_block, preferred_element_type=jnp.float32
            )
        key_grad = key_grad + put_rows(key_grad_sel * score_scale, wanted, stride, 0.0)
        value_grad = value_grad + put_rows(value_grad_sel, wanted, stride, 0.0)
    return (
        query_grad.astype(jnp.bfloat16),
        key_grad.astype(jnp.bfloat16),
        value_grad.astype(jnp.bfloat16),
    )

MESH = pl.DeviceIdType.MESH
LOG2E = 1.4426950408889634
HIDDEN = -1e30
ROWS = 16
VMEM_BYTES = 54752 * 1024


def dot_nn(a, b):
    return lax.dot_general(a, b, (((1,), (0,)), ((), ())), preferred_element_type=jnp.float32)


def dot_nt(a, b):
    return lax.dot_general(a, b, (((1,), (1,)), ((), ())), preferred_element_type=jnp.float32)


def dot_tn(a, b):
    return lax.dot_general(a, b, (((0,), (0,)), ((), ())), preferred_element_type=jnp.float32)


def iota(shape, axis):
    return lax.broadcasted_iota(jnp.int32, shape, axis)


def bias_of(count):
    return jnp.where(count > 0.5, jnp.log2(jnp.maximum(count, 1.0)), HIDDEN)


def fused(
    seqs,
    heads,
    seg1,
    features,
    off_hbm,
    q_hbm,
    k_hbm,
    v_hbm,
    c_hbm,
    gain_hbm,
    dq_ref,
    dk_ref,
    dv_ref,
    off_ref,
    gain_ref,
    xin,
    wide,
    mats,
    grads,
    weights,
    far_weights,
    bias,
    far_bias,
    late_score,
    picker,
    placer,
    kvsel,
    qsel,
    dosel,
    kvbuf,
    qbuf,
    dobuf,
    hsend,
    hbuf,
    rows_ref,
    outwide,
    in_sem,
    kv_send,
    kv_recv,
    q_send,
    q_recv,
    do_send,
    do_recv,
    h_send,
    h_recv,
):
    me = lax.axis_index("seq")
    mine = lax.axis_index("head")
    both, tok = mats.shape[1], mats.shape[2]
    size = mats.shape[3]
    far = seqs * ROWS
    half = ROWS // 2
    quad = RATE3 * seg1 // tok
    scale = size ** (-0.5)
    scale2 = scale * LOG2E

    loads = []
    for at, (source, target) in enumerate(
        (
            (off_hbm, off_ref),
            (k_hbm, xin.at[0]),
            (v_hbm, xin.at[1]),
            (q_hbm, xin.at[2]),
            (c_hbm, xin.at[3]),
            (gain_hbm, gain_ref),
        )
    ):
        copy = pltpu.make_async_copy(source, target, in_sem.at[at])
        copy.start()
        loads.append(copy)
    kvbuf[...] = jnp.zeros_like(kvbuf)
    qbuf[...] = jnp.zeros_like(qbuf)
    dobuf[...] = jnp.zeros_like(dobuf)
    hbuf[...] = jnp.zeros_like(hbuf)

    barrier = pltpu.get_barrier_semaphore()
    for step in range(1, seqs):
        pl.semaphore_signal(
            barrier, inc=1, device_id=(lax.rem(me + step, seqs), mine), device_id_type=MESH
        )
    for step in range(1, heads):
        pl.semaphore_signal(
            barrier, inc=1, device_id=(me, lax.rem(mine + step, heads)), device_id_type=MESH
        )
    rows_ref[...] = jnp.zeros_like(rows_ref)

    def remote(source, target, send, recv, step, owner):
        return pltpu.make_async_remote_copy(
            src_ref=source,
            dst_ref=target,
            send_sem=send.at[step - 1],
            recv_sem=recv.at[step - 1],
            device_id=owner,
            device_id_type=MESH,
        )

    def peer(step):
        owner = me
        for bit in range(step.bit_length()):
            if (step >> bit) & 1:
                owner = owner + 2**bit * (1 - 2 * ((me // 2**bit) % 2))
        return (owner, mine)

    kv_copies, q_copies, do_copies = {}, {}, {}
    for step in range(1, seqs):
        count = 2 * ROWS if step < quad else ROWS
        top = pl.ds(0, count)
        kv_copies[step] = remote(
            kvsel.at[:, top], kvbuf.at[:, me, top], kv_send, kv_recv, step, peer(step)
        )
        q_copies[step] = remote(qsel.at[top], qbuf.at[me, top], q_send, q_recv, step, peer(step))
        top = pl.ds(0, count + ROWS)
        do_copies[step] = remote(
            dosel.at[top], dobuf.at[me, top], do_send, do_recv, step, peer(step)
        )
    h_copies = [
        remote(hsend, hbuf.at[mine], h_send, h_recv, step, (me, lax.rem(mine + step, heads)))
        for step in range(1, heads)
    ]

    def each(side, copies, action):
        width = seqs // 2
        while width:
            @pl.when((me // width) % 2 == side)
            def _(width=width):
                for step in range(width, 2 * width):
                    getattr(copies[step], action)()

            width //= 2

    def per_head(mixed, h):
        groups = mixed.astype(jnp.float32).reshape(seqs, 2, both, half, size)
        return groups[:, :, h].reshape(far, size).astype(jnp.bfloat16)

    def select(at, g):
        rows = []
        for h in range(both):
            start = both * ((wanted[h] & (RATE4 - 1)) ^ (RATE3 * g)) + h
            rows.append(wide[at, pl.ds(start, half, stride=both * RATE4), :])
        return jnp.concatenate(rows, axis=0).astype(jnp.bfloat16)

    loads[0].wait()
    wanted = [off_ref[h] for h in range(both)]

    lane = iota((tok, 128), 1)
    token = iota((tok, 128), 0)
    causal = iota((tok, tok), 0) <= iota((tok, tok), 1)
    for h in range(both):
        off = wanted[h]
        marks = (token // seg1) == lane
        marks = marks | ((lane == 64) & ((token & (RATE2 - 1)) == (off & (RATE2 - 1))))
        marks = marks | ((lane == 65) & ((token & (RATE3 - 1)) == (off & (RATE3 - 1))))
        marks = marks | ((lane == 66) & ((token & (RATE4 - 1)) == (off & (RATE4 - 1))))
        marked = jnp.where(marks, 1.0, 0.0).astype(jnp.bfloat16)
        count = dot_nt(marked, marked)
        bias[h] = bias_of(jnp.where(causal, count, 0.0))

    for at in range(2):
        loads[1 + at].wait()
        wide[at] = xin[at].astype(jnp.float32)
        for g in range(2):
            kvsel[at, pl.ds(g * ROWS, ROWS), :] = select(at, g)
    pl.semaphore_wait(barrier, seqs + heads - 2)
    each(0, kv_copies, "start")

    loads[3].wait()
    wide[2] = xin[2].astype(jnp.float32)
    for g in range(2):
        qsel[pl.ds(g * ROWS, ROWS), :] = select(2, g)
    each(1, q_copies, "start")

    for at in range(3):
        for h in range(both):
            mats[at, h] = wide[at, pl.ds(h, tok, stride=both), :].astype(jnp.bfloat16)

    first_stats = []
    for h in range(both):
        score = dot_nt(mats[0, h], mats[2, h]) * scale2 + bias[h]
        peak = jnp.max(score, axis=0, keepdims=True)
        held = jnp.exp2(score - peak)
        weights[h] = held
        total = jnp.sum(held, axis=0, keepdims=True)
        out = dot_tn(mats[1, h], held.astype(jnp.bfloat16))
        first_stats.append((peak, total, out))

    loads[4].wait()
    loads[5].wait()
    wide[3] = xin[3].astype(jnp.float32)
    for h in range(both):
        grad = wide[3, pl.ds(h, tok, stride=both), :] * gain_ref[h : h + 1, :]
        grads[h] = grad.T

    for h in range(both):
        off = wanted[h]
        slot = iota((far, tok), 0) // ROWS
        query = iota((far, tok), 1)
        sel3 = (query & (RATE3 - 1)) == (off & (RATE3 - 1))
        sel4 = (query & (RATE4 - 1)) == (off & (RATE4 - 1))
        key4 = (iota((far, tok), 0) & half) == 0
        near = (slot // quad) == (me // quad)
        count = jnp.where(near & sel3, 1.0, 0.0) + jnp.where(key4 & sel4, 1.0, 0.0)
        far_bias[h] = bias_of(jnp.where(slot < me, count, 0.0))

    each(1, kv_copies, "wait_recv")

    sums = [jnp.zeros((1, tok), jnp.float32) for _ in range(4)]
    stats = []
    far_keys = [per_head(kvbuf[0], h) for h in range(both)]
    far_values = [per_head(kvbuf[1], h) for h in range(both)]
    for h in range(both):
        peak, total, out = first_stats[h]
        score = dot_nt(far_keys[h], mats[2, h]) * scale2 + far_bias[h]
        top = jnp.maximum(peak, jnp.max(score, axis=0, keepdims=True))
        shrink = jnp.exp2(peak - top)
        held = jnp.exp2(score - top)
        total = total * shrink + jnp.sum(held, axis=0, keepdims=True)
        ratio = 1.0 / total
        far_weights[h] = held * ratio
        out = (out * shrink + dot_tn(far_values[h], held.astype(jnp.bfloat16))) * ratio
        grad = grads[h]
        sums[0] = sums[0] + jnp.sum(out, axis=0, keepdims=True)
        sums[1] = sums[1] + jnp.sum(out * out, axis=0, keepdims=True)
        sums[2] = sums[2] + jnp.sum(grad, axis=0, keepdims=True)
        sums[3] = sums[3] + jnp.sum(grad * out, axis=0, keepdims=True)
        stats.append((out, shrink * ratio, top + jnp.log2(total)))
    for at in range(4):
        hsend[at : at + 1, :] = sums[at]
    for copy in h_copies:
        copy.start()

    for h in range(both):
        weights[h] = weights[h] * stats[h][1]
    row = iota((2 * ROWS, both * tok), 0)
    column = iota((2 * ROWS, both * tok), 1)
    head_of = (row // half) & 1
    start = jnp.where(head_of == 0, wanted[0], wanted[1]) & (RATE4 - 1)
    place = (start ^ (RATE3 * (row // ROWS))) + RATE4 * (row & (half - 1)) + tok * head_of
    picker[...] = jnp.where(column == place, 1.0, 0.0).astype(jnp.bfloat16)
    for h in range(both):
        token = iota((tok, far), 0)
        column = iota((tok, far), 1)
        start = (wanted[h] & (RATE4 - 1)) ^ (2 * (column & half))
        hit = (token == start + RATE4 * (column & (half - 1))) & (column // ROWS == me)
        placer[:, pl.ds(h * far, far)] = jnp.where(hit, 1.0, 0.0).astype(jnp.bfloat16)

    each(0, q_copies, "wait_recv")
    late_queries = [per_head(qbuf[...], h) for h in range(both)]
    for h in range(both):
        off = wanted[h]
        slot = iota((tok, far), 1) // ROWS
        key = iota((tok, far), 0)
        sel3 = (key & (RATE3 - 1)) == (off & (RATE3 - 1))
        sel4 = (key & (RATE4 - 1)) == (off & (RATE4 - 1))
        query4 = (iota((tok, far), 1) & half) == 0
        near = (slot // quad) == (me // quad)
        count = jnp.where(near & sel3, 1.0, 0.0) + jnp.where(query4 & sel4, 1.0, 0.0)
        late_bias = bias_of(jnp.where(slot > me, count, 0.0))
        late_score[h] = dot_nt(mats[0, h], late_queries[h]) * scale2 + late_bias

    for copy in h_copies:
        copy.wait_recv()
    full = hsend[...]
    for at in range(heads):
        full = full + hbuf[at]
    full = full * (1.0 / features)
    centre = full[0:1]
    inverse = lax.rsqrt(full[1:2] - centre * centre + epsilon)
    first = full[2:3]
    second = inverse * (full[3:4] - centre * first)

    douts = []
    for h in range(both):
        out, _, lse = stats[h]
        normed = (out - centre) * inverse
        dout = (inverse * (grads[h] - first - normed * second)).astype(jnp.bfloat16)
        delta = jnp.sum(dout.astype(jnp.float32) * out, axis=0, keepdims=True)
        for at, rest in enumerate((lse, delta)):
            for piece in range(3):
                part = rest.astype(jnp.bfloat16).astype(jnp.float32)
                rest = rest - part
                line = 8 * h + 2 * piece + at
                rows_ref[line : line + 1, :] = part
        douts.append((dout, delta))
    chosen = dot_nt(picker[...], jnp.concatenate([item[0] for item in douts], axis=1))
    moved = dot_nn(rows_ref[...].astype(jnp.bfloat16), placer[...])
    moved = jnp.concatenate([moved[0:8, 0:far], moved[8:16, far : 2 * far]], axis=0)
    dosel[0:ROWS, :] = chosen[0:ROWS].astype(jnp.bfloat16)
    dosel[ROWS : 2 * ROWS, :] = moved.astype(jnp.bfloat16)
    dosel[2 * ROWS : 3 * ROWS, :] = chosen[ROWS : 2 * ROWS].astype(jnp.bfloat16)
    each(1, do_copies, "start")

    key_parts = []
    for h in range(both):
        dout, delta = douts[h]
        weight = weights[h]
        weight_grad = dot_nn(mats[1, h], dout)
        score_grad = (weight * (weight_grad - delta)).astype(jnp.bfloat16)
        value_part = dot_nt(weight.astype(jnp.bfloat16), dout)
        key_part = dot_nn(score_grad, mats[2, h])
        far_grad = dot_nn(far_values[h], dout)
        far_score = (far_weights[h] * (far_grad - delta)).astype(jnp.bfloat16)
        query_part = dot_tn(mats[0, h], score_grad) + dot_tn(far_keys[h], far_score)
        outwide[0, pl.ds(h, tok, stride=both), :] = (query_part * scale).T
        key_parts.append((key_part, value_part))
    dq_ref[...] = outwide[0].astype(jnp.bfloat16)

    each(0, do_copies, "wait_recv")

    arrived = dobuf[...].astype(jnp.float32)
    mixed = jnp.stack([arrived[:, 0:ROWS], arrived[:, 2 * ROWS : 3 * ROWS]], axis=1)
    lines = arrived[0, ROWS : 2 * ROWS]
    for at in range(1, seqs):
        lines = lines + arrived[at, ROWS : 2 * ROWS]
    for h in range(both):
        key_part, value_part = key_parts[h]
        late_douts = per_head(mixed, h)
        at = 8 * h
        lse = lines[at : at + 1] + lines[at + 2 : at + 3] + lines[at + 4 : at + 5]
        delta = lines[at + 1 : at + 2] + lines[at + 3 : at + 4] + lines[at + 5 : at + 6]
        weight = jnp.exp2(late_score[h] - lse)
        weight_grad = dot_nt(mats[1, h], late_douts)
        score_grad = (weight * (weight_grad - delta)).astype(jnp.bfloat16)
        value_part = value_part + dot_nn(weight.astype(jnp.bfloat16), late_douts)
        key_part = key_part + dot_nn(score_grad, late_queries[h])
        outwide[1, pl.ds(h, tok, stride=both), :] = key_part * scale
        outwide[2, pl.ds(h, tok, stride=both), :] = value_part
    dk_ref[...] = outwide[1].astype(jnp.bfloat16)
    dv_ref[...] = outwide[2].astype(jnp.bfloat16)

    each(0, kv_copies, "wait_send")
    each(1, q_copies, "wait_send")
    each(1, do_copies, "wait_send")
    for copy in h_copies:
        copy.wait_send()


def place_outputs(dq_ref, dk_ref, dv_ref, dq_hbm, dk_hbm, dv_hbm, sem):
    copies = [
        pltpu.make_async_copy(source, target, sem.at[at])
        for at, (source, target) in enumerate(
            ((dq_ref, dq_hbm), (dk_ref, dk_hbm), (dv_ref, dv_hbm))
        )
    ]
    for copy in copies:
        copy.start()
    for copy in copies:
        copy.wait()


def fused_shards(query_rows, key_rows, value_rows, cotangent, norm_gain, offsets):
    tok, both, size = query_rows.shape
    seqs = lax.axis_size("seq")
    heads = lax.axis_size("head")
    seg1 = tok * seqs // RATE4
    far = seqs * ROWS
    flat = (both * tok, size)
    low, full = jnp.bfloat16, jnp.float32
    vmem = pl.BlockSpec(memory_space=pltpu.VMEM)
    hbm = pl.BlockSpec(memory_space=pltpu.HBM)
    outs = pl.pallas_call(
        functools.partial(fused, seqs, heads, seg1, both * size * heads),
        out_shape=[jax.ShapeDtypeStruct(flat, low)] * 3,
        in_specs=[hbm] * 6,
        out_specs=[vmem] * 3,
        scratch_shapes=[
            pltpu.SMEM((both,), jnp.int32),
            pltpu.VMEM((both, size), full),
            pltpu.VMEM((4,) + flat, low),
            pltpu.VMEM((4,) + flat, full),
            pltpu.VMEM((3, both, tok, size), low),
            pltpu.VMEM((both, size, tok), full),
            pltpu.VMEM((both, tok, tok), full),
            pltpu.VMEM((both, far, tok), full),
            pltpu.VMEM((both, tok, tok), full),
            pltpu.VMEM((both, far, tok), full),
            pltpu.VMEM((both, tok, far), full),
            pltpu.VMEM((2 * ROWS, both * tok), low),
            pltpu.VMEM((tok, both * far), low),
            pltpu.VMEM((2, 2 * ROWS, size), low),
            pltpu.VMEM((2 * ROWS, size), low),
            pltpu.VMEM((3 * ROWS, size), low),
            pltpu.VMEM((2, seqs, 2 * ROWS, size), low),
            pltpu.VMEM((seqs, 2 * ROWS, size), low),
            pltpu.VMEM((seqs, 3 * ROWS, size), low),
            pltpu.VMEM((4, tok), full),
            pltpu.VMEM((heads, 4, tok), full),
            pltpu.VMEM((8 * both, tok), full),
            pltpu.VMEM((3,) + flat, full),
            pltpu.SemaphoreType.DMA((6,)),
        ]
        + [pltpu.SemaphoreType.DMA((seqs - 1,))] * 6
        + [pltpu.SemaphoreType.DMA((heads - 1,))] * 2,
        compiler_params=pltpu.CompilerParams(
            collective_id=0, has_side_effects=True, vmem_limit_bytes=VMEM_BYTES
        ),
        name="fused_backward",
    )(
        offsets,
        query_rows.reshape(flat),
        key_rows.reshape(flat),
        value_rows.reshape(flat),
        cotangent.reshape(flat),
        norm_gain,
    )
    outs = pl.pallas_call(
        place_outputs,
        out_shape=[jax.ShapeDtypeStruct(flat, low)] * 3,
        in_specs=[vmem] * 3,
        out_specs=[hbm] * 3,
        scratch_shapes=[pltpu.SemaphoreType.DMA((3,))],
        name="place_outputs",
    )(*outs)
    return tuple(out.reshape(query_rows.shape) for out in outs)


def fits(mesh, tok, both, size):
    seqs = mesh.shape["seq"]
    seg1 = tok * seqs // RATE4
    return (
        tok == ROWS * RATE3
        and size == 128
        and both == 2
        and seqs * ROWS == 128
        and (RATE3 * seg1 // tok) & (RATE3 * seg1 // tok - 1) == 0
        and tok % (RATE2 * seg1) == 0
        and (RATE3 * seg1) % tok == 0
        and tok // seg1 <= 64
    )


def solution(mesh):
    placed = (
        P("seq", "head", None),
        P("seq", "head", None),
        P("seq", "head", None),
        P("seq", "head", None),
        P("head", None),
        P("head"),
    )

    def run(query_rows, key_rows, value_rows, cotangent, norm_gain, offsets):
        tokens, heads, size = query_rows.shape
        small = fits(mesh, tokens // mesh.shape["seq"], heads // mesh.shape["head"], size)
        return jax.shard_map(
            fused_shards if small else shards,
            mesh=mesh,
            in_specs=placed,
            out_specs=(P("seq", "head", None), P("seq", "head", None), P("seq", "head", None)),
            check_vma=False,
        )(query_rows, key_rows, value_rows, cotangent, norm_gain, offsets)

    return run
```

```python
import functools

import jax
import jax.numpy as jnp
from jax import lax
from jax.experimental import pallas as pl
from jax.experimental.pallas import tpu as pltpu
from jax.sharding import PartitionSpec as P

RATE2 = 4
RATE3 = 16
RATE4 = 32


neg_fill = -1e30
epsilon = 1e-05
block_width = 512


def passed_along(value, axis, steps):
    count = lax.axis_size(axis)
    leading, last = (max(0, -steps), min(count, count - steps))
    return lax.ppermute(value, axis, [(source, source + steps) for source in range(leading, last)])


def pick_rows(source, wanted, stride):
    row_count = source.shape[0] // stride
    shaped = source.reshape((row_count, stride) + source.shape[1:])
    trailing = (1,) * (source.ndim - 2)
    target = wanted.reshape((1, 1, -1) + trailing)
    column = jnp.arange(stride, dtype=jnp.int32).reshape((1, stride, 1) + trailing)
    zeroed = jnp.where(column == target, shaped, jnp.zeros((), source.dtype))
    return jnp.sum(zeroed, axis=1, dtype=source.dtype)


def put_rows(compact, wanted, stride, filler):
    trailing = (1,) * (compact.ndim - 2)
    target = wanted.reshape((1, 1, -1) + trailing)
    column = jnp.arange(stride, dtype=jnp.int32).reshape((1, stride, 1) + trailing)
    spread = jnp.where(column == target, compact[:, None], jnp.asarray(filler, compact.dtype))
    return spread.reshape((compact.shape[0] * stride,) + compact.shape[1:])


def row_places(device, slot_count, direction, row_count, stride, wanted, tok_dev):
    owners = device + direction * jnp.arange(slot_count, dtype=jnp.int32)
    within_dev = wanted[None, :] + stride * jnp.arange(row_count, dtype=jnp.int32)[:, None]
    places = owners[:, None, None] * tok_dev + within_dev[None]
    return places.reshape(slot_count * row_count, wanted.shape[0])


def masked_scores(query_blk, key_blk, query_pos, key_pos, seg_len, score_scale):
    raw = (
        jnp.einsum("qhd,khd->hqk", query_blk, key_blk, preferred_element_type=jnp.float32)
        * score_scale
    )
    query_at = query_pos.T[:, :, None]
    key_at = key_pos.T[:, None, :]
    linked = (query_at // seg_len == key_at // seg_len) & (key_at <= query_at)
    return jnp.where(linked, raw, neg_fill)


def flatten_slots(member):
    return member.reshape((member.shape[0] * member.shape[1],) + member.shape[2:])


def extend(buffers, target, sign, puller):
    while buffers[0].shape[0] < target:
        covered = buffers[0].shape[0]
        arrived = puller(buffers, sign * covered)
        buffers = tuple(
            (jnp.concatenate([held, current], axis=0) for held, current in zip(buffers, arrived))
        )
    return buffers


def pull_keys(buffers, offset):
    return passed_along((buffers[0], buffers[1]), "seq", offset)


def pull_queries(buffers, offset):
    moved = passed_along((buffers[0], buffers[1]), "seq", offset)
    stats = passed_along((buffers[2], buffers[3]), "seq", offset)
    return (moved[0], moved[1], stats[0], stats[1])


def feature_sums(first, second):
    return lax.psum((first, second), "head")


def shards(query_rows, key_rows, value_rows, cotangent, norm_gain, offsets):
    tok_dev, heads_dev, head_size = query_rows.shape
    seq_count = lax.axis_size("seq")
    device = lax.axis_index("seq")
    group_rows = tok_dev * seq_count // RATE4
    score_scale = head_size ** (-0.5)
    features = heads_dev * head_size * lax.axis_size("head")
    levels = []
    for stride in (1, RATE2, RATE3, RATE4):
        seg_len = stride * group_rows
        levels.append((stride, seg_len, max(1, seg_len // tok_dev), offsets % stride))
    key_sets = []
    for stride, seg_len, span_devices, wanted in levels:
        own_rows = (
            pick_rows(key_rows, wanted, stride)[None],
            pick_rows(value_rows, wanted, stride)[None],
        )
        key_sets.append(extend(own_rows, span_devices, 1, pull_keys))
    prepared = []
    for (stride, seg_len, span_devices, wanted), key_set in zip(levels, key_sets):
        row_count = tok_dev // stride
        key_flat = flatten_slots(key_set[0])
        value_flat = flatten_slots(key_set[1])
        key_places = row_places(device, key_set[0].shape[0], -1, row_count, stride, wanted, tok_dev)
        query_sel = pick_rows(query_rows, wanted, stride)
        query_places = row_places(device, 1, -1, row_count, stride, wanted, tok_dev)
        prepared.append(
            (
                stride,
                seg_len,
                span_devices,
                wanted,
                row_count,
                key_flat,
                value_flat,
                key_places,
                query_sel,
                query_places,
            )
        )
    lse_total = jnp.full((tok_dev, heads_dev), neg_fill, jnp.float32)
    for (
        stride,
        seg_len,
        span_devices,
        wanted,
        row_count,
        key_flat,
        value_flat,
        key_places,
        query_sel,
        query_places,
    ) in prepared:
        level_lse = jnp.full((row_count, heads_dev), neg_fill, jnp.float32)
        for first_row in range(0, key_flat.shape[0], block_width):
            scores = masked_scores(
                query_sel,
                key_flat[first_row : first_row + block_width],
                query_places,
                key_places[first_row : first_row + block_width],
                seg_len,
                score_scale,
            )
            row_peak = jnp.max(scores, axis=2)
            block_lse = row_peak + jnp.log(jnp.sum(jnp.exp(scores - row_peak[:, :, None]), axis=2))
            level_lse = jnp.logaddexp(level_lse, block_lse.T)
        lse_total = jnp.logaddexp(lse_total, put_rows(level_lse, wanted, stride, neg_fill))
    attended = jnp.zeros((tok_dev, heads_dev, head_size), jnp.float32)
    for (
        stride,
        seg_len,
        span_devices,
        wanted,
        row_count,
        key_flat,
        value_flat,
        key_places,
        query_sel,
        query_places,
    ) in prepared:
        lse_sel = pick_rows(lse_total, wanted, stride)
        out_sel = jnp.zeros((row_count, heads_dev, head_size), jnp.float32)
        for first_row in range(0, key_flat.shape[0], block_width):
            scores = masked_scores(
                query_sel,
                key_flat[first_row : first_row + block_width],
                query_places,
                key_places[first_row : first_row + block_width],
                seg_len,
                score_scale,
            )
            weights = jnp.exp(scores - lse_sel.T[:, :, None]).astype(jnp.bfloat16)
            out_sel = out_sel + jnp.einsum(
                "hqk,khd->qhd",
                weights,
                value_flat[first_row : first_row + block_width],
                preferred_element_type=jnp.float32,
            )
        attended = attended + put_rows(out_sel, wanted, stride, 0.0)
    totals = feature_sums(jnp.sum(attended, axis=(1, 2)), jnp.sum(attended * attended, axis=(1, 2)))
    centre = totals[0] / features
    variance = totals[1] / features - centre * centre
    inverse = lax.rsqrt(variance + epsilon)
    normed = (attended - centre[:, None, None]) * inverse[:, None, None]
    grad_in = cotangent.astype(jnp.float32) * norm_gain[None]
    moments = feature_sums(jnp.sum(grad_in, axis=(1, 2)), jnp.sum(grad_in * normed, axis=(1, 2)))
    first_mean = moments[0] / features
    second_mean = moments[1] / features
    d_attended = (
        inverse[:, None, None]
        * (grad_in - first_mean[:, None, None] - normed * second_mean[:, None, None])
    ).astype(jnp.bfloat16)
    row_delta = jnp.sum(d_attended.astype(jnp.float32) * attended, axis=2)
    query_grad = jnp.zeros((tok_dev, heads_dev, head_size), jnp.float32)
    for (
        stride,
        seg_len,
        span_devices,
        wanted,
        row_count,
        key_flat,
        value_flat,
        key_places,
        query_sel,
        query_places,
    ) in prepared:
        lse_sel = pick_rows(lse_total, wanted, stride)
        dout_sel = pick_rows(d_attended, wanted, stride)
        delta_sel = pick_rows(row_delta, wanted, stride)
        grad_sel = jnp.zeros((row_count, heads_dev, head_size), jnp.float32)
        for first_row in range(0, key_flat.shape[0], block_width):
            key_block = key_flat[first_row : first_row + block_width]
            scores = masked_scores(
                query_sel,
                key_block,
                query_places,
                key_places[first_row : first_row + block_width],
                seg_len,
                score_scale,
            )
            weights = jnp.exp(scores - lse_sel.T[:, :, None])
            weight_grad = jnp.einsum(
                "qhd,khd->hqk",
                dout_sel,
                value_flat[first_row : first_row + block_width],
                preferred_element_type=jnp.float32,
            )
            score_grad = (weights * (weight_grad - delta_sel.T[:, :, None])).astype(jnp.bfloat16)
            grad_sel = grad_sel + jnp.einsum(
                "hqk,khd->qhd", score_grad, key_block, preferred_element_type=jnp.float32
            )
        query_grad = query_grad + put_rows(grad_sel * score_scale, wanted, stride, 0.0)
    query_sets = []
    for stride, seg_len, span_devices, wanted in levels:
        own_rows = (
            pick_rows(query_rows, wanted, stride)[None],
            pick_rows(d_attended, wanted, stride)[None],
            pick_rows(lse_total, wanted, stride)[None],
            pick_rows(row_delta, wanted, stride)[None],
        )
        query_sets.append(extend(own_rows, span_devices, -1, pull_queries))
    key_grad = jnp.zeros((tok_dev, heads_dev, head_size), jnp.float32)
    value_grad = jnp.zeros((tok_dev, heads_dev, head_size), jnp.float32)
    for (
        stride,
        seg_len,
        span_devices,
        wanted,
        row_count,
        key_flat,
        value_flat,
        key_places,
        query_sel,
        query_places,
    ), query_set in zip(prepared, query_sets):
        query_flat = flatten_slots(query_set[0])
        dout_flat = flatten_slots(query_set[1])
        lse_flat = flatten_slots(query_set[2])
        delta_flat = flatten_slots(query_set[3])
        query_far = row_places(device, query_set[0].shape[0], 1, row_count, stride, wanted, tok_dev)
        key_sel = pick_rows(key_rows, wanted, stride)
        value_sel = pick_rows(value_rows, wanted, stride)
        key_grad_sel = jnp.zeros((row_count, heads_dev, head_size), jnp.float32)
        value_grad_sel = jnp.zeros((row_count, heads_dev, head_size), jnp.float32)
        for first_row in range(0, query_flat.shape[0], block_width):
            query_block = query_flat[first_row : first_row + block_width]
            dout_block = dout_flat[first_row : first_row + block_width]
            lse_block = lse_flat[first_row : first_row + block_width]
            delta_block = delta_flat[first_row : first_row + block_width]
            scores = masked_scores(
                query_block,
                key_sel,
                query_far[first_row : first_row + block_width],
                query_places,
                seg_len,
                score_scale,
            )
            weights = jnp.exp(scores - lse_block.T[:, :, None])
            value_grad_sel = value_grad_sel + jnp.einsum(
                "hqk,qhd->khd",
                weights.astype(jnp.bfloat16),
                dout_block,
                preferred_element_type=jnp.float32,
            )
            weight_grad = jnp.einsum(
                "qhd,khd->hqk", dout_block, value_sel, preferred_element_type=jnp.float32
            )
            score_grad = (weights * (weight_grad - delta_block.T[:, :, None])).astype(jnp.bfloat16)
            key_grad_sel = key_grad_sel + jnp.einsum(
                "hqk,qhd->khd", score_grad, query_block, preferred_element_type=jnp.float32
            )
        key_grad = key_grad + put_rows(key_grad_sel * score_scale, wanted, stride, 0.0)
        value_grad = value_grad + put_rows(value_grad_sel, wanted, stride, 0.0)
    return (
        query_grad.astype(jnp.bfloat16),
        key_grad.astype(jnp.bfloat16),
        value_grad.astype(jnp.bfloat16),
    )

MESH = pl.DeviceIdType.MESH
LOG2E = 1.4426950408889634
HIDDEN = -1e30
ROWS = 16
VMEM_BYTES = 54752 * 1024


def dot_nn(a, b):
    return lax.dot_general(a, b, (((1,), (0,)), ((), ())), preferred_element_type=jnp.float32)


def dot_nt(a, b):
    return lax.dot_general(a, b, (((1,), (1,)), ((), ())), preferred_element_type=jnp.float32)


def dot_tn(a, b):
    return lax.dot_general(a, b, (((0,), (0,)), ((), ())), preferred_element_type=jnp.float32)


def iota(shape, axis):
    return lax.broadcasted_iota(jnp.int32, shape, axis)


def bias_of(count):
    return jnp.where(count > 0.5, jnp.log2(jnp.maximum(count, 1.0)), HIDDEN)


def fused(
    seqs,
    heads,
    seg1,
    features,
    off_hbm,
    q_hbm,
    k_hbm,
    v_hbm,
    c_hbm,
    gain_hbm,
    dq_ref,
    dk_ref,
    dv_ref,
    off_ref,
    gain_ref,
    xin,
    wide,
    mats,
    grads,
    weights,
    far_weights,
    bias,
    far_bias,
    late_score,
    picker,
    placer,
    kvsel,
    qsel,
    dosel,
    kvbuf,
    qbuf,
    dobuf,
    hsend,
    hbuf,
    rows_ref,
    outwide,
    in_sem,
    kv_send,
    kv_recv,
    q_send,
    q_recv,
    do_send,
    do_recv,
    h_send,
    h_recv,
):
    me = lax.axis_index("seq")
    mine = lax.axis_index("head")
    both, tok = mats.shape[1], mats.shape[2]
    size = mats.shape[3]
    far = seqs * ROWS
    half = ROWS // 2
    quad = RATE3 * seg1 // tok
    scale = size ** (-0.5)
    scale2 = scale * LOG2E

    loads = []
    for at, (source, target) in enumerate(
        (
            (off_hbm, off_ref),
            (k_hbm, xin.at[0]),
            (v_hbm, xin.at[1]),
            (q_hbm, xin.at[2]),
            (c_hbm, xin.at[3]),
            (gain_hbm, gain_ref),
        )
    ):
        copy = pltpu.make_async_copy(source, target, in_sem.at[at])
        copy.start()
        loads.append(copy)
    kvbuf[...] = jnp.zeros_like(kvbuf)
    qbuf[...] = jnp.zeros_like(qbuf)
    dobuf[...] = jnp.zeros_like(dobuf)
    hbuf[...] = jnp.zeros_like(hbuf)

    barrier = pltpu.get_barrier_semaphore()
    for step in range(1, seqs):
        pl.semaphore_signal(
            barrier, inc=1, device_id=(lax.rem(me + step, seqs), mine), device_id_type=MESH
        )
    for step in range(1, heads):
        pl.semaphore_signal(
            barrier, inc=1, device_id=(me, lax.rem(mine + step, heads)), device_id_type=MESH
        )
    rows_ref[...] = jnp.zeros_like(rows_ref)

    def remote(source, target, send, recv, step, owner):
        return pltpu.make_async_remote_copy(
            src_ref=source,
            dst_ref=target,
            send_sem=send.at[step - 1],
            recv_sem=recv.at[step - 1],
            device_id=owner,
            device_id_type=MESH,
        )

    def peer(step):
        owner = me
        for bit in range(step.bit_length()):
            if (step >> bit) & 1:
                owner = owner + 2**bit * (1 - 2 * ((me // 2**bit) % 2))
        return (owner, mine)

    kv_copies, q_copies, do_copies = {}, {}, {}
    for step in range(1, seqs):
        count = 2 * ROWS if step < quad else ROWS
        top = pl.ds(0, count)
        kv_copies[step] = remote(
            kvsel.at[:, top], kvbuf.at[:, me, top], kv_send, kv_recv, step, peer(step)
        )
        q_copies[step] = remote(qsel.at[top], qbuf.at[me, top], q_send, q_recv, step, peer(step))
        top = pl.ds(0, count + ROWS)
        do_copies[step] = remote(
            dosel.at[top], dobuf.at[me, top], do_send, do_recv, step, peer(step)
        )
    h_copies = [
        remote(hsend, hbuf.at[mine], h_send, h_recv, step, (me, lax.rem(mine + step, heads)))
        for step in range(1, heads)
    ]

    def each(side, copies, action):
        width = seqs // 2
        while width:
            @pl.when((me // width) % 2 == side)
            def _(width=width):
                for step in range(width, 2 * width):
                    getattr(copies[step], action)()

            width //= 2

    def per_head(mixed, h):
        groups = mixed.astype(jnp.float32).reshape(seqs, 2, both, half, size)
        return groups[:, :, h].reshape(far, size).astype(jnp.bfloat16)

    def select(at, g):
        rows = []
        for h in range(both):
            start = both * ((wanted[h] & (RATE4 - 1)) ^ (RATE3 * g)) + h
            rows.append(wide[at, pl.ds(start, half, stride=both * RATE4), :])
        return jnp.concatenate(rows, axis=0).astype(jnp.bfloat16)

    loads[0].wait()
    wanted = [off_ref[h] for h in range(both)]

    lane = iota((tok, 128), 1)
    token = iota((tok, 128), 0)
    causal = iota((tok, tok), 0) <= iota((tok, tok), 1)
    for h in range(both):
        off = wanted[h]
        marks = (token // seg1) == lane
        marks = marks | ((lane == 64) & ((token & (RATE2 - 1)) == (off & (RATE2 - 1))))
        marks = marks | ((lane == 65) & ((token & (RATE3 - 1)) == (off & (RATE3 - 1))))
        marks = marks | ((lane == 66) & ((token & (RATE4 - 1)) == (off & (RATE4 - 1))))
        marked = jnp.where(marks, 1.0, 0.0).astype(jnp.bfloat16)
        count = dot_nt(marked, marked)
        bias[h] = bias_of(jnp.where(causal, count, 0.0))

    for h in range(both):
        off = wanted[h]
        slot = iota((far, tok), 0) // ROWS
        query = iota((far, tok), 1)
        sel3 = (query & (RATE3 - 1)) == (off & (RATE3 - 1))
        sel4 = (query & (RATE4 - 1)) == (off & (RATE4 - 1))
        key4 = (iota((far, tok), 0) & half) == 0
        near = (slot // quad) == (me // quad)
        count = jnp.where(near & sel3, 1.0, 0.0) + jnp.where(key4 & sel4, 1.0, 0.0)
        far_bias[h] = bias_of(jnp.where(slot < me, count, 0.0))

    for at in range(2):
        loads[1 + at].wait()
        wide[at] = xin[at].astype(jnp.float32)
        for g in range(2):
            kvsel[at, pl.ds(g * ROWS, ROWS), :] = select(at, g)
    pl.semaphore_wait(barrier, seqs + heads - 2)
    each(0, kv_copies, "start")

    loads[3].wait()
    wide[2] = xin[2].astype(jnp.float32)
    for g in range(2):
        qsel[pl.ds(g * ROWS, ROWS), :] = select(2, g)
    each(1, q_copies, "start")

    for at in range(3):
        for h in range(both):
            mats[at, h] = wide[at, pl.ds(h, tok, stride=both), :].astype(jnp.bfloat16)

    first_stats = []
    for h in range(both):
        score = dot_nt(mats[0, h], mats[2, h]) * scale2 + bias[h]
        peak = jnp.max(score, axis=0, keepdims=True)
        held = jnp.exp2(score - peak)
        weights[h] = held
        total = jnp.sum(held, axis=0, keepdims=True)
        out = dot_tn(mats[1, h], held.astype(jnp.bfloat16))
        first_stats.append((peak, total, out))

    loads[4].wait()
    loads[5].wait()
    wide[3] = xin[3].astype(jnp.float32)
    for h in range(both):
        grad = wide[3, pl.ds(h, tok, stride=both), :] * gain_ref[h : h + 1, :]
        grads[h] = grad.T

    each(1, kv_copies, "wait_recv")

    sums = [jnp.zeros((1, tok), jnp.float32) for _ in range(4)]
    stats = []
    far_keys = [per_head(kvbuf[0], h) for h in range(both)]
    far_values = [per_head(kvbuf[1], h) for h in range(both)]
    for h in range(both):
        peak, total, out = first_stats[h]
        score = dot_nt(far_keys[h], mats[2, h]) * scale2 + far_bias[h]
        top = jnp.maximum(peak, jnp.max(score, axis=0, keepdims=True))
        shrink = jnp.exp2(peak - top)
        held = jnp.exp2(score - top)
        total = total * shrink + jnp.sum(held, axis=0, keepdims=True)
        ratio = 1.0 / total
        far_weights[h] = held * ratio
        out = (out * shrink + dot_tn(far_values[h], held.astype(jnp.bfloat16))) * ratio
        grad = grads[h]
        sums[0] = sums[0] + jnp.sum(out, axis=0, keepdims=True)
        sums[1] = sums[1] + jnp.sum(out * out, axis=0, keepdims=True)
        sums[2] = sums[2] + jnp.sum(grad, axis=0, keepdims=True)
        sums[3] = sums[3] + jnp.sum(grad * out, axis=0, keepdims=True)
        stats.append((out, shrink * ratio, top + jnp.log2(total)))
    for at in range(4):
        hsend[at : at + 1, :] = sums[at]
    for copy in h_copies:
        copy.start()

    for h in range(both):
        weights[h] = weights[h] * stats[h][1]
    row = iota((2 * ROWS, both * tok), 0)
    column = iota((2 * ROWS, both * tok), 1)
    head_of = (row // half) & 1
    start = jnp.where(head_of == 0, wanted[0], wanted[1]) & (RATE4 - 1)
    place = (start ^ (RATE3 * (row // ROWS))) + RATE4 * (row & (half - 1)) + tok * head_of
    picker[...] = jnp.where(column == place, 1.0, 0.0).astype(jnp.bfloat16)
    for h in range(both):
        token = iota((tok, far), 0)
        column = iota((tok, far), 1)
        start = (wanted[h] & (RATE4 - 1)) ^ (2 * (column & half))
        hit = (token == start + RATE4 * (column & (half - 1))) & (column // ROWS == me)
        placer[:, pl.ds(h * far, far)] = jnp.where(hit, 1.0, 0.0).astype(jnp.bfloat16)

    each(0, q_copies, "wait_recv")
    late_queries = [per_head(qbuf[...], h) for h in range(both)]
    for h in range(both):
        off = wanted[h]
        slot = iota((tok, far), 1) // ROWS
        key = iota((tok, far), 0)
        sel3 = (key & (RATE3 - 1)) == (off & (RATE3 - 1))
        sel4 = (key & (RATE4 - 1)) == (off & (RATE4 - 1))
        query4 = (iota((tok, far), 1) & half) == 0
        near = (slot // quad) == (me // quad)
        count = jnp.where(near & sel3, 1.0, 0.0) + jnp.where(query4 & sel4, 1.0, 0.0)
        late_bias = bias_of(jnp.where(slot > me, count, 0.0))
        late_score[h] = dot_nt(mats[0, h], late_queries[h]) * scale2 + late_bias

    for copy in h_copies:
        copy.wait_recv()
    full = hsend[...]
    for at in range(heads):
        full = full + hbuf[at]
    full = full * (1.0 / features)
    centre = full[0:1]
    inverse = lax.rsqrt(full[1:2] - centre * centre + epsilon)
    first = full[2:3]
    second = inverse * (full[3:4] - centre * first)

    douts = []
    for h in range(both):
        out, _, lse = stats[h]
        normed = (out - centre) * inverse
        dout = (inverse * (grads[h] - first - normed * second)).astype(jnp.bfloat16)
        delta = jnp.sum(dout.astype(jnp.float32) * out, axis=0, keepdims=True)
        for at, rest in enumerate((lse, delta)):
            for piece in range(3):
                part = rest.astype(jnp.bfloat16).astype(jnp.float32)
                rest = rest - part
                line = 8 * h + 2 * piece + at
                rows_ref[line : line + 1, :] = part
        douts.append((dout, delta))
    chosen = dot_nt(picker[...], jnp.concatenate([item[0] for item in douts], axis=1))
    moved = dot_nn(rows_ref[...].astype(jnp.bfloat16), placer[...])
    moved = jnp.concatenate([moved[0:8, 0:far], moved[8:16, far : 2 * far]], axis=0)
    dosel[0:ROWS, :] = chosen[0:ROWS].astype(jnp.bfloat16)
    dosel[ROWS : 2 * ROWS, :] = moved.astype(jnp.bfloat16)
    dosel[2 * ROWS : 3 * ROWS, :] = chosen[ROWS : 2 * ROWS].astype(jnp.bfloat16)
    each(1, do_copies, "start")

    key_parts = []
    for h in range(both):
        dout, delta = douts[h]
        weight = weights[h]
        weight_grad = dot_nn(mats[1, h], dout)
        score_grad = (weight * (weight_grad - delta)).astype(jnp.bfloat16)
        value_part = dot_nt(weight.astype(jnp.bfloat16), dout)
        key_part = dot_nn(score_grad, mats[2, h])
        far_grad = dot_nn(far_values[h], dout)
        far_score = (far_weights[h] * (far_grad - delta)).astype(jnp.bfloat16)
        query_part = dot_tn(mats[0, h], score_grad) + dot_tn(far_keys[h], far_score)
        outwide[0, pl.ds(h, tok, stride=both), :] = (query_part * scale).T
        key_parts.append((key_part, value_part))
    dq_ref[...] = outwide[0].astype(jnp.bfloat16)

    each(0, do_copies, "wait_recv")

    arrived = dobuf[...].astype(jnp.float32)
    mixed = jnp.stack([arrived[:, 0:ROWS], arrived[:, 2 * ROWS : 3 * ROWS]], axis=1)
    lines = arrived[0, ROWS : 2 * ROWS]
    for at in range(1, seqs):
        lines = lines + arrived[at, ROWS : 2 * ROWS]
    for h in range(both):
        key_part, value_part = key_parts[h]
        late_douts = per_head(mixed, h)
        at = 8 * h
        lse = lines[at : at + 1] + lines[at + 2 : at + 3] + lines[at + 4 : at + 5]
        delta = lines[at + 1 : at + 2] + lines[at + 3 : at + 4] + lines[at + 5 : at + 6]
        weight = jnp.exp2(late_score[h] - lse)
        weight_grad = dot_nt(mats[1, h], late_douts)
        score_grad = (weight * (weight_grad - delta)).astype(jnp.bfloat16)
        value_part = value_part + dot_nn(weight.astype(jnp.bfloat16), late_douts)
        key_part = key_part + dot_nn(score_grad, late_queries[h])
        outwide[1, pl.ds(h, tok, stride=both), :] = key_part * scale
        outwide[2, pl.ds(h, tok, stride=both), :] = value_part
    dk_ref[...] = outwide[1].astype(jnp.bfloat16)
    dv_ref[...] = outwide[2].astype(jnp.bfloat16)

    each(0, kv_copies, "wait_send")
    each(1, q_copies, "wait_send")
    each(1, do_copies, "wait_send")
    for copy in h_copies:
        copy.wait_send()


def place_outputs(dq_ref, dk_ref, dv_ref, dq_hbm, dk_hbm, dv_hbm, sem):
    copies = [
        pltpu.make_async_copy(source, target, sem.at[at])
        for at, (source, target) in enumerate(
            ((dq_ref, dq_hbm), (dk_ref, dk_hbm), (dv_ref, dv_hbm))
        )
    ]
    for copy in copies:
        copy.start()
    for copy in copies:
        copy.wait()


def fused_shards(query_rows, key_rows, value_rows, cotangent, norm_gain, offsets):
    tok, both, size = query_rows.shape
    seqs = lax.axis_size("seq")
    heads = lax.axis_size("head")
    seg1 = tok * seqs // RATE4
    far = seqs * ROWS
    flat = (both * tok, size)
    low, full = jnp.bfloat16, jnp.float32
    vmem = pl.BlockSpec(memory_space=pltpu.VMEM)
    hbm = pl.BlockSpec(memory_space=pltpu.HBM)
    outs = pl.pallas_call(
        functools.partial(fused, seqs, heads, seg1, both * size * heads),
        out_shape=[jax.ShapeDtypeStruct(flat, low)] * 3,
        in_specs=[hbm] * 6,
        out_specs=[vmem] * 3,
        scratch_shapes=[
            pltpu.SMEM((both,), jnp.int32),
            pltpu.VMEM((both, size), full),
            pltpu.VMEM((4,) + flat, low),
            pltpu.VMEM((4,) + flat, full),
            pltpu.VMEM((3, both, tok, size), low),
            pltpu.VMEM((both, size, tok), full),
            pltpu.VMEM((both, tok, tok), full),
            pltpu.VMEM((both, far, tok), full),
            pltpu.VMEM((both, tok, tok), full),
            pltpu.VMEM((both, far, tok), full),
            pltpu.VMEM((both, tok, far), full),
            pltpu.VMEM((2 * ROWS, both * tok), low),
            pltpu.VMEM((tok, both * far), low),
            pltpu.VMEM((2, 2 * ROWS, size), low),
            pltpu.VMEM((2 * ROWS, size), low),
            pltpu.VMEM((3 * ROWS, size), low),
            pltpu.VMEM((2, seqs, 2 * ROWS, size), low),
            pltpu.VMEM((seqs, 2 * ROWS, size), low),
            pltpu.VMEM((seqs, 3 * ROWS, size), low),
            pltpu.VMEM((4, tok), full),
            pltpu.VMEM((heads, 4, tok), full),
            pltpu.VMEM((8 * both, tok), full),
            pltpu.VMEM((3,) + flat, full),
            pltpu.SemaphoreType.DMA((6,)),
        ]
        + [pltpu.SemaphoreType.DMA((seqs - 1,))] * 6
        + [pltpu.SemaphoreType.DMA((heads - 1,))] * 2,
        compiler_params=pltpu.CompilerParams(
            collective_id=0, has_side_effects=True, vmem_limit_bytes=VMEM_BYTES
        ),
        name="fused_backward",
    )(
        offsets,
        query_rows.reshape(flat),
        key_rows.reshape(flat),
        value_rows.reshape(flat),
        cotangent.reshape(flat),
        norm_gain,
    )
    outs = pl.pallas_call(
        place_outputs,
        out_shape=[jax.ShapeDtypeStruct(flat, low)] * 3,
        in_specs=[vmem] * 3,
        out_specs=[hbm] * 3,
        scratch_shapes=[pltpu.SemaphoreType.DMA((3,))],
        compiler_params=pltpu.CompilerParams(vmem_limit_bytes=1024 * 1024),
        name="place_outputs",
    )(*outs)
    return tuple(out.reshape(query_rows.shape) for out in outs)


def fits(mesh, tok, both, size):
    seqs = mesh.shape["seq"]
    seg1 = tok * seqs // RATE4
    return (
        tok == ROWS * RATE3
        and size == 128
        and both == 2
        and seqs * ROWS == 128
        and (RATE3 * seg1 // tok) & (RATE3 * seg1 // tok - 1) == 0
        and tok % (RATE2 * seg1) == 0
        and (RATE3 * seg1) % tok == 0
        and tok // seg1 <= 64
    )


def solution(mesh):
    placed = (
        P("seq", "head", None),
        P("seq", "head", None),
        P("seq", "head", None),
        P("seq", "head", None),
        P("head", None),
        P("head"),
    )

    def run(query_rows, key_rows, value_rows, cotangent, norm_gain, offsets):
        tokens, heads, size = query_rows.shape
        small = fits(mesh, tokens // mesh.shape["seq"], heads // mesh.shape["head"], size)
        return jax.shard_map(
            fused_shards if small else shards,
            mesh=mesh,
            in_specs=placed,
            out_specs=(P("seq", "head", None), P("seq", "head", None), P("seq", "head", None)),
            check_vma=False,
        )(query_rows, key_rows, value_rows, cotangent, norm_gain, offsets)

    return run
```

```python
import functools

import jax
import jax.numpy as jnp
from jax import lax
from jax.experimental import pallas as pl
from jax.experimental.pallas import tpu as pltpu
from jax.sharding import PartitionSpec as P

RATE2 = 4
RATE3 = 16
RATE4 = 32


neg_fill = -1e30
epsilon = 1e-05
block_width = 512


def passed_along(value, axis, steps):
    count = lax.axis_size(axis)
    leading, last = (max(0, -steps), min(count, count - steps))
    return lax.ppermute(value, axis, [(source, source + steps) for source in range(leading, last)])


def pick_rows(source, wanted, stride):
    row_count = source.shape[0] // stride
    shaped = source.reshape((row_count, stride) + source.shape[1:])
    trailing = (1,) * (source.ndim - 2)
    target = wanted.reshape((1, 1, -1) + trailing)
    column = jnp.arange(stride, dtype=jnp.int32).reshape((1, stride, 1) + trailing)
    zeroed = jnp.where(column == target, shaped, jnp.zeros((), source.dtype))
    return jnp.sum(zeroed, axis=1, dtype=source.dtype)


def put_rows(compact, wanted, stride, filler):
    trailing = (1,) * (compact.ndim - 2)
    target = wanted.reshape((1, 1, -1) + trailing)
    column = jnp.arange(stride, dtype=jnp.int32).reshape((1, stride, 1) + trailing)
    spread = jnp.where(column == target, compact[:, None], jnp.asarray(filler, compact.dtype))
    return spread.reshape((compact.shape[0] * stride,) + compact.shape[1:])


def row_places(device, slot_count, direction, row_count, stride, wanted, tok_dev):
    owners = device + direction * jnp.arange(slot_count, dtype=jnp.int32)
    within_dev = wanted[None, :] + stride * jnp.arange(row_count, dtype=jnp.int32)[:, None]
    places = owners[:, None, None] * tok_dev + within_dev[None]
    return places.reshape(slot_count * row_count, wanted.shape[0])


def masked_scores(query_blk, key_blk, query_pos, key_pos, seg_len, score_scale):
    raw = (
        jnp.einsum("qhd,khd->hqk", query_blk, key_blk, preferred_element_type=jnp.float32)
        * score_scale
    )
    query_at = query_pos.T[:, :, None]
    key_at = key_pos.T[:, None, :]
    linked = (query_at // seg_len == key_at // seg_len) & (key_at <= query_at)
    return jnp.where(linked, raw, neg_fill)


def flatten_slots(member):
    return member.reshape((member.shape[0] * member.shape[1],) + member.shape[2:])


def extend(buffers, target, sign, puller):
    while buffers[0].shape[0] < target:
        covered = buffers[0].shape[0]
        arrived = puller(buffers, sign * covered)
        buffers = tuple(
            (jnp.concatenate([held, current], axis=0) for held, current in zip(buffers, arrived))
        )
    return buffers


def pull_keys(buffers, offset):
    return passed_along((buffers[0], buffers[1]), "seq", offset)


def pull_queries(buffers, offset):
    moved = passed_along((buffers[0], buffers[1]), "seq", offset)
    stats = passed_along((buffers[2], buffers[3]), "seq", offset)
    return (moved[0], moved[1], stats[0], stats[1])


def feature_sums(first, second):
    return lax.psum((first, second), "head")


def shards(query_rows, key_rows, value_rows, cotangent, norm_gain, offsets):
    tok_dev, heads_dev, head_size = query_rows.shape
    seq_count = lax.axis_size("seq")
    device = lax.axis_index("seq")
    group_rows = tok_dev * seq_count // RATE4
    score_scale = head_size ** (-0.5)
    features = heads_dev * head_size * lax.axis_size("head")
    levels = []
    for stride in (1, RATE2, RATE3, RATE4):
        seg_len = stride * group_rows
        levels.append((stride, seg_len, max(1, seg_len // tok_dev), offsets % stride))
    key_sets = []
    for stride, seg_len, span_devices, wanted in levels:
        own_rows = (
            pick_rows(key_rows, wanted, stride)[None],
            pick_rows(value_rows, wanted, stride)[None],
        )
        key_sets.append(extend(own_rows, span_devices, 1, pull_keys))
    prepared = []
    for (stride, seg_len, span_devices, wanted), key_set in zip(levels, key_sets):
        row_count = tok_dev // stride
        key_flat = flatten_slots(key_set[0])
        value_flat = flatten_slots(key_set[1])
        key_places = row_places(device, key_set[0].shape[0], -1, row_count, stride, wanted, tok_dev)
        query_sel = pick_rows(query_rows, wanted, stride)
        query_places = row_places(device, 1, -1, row_count, stride, wanted, tok_dev)
        prepared.append(
            (
                stride,
                seg_len,
                span_devices,
                wanted,
                row_count,
                key_flat,
                value_flat,
                key_places,
                query_sel,
                query_places,
            )
        )
    lse_total = jnp.full((tok_dev, heads_dev), neg_fill, jnp.float32)
    for (
        stride,
        seg_len,
        span_devices,
        wanted,
        row_count,
        key_flat,
        value_flat,
        key_places,
        query_sel,
        query_places,
    ) in prepared:
        level_lse = jnp.full((row_count, heads_dev), neg_fill, jnp.float32)
        for first_row in range(0, key_flat.shape[0], block_width):
            scores = masked_scores(
                query_sel,
                key_flat[first_row : first_row + block_width],
                query_places,
                key_places[first_row : first_row + block_width],
                seg_len,
                score_scale,
            )
            row_peak = jnp.max(scores, axis=2)
            block_lse = row_peak + jnp.log(jnp.sum(jnp.exp(scores - row_peak[:, :, None]), axis=2))
            level_lse = jnp.logaddexp(level_lse, block_lse.T)
        lse_total = jnp.logaddexp(lse_total, put_rows(level_lse, wanted, stride, neg_fill))
    attended = jnp.zeros((tok_dev, heads_dev, head_size), jnp.float32)
    for (
        stride,
        seg_len,
        span_devices,
        wanted,
        row_count,
        key_flat,
        value_flat,
        key_places,
        query_sel,
        query_places,
    ) in prepared:
        lse_sel = pick_rows(lse_total, wanted, stride)
        out_sel = jnp.zeros((row_count, heads_dev, head_size), jnp.float32)
        for first_row in range(0, key_flat.shape[0], block_width):
            scores = masked_scores(
                query_sel,
                key_flat[first_row : first_row + block_width],
                query_places,
                key_places[first_row : first_row + block_width],
                seg_len,
                score_scale,
            )
            weights = jnp.exp(scores - lse_sel.T[:, :, None]).astype(jnp.bfloat16)
            out_sel = out_sel + jnp.einsum(
                "hqk,khd->qhd",
                weights,
                value_flat[first_row : first_row + block_width],
                preferred_element_type=jnp.float32,
            )
        attended = attended + put_rows(out_sel, wanted, stride, 0.0)
    totals = feature_sums(jnp.sum(attended, axis=(1, 2)), jnp.sum(attended * attended, axis=(1, 2)))
    centre = totals[0] / features
    variance = totals[1] / features - centre * centre
    inverse = lax.rsqrt(variance + epsilon)
    normed = (attended - centre[:, None, None]) * inverse[:, None, None]
    grad_in = cotangent.astype(jnp.float32) * norm_gain[None]
    moments = feature_sums(jnp.sum(grad_in, axis=(1, 2)), jnp.sum(grad_in * normed, axis=(1, 2)))
    first_mean = moments[0] / features
    second_mean = moments[1] / features
    d_attended = (
        inverse[:, None, None]
        * (grad_in - first_mean[:, None, None] - normed * second_mean[:, None, None])
    ).astype(jnp.bfloat16)
    row_delta = jnp.sum(d_attended.astype(jnp.float32) * attended, axis=2)
    query_grad = jnp.zeros((tok_dev, heads_dev, head_size), jnp.float32)
    for (
        stride,
        seg_len,
        span_devices,
        wanted,
        row_count,
        key_flat,
        value_flat,
        key_places,
        query_sel,
        query_places,
    ) in prepared:
        lse_sel = pick_rows(lse_total, wanted, stride)
        dout_sel = pick_rows(d_attended, wanted, stride)
        delta_sel = pick_rows(row_delta, wanted, stride)
        grad_sel = jnp.zeros((row_count, heads_dev, head_size), jnp.float32)
        for first_row in range(0, key_flat.shape[0], block_width):
            key_block = key_flat[first_row : first_row + block_width]
            scores = masked_scores(
                query_sel,
                key_block,
                query_places,
                key_places[first_row : first_row + block_width],
                seg_len,
                score_scale,
            )
            weights = jnp.exp(scores - lse_sel.T[:, :, None])
            weight_grad = jnp.einsum(
                "qhd,khd->hqk",
                dout_sel,
                value_flat[first_row : first_row + block_width],
                preferred_element_type=jnp.float32,
            )
            score_grad = (weights * (weight_grad - delta_sel.T[:, :, None])).astype(jnp.bfloat16)
            grad_sel = grad_sel + jnp.einsum(
                "hqk,khd->qhd", score_grad, key_block, preferred_element_type=jnp.float32
            )
        query_grad = query_grad + put_rows(grad_sel * score_scale, wanted, stride, 0.0)
    query_sets = []
    for stride, seg_len, span_devices, wanted in levels:
        own_rows = (
            pick_rows(query_rows, wanted, stride)[None],
            pick_rows(d_attended, wanted, stride)[None],
            pick_rows(lse_total, wanted, stride)[None],
            pick_rows(row_delta, wanted, stride)[None],
        )
        query_sets.append(extend(own_rows, span_devices, -1, pull_queries))
    key_grad = jnp.zeros((tok_dev, heads_dev, head_size), jnp.float32)
    value_grad = jnp.zeros((tok_dev, heads_dev, head_size), jnp.float32)
    for (
        stride,
        seg_len,
        span_devices,
        wanted,
        row_count,
        key_flat,
        value_flat,
        key_places,
        query_sel,
        query_places,
    ), query_set in zip(prepared, query_sets):
        query_flat = flatten_slots(query_set[0])
        dout_flat = flatten_slots(query_set[1])
        lse_flat = flatten_slots(query_set[2])
        delta_flat = flatten_slots(query_set[3])
        query_far = row_places(device, query_set[0].shape[0], 1, row_count, stride, wanted, tok_dev)
        key_sel = pick_rows(key_rows, wanted, stride)
        value_sel = pick_rows(value_rows, wanted, stride)
        key_grad_sel = jnp.zeros((row_count, heads_dev, head_size), jnp.float32)
        value_grad_sel = jnp.zeros((row_count, heads_dev, head_size), jnp.float32)
        for first_row in range(0, query_flat.shape[0], block_width):
            query_block = query_flat[first_row : first_row + block_width]
            dout_block = dout_flat[first_row : first_row + block_width]
            lse_block = lse_flat[first_row : first_row + block_width]
            delta_block = delta_flat[first_row : first_row + block_width]
            scores = masked_scores(
                query_block,
                key_sel,
                query_far[first_row : first_row + block_width],
                query_places,
                seg_len,
                score_scale,
            )
            weights = jnp.exp(scores - lse_block.T[:, :, None])
            value_grad_sel = value_grad_sel + jnp.einsum(
                "hqk,qhd->khd",
                weights.astype(jnp.bfloat16),
                dout_block,
                preferred_element_type=jnp.float32,
            )
            weight_grad = jnp.einsum(
                "qhd,khd->hqk", dout_block, value_sel, preferred_element_type=jnp.float32
            )
            score_grad = (weights * (weight_grad - delta_block.T[:, :, None])).astype(jnp.bfloat16)
            key_grad_sel = key_grad_sel + jnp.einsum(
                "hqk,qhd->khd", score_grad, query_block, preferred_element_type=jnp.float32
            )
        key_grad = key_grad + put_rows(key_grad_sel * score_scale, wanted, stride, 0.0)
        value_grad = value_grad + put_rows(value_grad_sel, wanted, stride, 0.0)
    return (
        query_grad.astype(jnp.bfloat16),
        key_grad.astype(jnp.bfloat16),
        value_grad.astype(jnp.bfloat16),
    )

MESH = pl.DeviceIdType.MESH
LOG2E = 1.4426950408889634
HIDDEN = -1e30
ROWS = 16
VMEM_BYTES = 54752 * 1024


def dot_nn(a, b):
    return lax.dot_general(a, b, (((1,), (0,)), ((), ())), preferred_element_type=jnp.float32)


def dot_nt(a, b):
    return lax.dot_general(a, b, (((1,), (1,)), ((), ())), preferred_element_type=jnp.float32)


def dot_tn(a, b):
    return lax.dot_general(a, b, (((0,), (0,)), ((), ())), preferred_element_type=jnp.float32)


def iota(shape, axis):
    return lax.broadcasted_iota(jnp.int32, shape, axis)


def bias_of(count):
    return jnp.where(count > 0.5, jnp.log2(jnp.maximum(count, 1.0)), HIDDEN)


def fused(
    seqs,
    heads,
    seg1,
    features,
    off_hbm,
    q_hbm,
    k_hbm,
    v_hbm,
    c_hbm,
    gain_hbm,
    dq_ref,
    dk_ref,
    dv_ref,
    off_ref,
    gain_ref,
    xin,
    wide,
    mats,
    grads,
    weights,
    far_weights,
    bias,
    far_bias,
    late_score,
    picker,
    placer,
    kvsel,
    qsel,
    dosel,
    kvbuf,
    qbuf,
    dobuf,
    hsend,
    hbuf,
    rows_ref,
    outwide,
    in_sem,
    kv_send,
    kv_recv,
    q_send,
    q_recv,
    do_send,
    do_recv,
    h_send,
    h_recv,
):
    me = lax.axis_index("seq")
    mine = lax.axis_index("head")
    both, tok = mats.shape[1], mats.shape[2]
    size = mats.shape[3]
    far = seqs * ROWS
    half = ROWS // 2
    quad = RATE3 * seg1 // tok
    scale = size ** (-0.5)
    scale2 = scale * LOG2E

    loads = []
    for at, (source, target) in enumerate(
        (
            (off_hbm, off_ref),
            (k_hbm, xin.at[0]),
            (v_hbm, xin.at[1]),
            (q_hbm, xin.at[2]),
            (c_hbm, xin.at[3]),
            (gain_hbm, gain_ref),
        )
    ):
        copy = pltpu.make_async_copy(source, target, in_sem.at[at])
        copy.start()
        loads.append(copy)
    kvbuf[...] = jnp.zeros_like(kvbuf)
    qbuf[...] = jnp.zeros_like(qbuf)
    dobuf[...] = jnp.zeros_like(dobuf)
    hbuf[...] = jnp.zeros_like(hbuf)

    barrier = pltpu.get_barrier_semaphore()
    for step in range(1, seqs):
        pl.semaphore_signal(
            barrier, inc=1, device_id=(lax.rem(me + step, seqs), mine), device_id_type=MESH
        )
    for step in range(1, heads):
        pl.semaphore_signal(
            barrier, inc=1, device_id=(me, lax.rem(mine + step, heads)), device_id_type=MESH
        )
    rows_ref[...] = jnp.zeros_like(rows_ref)

    def remote(source, target, send, recv, step, owner):
        return pltpu.make_async_remote_copy(
            src_ref=source,
            dst_ref=target,
            send_sem=send.at[step - 1],
            recv_sem=recv.at[step - 1],
            device_id=owner,
            device_id_type=MESH,
        )

    def peer(step):
        owner = me
        for bit in range(step.bit_length()):
            if (step >> bit) & 1:
                owner = owner + 2**bit * (1 - 2 * ((me // 2**bit) % 2))
        return (owner, mine)

    kv_copies, q_copies, do_copies = {}, {}, {}
    for step in range(1, seqs):
        count = 2 * ROWS if step < quad else ROWS
        top = pl.ds(0, count)
        kv_copies[step] = remote(
            kvsel.at[:, top], kvbuf.at[:, me, top], kv_send, kv_recv, step, peer(step)
        )
        q_copies[step] = remote(qsel.at[top], qbuf.at[me, top], q_send, q_recv, step, peer(step))
        top = pl.ds(0, count + ROWS)
        do_copies[step] = remote(
            dosel.at[top], dobuf.at[me, top], do_send, do_recv, step, peer(step)
        )
    h_copies = [
        remote(hsend, hbuf.at[mine], h_send, h_recv, step, (me, lax.rem(mine + step, heads)))
        for step in range(1, heads)
    ]

    def each(side, copies, action):
        width = seqs // 2
        while width:
            @pl.when((me // width) % 2 == side)
            def _(width=width):
                for step in range(width, 2 * width):
                    getattr(copies[step], action)()

            width //= 2

    def per_head(mixed, h):
        groups = mixed.astype(jnp.float32).reshape(seqs, 2, both, half, size)
        return groups[:, :, h].reshape(far, size).astype(jnp.bfloat16)

    def select(at, g):
        rows = []
        for h in range(both):
            start = both * ((wanted[h] & (RATE4 - 1)) ^ (RATE3 * g)) + h
            rows.append(wide[at, pl.ds(start, half, stride=both * RATE4), :])
        return jnp.concatenate(rows, axis=0).astype(jnp.bfloat16)

    loads[0].wait()
    wanted = [off_ref[h] for h in range(both)]

    lane = iota((tok, 128), 1)
    token = iota((tok, 128), 0)
    causal = iota((tok, tok), 0) <= iota((tok, tok), 1)
    for h in range(both):
        off = wanted[h]
        marks = (token // seg1) == lane
        marks = marks | ((lane == 64) & ((token & (RATE2 - 1)) == (off & (RATE2 - 1))))
        marks = marks | ((lane == 65) & ((token & (RATE3 - 1)) == (off & (RATE3 - 1))))
        marks = marks | ((lane == 66) & ((token & (RATE4 - 1)) == (off & (RATE4 - 1))))
        marked = jnp.where(marks, 1.0, 0.0).astype(jnp.bfloat16)
        count = dot_nt(marked, marked)
        bias[h] = bias_of(jnp.where(causal, count, 0.0))

    for h in range(both):
        off = wanted[h]
        slot = iota((far, tok), 0) // ROWS
        query = iota((far, tok), 1)
        sel3 = (query & (RATE3 - 1)) == (off & (RATE3 - 1))
        sel4 = (query & (RATE4 - 1)) == (off & (RATE4 - 1))
        key4 = (iota((far, tok), 0) & half) == 0
        near = (slot // quad) == (me // quad)
        count = jnp.where(near & sel3, 1.0, 0.0) + jnp.where(key4 & sel4, 1.0, 0.0)
        far_bias[h] = bias_of(jnp.where(slot < me, count, 0.0))

    for at in range(2):
        loads[1 + at].wait()
        wide[at] = xin[at].astype(jnp.float32)
        for g in range(2):
            kvsel[at, pl.ds(g * ROWS, ROWS), :] = select(at, g)
    pl.semaphore_wait(barrier, seqs + heads - 2)
    each(0, kv_copies, "start")

    loads[3].wait()
    wide[2] = xin[2].astype(jnp.float32)
    for g in range(2):
        qsel[pl.ds(g * ROWS, ROWS), :] = select(2, g)

    for at in range(3):
        for h in range(both):
            mats[at, h] = wide[at, pl.ds(h, tok, stride=both), :].astype(jnp.bfloat16)

    first_stats = []
    for h in range(both):
        score = dot_nt(mats[0, h], mats[2, h]) * scale2 + bias[h]
        peak = jnp.max(score, axis=0, keepdims=True)
        held = jnp.exp2(score - peak)
        weights[h] = held
        total = jnp.sum(held, axis=0, keepdims=True)
        out = dot_tn(mats[1, h], held.astype(jnp.bfloat16))
        first_stats.append((peak, total, out))

    loads[4].wait()
    loads[5].wait()
    wide[3] = xin[3].astype(jnp.float32)
    for h in range(both):
        grad = wide[3, pl.ds(h, tok, stride=both), :] * gain_ref[h : h + 1, :]
        grads[h] = grad.T

    each(1, kv_copies, "wait_recv")

    sums = [jnp.zeros((1, tok), jnp.float32) for _ in range(4)]
    stats = []
    far_keys = [per_head(kvbuf[0], h) for h in range(both)]
    far_values = [per_head(kvbuf[1], h) for h in range(both)]
    for h in range(both):
        peak, total, out = first_stats[h]
        score = dot_nt(far_keys[h], mats[2, h]) * scale2 + far_bias[h]
        top = jnp.maximum(peak, jnp.max(score, axis=0, keepdims=True))
        shrink = jnp.exp2(peak - top)
        held = jnp.exp2(score - top)
        total = total * shrink + jnp.sum(held, axis=0, keepdims=True)
        ratio = 1.0 / total
        far_weights[h] = held * ratio
        out = (out * shrink + dot_tn(far_values[h], held.astype(jnp.bfloat16))) * ratio
        grad = grads[h]
        sums[0] = sums[0] + jnp.sum(out, axis=0, keepdims=True)
        sums[1] = sums[1] + jnp.sum(out * out, axis=0, keepdims=True)
        sums[2] = sums[2] + jnp.sum(grad, axis=0, keepdims=True)
        sums[3] = sums[3] + jnp.sum(grad * out, axis=0, keepdims=True)
        stats.append((out, shrink * ratio, top + jnp.log2(total)))
    for at in range(4):
        hsend[at : at + 1, :] = sums[at]
    for copy in h_copies:
        copy.start()
    each(1, q_copies, "start")

    for h in range(both):
        weights[h] = weights[h] * stats[h][1]
    row = iota((2 * ROWS, both * tok), 0)
    column = iota((2 * ROWS, both * tok), 1)
    head_of = (row // half) & 1
    start = jnp.where(head_of == 0, wanted[0], wanted[1]) & (RATE4 - 1)
    place = (start ^ (RATE3 * (row // ROWS))) + RATE4 * (row & (half - 1)) + tok * head_of
    picker[...] = jnp.where(column == place, 1.0, 0.0).astype(jnp.bfloat16)
    for h in range(both):
        token = iota((tok, far), 0)
        column = iota((tok, far), 1)
        start = (wanted[h] & (RATE4 - 1)) ^ (2 * (column & half))
        hit = (token == start + RATE4 * (column & (half - 1))) & (column // ROWS == me)
        placer[:, pl.ds(h * far, far)] = jnp.where(hit, 1.0, 0.0).astype(jnp.bfloat16)

    def put_pieces(h, at, rest):
        for piece in range(3):
            part = rest.astype(jnp.bfloat16).astype(jnp.float32)
            rest = rest - part
            line = 8 * h + 2 * piece + at
            rows_ref[line : line + 1, :] = part

    for h in range(both):
        put_pieces(h, 0, stats[h][2])

    for copy in h_copies:
        copy.wait_recv()
    full = hsend[...]
    for at in range(heads):
        full = full + hbuf[at]
    full = full * (1.0 / features)
    centre = full[0:1]
    inverse = lax.rsqrt(full[1:2] - centre * centre + epsilon)
    first = full[2:3]
    second = inverse * (full[3:4] - centre * first)

    douts = []
    for h in range(both):
        out = stats[h][0]
        normed = (out - centre) * inverse
        dout = (inverse * (grads[h] - first - normed * second)).astype(jnp.bfloat16)
        delta = jnp.sum(dout.astype(jnp.float32) * out, axis=0, keepdims=True)
        put_pieces(h, 1, delta)
        douts.append((dout, delta))
    chosen = dot_nt(picker[...], jnp.concatenate([item[0] for item in douts], axis=1))
    moved = dot_nn(rows_ref[...].astype(jnp.bfloat16), placer[...])
    moved = jnp.concatenate([moved[0:8, 0:far], moved[8:16, far : 2 * far]], axis=0)
    dosel[0:ROWS, :] = chosen[0:ROWS].astype(jnp.bfloat16)
    dosel[ROWS : 2 * ROWS, :] = moved.astype(jnp.bfloat16)
    dosel[2 * ROWS : 3 * ROWS, :] = chosen[ROWS : 2 * ROWS].astype(jnp.bfloat16)
    each(1, do_copies, "start")

    key_parts = []
    for h in range(both):
        dout, delta = douts[h]
        weight = weights[h]
        weight_grad = dot_nn(mats[1, h], dout)
        score_grad = (weight * (weight_grad - delta)).astype(jnp.bfloat16)
        value_part = dot_nt(weight.astype(jnp.bfloat16), dout)
        key_part = dot_nn(score_grad, mats[2, h])
        far_grad = dot_nn(far_values[h], dout)
        far_score = (far_weights[h] * (far_grad - delta)).astype(jnp.bfloat16)
        query_part = dot_tn(mats[0, h], score_grad) + dot_tn(far_keys[h], far_score)
        outwide[0, pl.ds(h, tok, stride=both), :] = (query_part * scale).T
        key_parts.append((key_part, value_part))
    dq_ref[...] = outwide[0].astype(jnp.bfloat16)

    each(0, q_copies, "wait_recv")
    late_queries = [per_head(qbuf[...], h) for h in range(both)]
    for h in range(both):
        off = wanted[h]
        slot = iota((tok, far), 1) // ROWS
        key = iota((tok, far), 0)
        sel3 = (key & (RATE3 - 1)) == (off & (RATE3 - 1))
        sel4 = (key & (RATE4 - 1)) == (off & (RATE4 - 1))
        query4 = (iota((tok, far), 1) & half) == 0
        near = (slot // quad) == (me // quad)
        count = jnp.where(near & sel3, 1.0, 0.0) + jnp.where(query4 & sel4, 1.0, 0.0)
        late_bias = bias_of(jnp.where(slot > me, count, 0.0))
        late_score[h] = dot_nt(mats[0, h], late_queries[h]) * scale2 + late_bias

    each(0, do_copies, "wait_recv")

    arrived = dobuf[...].astype(jnp.float32)
    mixed = jnp.stack([arrived[:, 0:ROWS], arrived[:, 2 * ROWS : 3 * ROWS]], axis=1)
    lines = arrived[0, ROWS : 2 * ROWS]
    for at in range(1, seqs):
        lines = lines + arrived[at, ROWS : 2 * ROWS]
    for h in range(both):
        key_part, value_part = key_parts[h]
        late_douts = per_head(mixed, h)
        at = 8 * h
        lse = lines[at : at + 1] + lines[at + 2 : at + 3] + lines[at + 4 : at + 5]
        delta = lines[at + 1 : at + 2] + lines[at + 3 : at + 4] + lines[at + 5 : at + 6]
        weight = jnp.exp2(late_score[h] - lse)
        weight_grad = dot_nt(mats[1, h], late_douts)
        score_grad = (weight * (weight_grad - delta)).astype(jnp.bfloat16)
        value_part = value_part + dot_nn(weight.astype(jnp.bfloat16), late_douts)
        key_part = key_part + dot_nn(score_grad, late_queries[h])
        outwide[1, pl.ds(h, tok, stride=both), :] = key_part * scale
        outwide[2, pl.ds(h, tok, stride=both), :] = value_part
    dk_ref[...] = outwide[1].astype(jnp.bfloat16)
    dv_ref[...] = outwide[2].astype(jnp.bfloat16)

    each(0, kv_copies, "wait_send")
    each(1, q_copies, "wait_send")
    each(1, do_copies, "wait_send")
    for copy in h_copies:
        copy.wait_send()


def place_outputs(dq_ref, dk_ref, dv_ref, dq_hbm, dk_hbm, dv_hbm, sem):
    copies = [
        pltpu.make_async_copy(source, target, sem.at[at])
        for at, (source, target) in enumerate(
            ((dq_ref, dq_hbm), (dk_ref, dk_hbm), (dv_ref, dv_hbm))
        )
    ]
    for copy in copies:
        copy.start()
    for copy in copies:
        copy.wait()


def fused_shards(query_rows, key_rows, value_rows, cotangent, norm_gain, offsets):
    tok, both, size = query_rows.shape
    seqs = lax.axis_size("seq")
    heads = lax.axis_size("head")
    seg1 = tok * seqs // RATE4
    far = seqs * ROWS
    flat = (both * tok, size)
    low, full = jnp.bfloat16, jnp.float32
    vmem = pl.BlockSpec(memory_space=pltpu.VMEM)
    hbm = pl.BlockSpec(memory_space=pltpu.HBM)
    outs = pl.pallas_call(
        functools.partial(fused, seqs, heads, seg1, both * size * heads),
        out_shape=[jax.ShapeDtypeStruct(flat, low)] * 3,
        in_specs=[hbm] * 6,
        out_specs=[vmem] * 3,
        scratch_shapes=[
            pltpu.SMEM((both,), jnp.int32),
            pltpu.VMEM((both, size), full),
            pltpu.VMEM((4,) + flat, low),
            pltpu.VMEM((4,) + flat, full),
            pltpu.VMEM((3, both, tok, size), low),
            pltpu.VMEM((both, size, tok), full),
            pltpu.VMEM((both, tok, tok), full),
            pltpu.VMEM((both, far, tok), full),
            pltpu.VMEM((both, tok, tok), full),
            pltpu.VMEM((both, far, tok), full),
            pltpu.VMEM((both, tok, far), full),
            pltpu.VMEM((2 * ROWS, both * tok), low),
            pltpu.VMEM((tok, both * far), low),
            pltpu.VMEM((2, 2 * ROWS, size), low),
            pltpu.VMEM((2 * ROWS, size), low),
            pltpu.VMEM((3 * ROWS, size), low),
            pltpu.VMEM((2, seqs, 2 * ROWS, size), low),
            pltpu.VMEM((seqs, 2 * ROWS, size), low),
            pltpu.VMEM((seqs, 3 * ROWS, size), low),
            pltpu.VMEM((4, tok), full),
            pltpu.VMEM((heads, 4, tok), full),
            pltpu.VMEM((8 * both, tok), full),
            pltpu.VMEM((3,) + flat, full),
            pltpu.SemaphoreType.DMA((6,)),
        ]
        + [pltpu.SemaphoreType.DMA((seqs - 1,))] * 6
        + [pltpu.SemaphoreType.DMA((heads - 1,))] * 2,
        compiler_params=pltpu.CompilerParams(
            collective_id=0, has_side_effects=True, vmem_limit_bytes=VMEM_BYTES
        ),
        name="fused_backward",
    )(
        offsets,
        query_rows.reshape(flat),
        key_rows.reshape(flat),
        value_rows.reshape(flat),
        cotangent.reshape(flat),
        norm_gain,
    )
    outs = pl.pallas_call(
        place_outputs,
        out_shape=[jax.ShapeDtypeStruct(flat, low)] * 3,
        in_specs=[vmem] * 3,
        out_specs=[hbm] * 3,
        scratch_shapes=[pltpu.SemaphoreType.DMA((3,))],
        compiler_params=pltpu.CompilerParams(vmem_limit_bytes=1024 * 1024),
        name="place_outputs",
    )(*outs)
    return tuple(out.reshape(query_rows.shape) for out in outs)


def fits(mesh, tok, both, size):
    seqs = mesh.shape["seq"]
    seg1 = tok * seqs // RATE4
    return (
        tok == ROWS * RATE3
        and size == 128
        and both == 2
        and seqs * ROWS == 128
        and (RATE3 * seg1 // tok) & (RATE3 * seg1 // tok - 1) == 0
        and tok % (RATE2 * seg1) == 0
        and (RATE3 * seg1) % tok == 0
        and tok // seg1 <= 64
    )


def solution(mesh):
    placed = (
        P("seq", "head", None),
        P("seq", "head", None),
        P("seq", "head", None),
        P("seq", "head", None),
        P("head", None),
        P("head"),
    )

    def run(query_rows, key_rows, value_rows, cotangent, norm_gain, offsets):
        tokens, heads, size = query_rows.shape
        small = fits(mesh, tokens // mesh.shape["seq"], heads // mesh.shape["head"], size)
        return jax.shard_map(
            fused_shards if small else shards,
            mesh=mesh,
            in_specs=placed,
            out_specs=(P("seq", "head", None), P("seq", "head", None), P("seq", "head", None)),
            check_vma=False,
        )(query_rows, key_rows, value_rows, cotangent, norm_gain, offsets)

    return run
```

```python
import functools

import jax
import jax.numpy as jnp
from jax import lax
from jax.experimental import pallas as pl
from jax.experimental.pallas import tpu as pltpu
from jax.sharding import PartitionSpec as P

RATE2 = 4
RATE3 = 16
RATE4 = 32


neg_fill = -1e30
epsilon = 1e-05
block_width = 512


def passed_along(value, axis, steps):
    count = lax.axis_size(axis)
    leading, last = (max(0, -steps), min(count, count - steps))
    return lax.ppermute(value, axis, [(source, source + steps) for source in range(leading, last)])


def pick_rows(source, wanted, stride):
    row_count = source.shape[0] // stride
    shaped = source.reshape((row_count, stride) + source.shape[1:])
    trailing = (1,) * (source.ndim - 2)
    target = wanted.reshape((1, 1, -1) + trailing)
    column = jnp.arange(stride, dtype=jnp.int32).reshape((1, stride, 1) + trailing)
    zeroed = jnp.where(column == target, shaped, jnp.zeros((), source.dtype))
    return jnp.sum(zeroed, axis=1, dtype=source.dtype)


def put_rows(compact, wanted, stride, filler):
    trailing = (1,) * (compact.ndim - 2)
    target = wanted.reshape((1, 1, -1) + trailing)
    column = jnp.arange(stride, dtype=jnp.int32).reshape((1, stride, 1) + trailing)
    spread = jnp.where(column == target, compact[:, None], jnp.asarray(filler, compact.dtype))
    return spread.reshape((compact.shape[0] * stride,) + compact.shape[1:])


def row_places(device, slot_count, direction, row_count, stride, wanted, tok_dev):
    owners = device + direction * jnp.arange(slot_count, dtype=jnp.int32)
    within_dev = wanted[None, :] + stride * jnp.arange(row_count, dtype=jnp.int32)[:, None]
    places = owners[:, None, None] * tok_dev + within_dev[None]
    return places.reshape(slot_count * row_count, wanted.shape[0])


def masked_scores(query_blk, key_blk, query_pos, key_pos, seg_len, score_scale):
    raw = (
        jnp.einsum("qhd,khd->hqk", query_blk, key_blk, preferred_element_type=jnp.float32)
        * score_scale
    )
    query_at = query_pos.T[:, :, None]
    key_at = key_pos.T[:, None, :]
    linked = (query_at // seg_len == key_at // seg_len) & (key_at <= query_at)
    return jnp.where(linked, raw, neg_fill)


def flatten_slots(member):
    return member.reshape((member.shape[0] * member.shape[1],) + member.shape[2:])


def extend(buffers, target, sign, puller):
    while buffers[0].shape[0] < target:
        covered = buffers[0].shape[0]
        arrived = puller(buffers, sign * covered)
        buffers = tuple(
            (jnp.concatenate([held, current], axis=0) for held, current in zip(buffers, arrived))
        )
    return buffers


def pull_keys(buffers, offset):
    return passed_along((buffers[0], buffers[1]), "seq", offset)


def pull_queries(buffers, offset):
    moved = passed_along((buffers[0], buffers[1]), "seq", offset)
    stats = passed_along((buffers[2], buffers[3]), "seq", offset)
    return (moved[0], moved[1], stats[0], stats[1])


def feature_sums(first, second):
    return lax.psum((first, second), "head")


def shards(query_rows, key_rows, value_rows, cotangent, norm_gain, offsets):
    tok_dev, heads_dev, head_size = query_rows.shape
    seq_count = lax.axis_size("seq")
    device = lax.axis_index("seq")
    group_rows = tok_dev * seq_count // RATE4
    score_scale = head_size ** (-0.5)
    features = heads_dev * head_size * lax.axis_size("head")
    levels = []
    for stride in (1, RATE2, RATE3, RATE4):
        seg_len = stride * group_rows
        levels.append((stride, seg_len, max(1, seg_len // tok_dev), offsets % stride))
    key_sets = []
    for stride, seg_len, span_devices, wanted in levels:
        own_rows = (
            pick_rows(key_rows, wanted, stride)[None],
            pick_rows(value_rows, wanted, stride)[None],
        )
        key_sets.append(extend(own_rows, span_devices, 1, pull_keys))
    prepared = []
    for (stride, seg_len, span_devices, wanted), key_set in zip(levels, key_sets):
        row_count = tok_dev // stride
        key_flat = flatten_slots(key_set[0])
        value_flat = flatten_slots(key_set[1])
        key_places = row_places(device, key_set[0].shape[0], -1, row_count, stride, wanted, tok_dev)
        query_sel = pick_rows(query_rows, wanted, stride)
        query_places = row_places(device, 1, -1, row_count, stride, wanted, tok_dev)
        prepared.append(
            (
                stride,
                seg_len,
                span_devices,
                wanted,
                row_count,
                key_flat,
                value_flat,
                key_places,
                query_sel,
                query_places,
            )
        )
    lse_total = jnp.full((tok_dev, heads_dev), neg_fill, jnp.float32)
    for (
        stride,
        seg_len,
        span_devices,
        wanted,
        row_count,
        key_flat,
        value_flat,
        key_places,
        query_sel,
        query_places,
    ) in prepared:
        level_lse = jnp.full((row_count, heads_dev), neg_fill, jnp.float32)
        for first_row in range(0, key_flat.shape[0], block_width):
            scores = masked_scores(
                query_sel,
                key_flat[first_row : first_row + block_width],
                query_places,
                key_places[first_row : first_row + block_width],
                seg_len,
                score_scale,
            )
            row_peak = jnp.max(scores, axis=2)
            block_lse = row_peak + jnp.log(jnp.sum(jnp.exp(scores - row_peak[:, :, None]), axis=2))
            level_lse = jnp.logaddexp(level_lse, block_lse.T)
        lse_total = jnp.logaddexp(lse_total, put_rows(level_lse, wanted, stride, neg_fill))
    attended = jnp.zeros((tok_dev, heads_dev, head_size), jnp.float32)
    for (
        stride,
        seg_len,
        span_devices,
        wanted,
        row_count,
        key_flat,
        value_flat,
        key_places,
        query_sel,
        query_places,
    ) in prepared:
        lse_sel = pick_rows(lse_total, wanted, stride)
        out_sel = jnp.zeros((row_count, heads_dev, head_size), jnp.float32)
        for first_row in range(0, key_flat.shape[0], block_width):
            scores = masked_scores(
                query_sel,
                key_flat[first_row : first_row + block_width],
                query_places,
                key_places[first_row : first_row + block_width],
                seg_len,
                score_scale,
            )
            weights = jnp.exp(scores - lse_sel.T[:, :, None]).astype(jnp.bfloat16)
            out_sel = out_sel + jnp.einsum(
                "hqk,khd->qhd",
                weights,
                value_flat[first_row : first_row + block_width],
                preferred_element_type=jnp.float32,
            )
        attended = attended + put_rows(out_sel, wanted, stride, 0.0)
    totals = feature_sums(jnp.sum(attended, axis=(1, 2)), jnp.sum(attended * attended, axis=(1, 2)))
    centre = totals[0] / features
    variance = totals[1] / features - centre * centre
    inverse = lax.rsqrt(variance + epsilon)
    normed = (attended - centre[:, None, None]) * inverse[:, None, None]
    grad_in = cotangent.astype(jnp.float32) * norm_gain[None]
    moments = feature_sums(jnp.sum(grad_in, axis=(1, 2)), jnp.sum(grad_in * normed, axis=(1, 2)))
    first_mean = moments[0] / features
    second_mean = moments[1] / features
    d_attended = (
        inverse[:, None, None]
        * (grad_in - first_mean[:, None, None] - normed * second_mean[:, None, None])
    ).astype(jnp.bfloat16)
    row_delta = jnp.sum(d_attended.astype(jnp.float32) * attended, axis=2)
    query_grad = jnp.zeros((tok_dev, heads_dev, head_size), jnp.float32)
    for (
        stride,
        seg_len,
        span_devices,
        wanted,
        row_count,
        key_flat,
        value_flat,
        key_places,
        query_sel,
        query_places,
    ) in prepared:
        lse_sel = pick_rows(lse_total, wanted, stride)
        dout_sel = pick_rows(d_attended, wanted, stride)
        delta_sel = pick_rows(row_delta, wanted, stride)
        grad_sel = jnp.zeros((row_count, heads_dev, head_size), jnp.float32)
        for first_row in range(0, key_flat.shape[0], block_width):
            key_block = key_flat[first_row : first_row + block_width]
            scores = masked_scores(
                query_sel,
                key_block,
                query_places,
                key_places[first_row : first_row + block_width],
                seg_len,
                score_scale,
            )
            weights = jnp.exp(scores - lse_sel.T[:, :, None])
            weight_grad = jnp.einsum(
                "qhd,khd->hqk",
                dout_sel,
                value_flat[first_row : first_row + block_width],
                preferred_element_type=jnp.float32,
            )
            score_grad = (weights * (weight_grad - delta_sel.T[:, :, None])).astype(jnp.bfloat16)
            grad_sel = grad_sel + jnp.einsum(
                "hqk,khd->qhd", score_grad, key_block, preferred_element_type=jnp.float32
            )
        query_grad = query_grad + put_rows(grad_sel * score_scale, wanted, stride, 0.0)
    query_sets = []
    for stride, seg_len, span_devices, wanted in levels:
        own_rows = (
            pick_rows(query_rows, wanted, stride)[None],
            pick_rows(d_attended, wanted, stride)[None],
            pick_rows(lse_total, wanted, stride)[None],
            pick_rows(row_delta, wanted, stride)[None],
        )
        query_sets.append(extend(own_rows, span_devices, -1, pull_queries))
    key_grad = jnp.zeros((tok_dev, heads_dev, head_size), jnp.float32)
    value_grad = jnp.zeros((tok_dev, heads_dev, head_size), jnp.float32)
    for (
        stride,
        seg_len,
        span_devices,
        wanted,
        row_count,
        key_flat,
        value_flat,
        key_places,
        query_sel,
        query_places,
    ), query_set in zip(prepared, query_sets):
        query_flat = flatten_slots(query_set[0])
        dout_flat = flatten_slots(query_set[1])
        lse_flat = flatten_slots(query_set[2])
        delta_flat = flatten_slots(query_set[3])
        query_far = row_places(device, query_set[0].shape[0], 1, row_count, stride, wanted, tok_dev)
        key_sel = pick_rows(key_rows, wanted, stride)
        value_sel = pick_rows(value_rows, wanted, stride)
        key_grad_sel = jnp.zeros((row_count, heads_dev, head_size), jnp.float32)
        value_grad_sel = jnp.zeros((row_count, heads_dev, head_size), jnp.float32)
        for first_row in range(0, query_flat.shape[0], block_width):
            query_block = query_flat[first_row : first_row + block_width]
            dout_block = dout_flat[first_row : first_row + block_width]
            lse_block = lse_flat[first_row : first_row + block_width]
            delta_block = delta_flat[first_row : first_row + block_width]
            scores = masked_scores(
                query_block,
                key_sel,
                query_far[first_row : first_row + block_width],
                query_places,
                seg_len,
                score_scale,
            )
            weights = jnp.exp(scores - lse_block.T[:, :, None])
            value_grad_sel = value_grad_sel + jnp.einsum(
                "hqk,qhd->khd",
                weights.astype(jnp.bfloat16),
                dout_block,
                preferred_element_type=jnp.float32,
            )
            weight_grad = jnp.einsum(
                "qhd,khd->hqk", dout_block, value_sel, preferred_element_type=jnp.float32
            )
            score_grad = (weights * (weight_grad - delta_block.T[:, :, None])).astype(jnp.bfloat16)
            key_grad_sel = key_grad_sel + jnp.einsum(
                "hqk,qhd->khd", score_grad, query_block, preferred_element_type=jnp.float32
            )
        key_grad = key_grad + put_rows(key_grad_sel * score_scale, wanted, stride, 0.0)
        value_grad = value_grad + put_rows(value_grad_sel, wanted, stride, 0.0)
    return (
        query_grad.astype(jnp.bfloat16),
        key_grad.astype(jnp.bfloat16),
        value_grad.astype(jnp.bfloat16),
    )

MESH = pl.DeviceIdType.MESH
LOG2E = 1.4426950408889634
HIDDEN = -1e30
ROWS = 16
VMEM_BYTES = 54752 * 1024


def dot_nn(a, b):
    return lax.dot_general(a, b, (((1,), (0,)), ((), ())), preferred_element_type=jnp.float32)


def dot_nt(a, b):
    return lax.dot_general(a, b, (((1,), (1,)), ((), ())), preferred_element_type=jnp.float32)


def dot_tn(a, b):
    return lax.dot_general(a, b, (((0,), (0,)), ((), ())), preferred_element_type=jnp.float32)


def iota(shape, axis):
    return lax.broadcasted_iota(jnp.int32, shape, axis)


def bias_of(count):
    return jnp.where(count > 0.5, jnp.log2(jnp.maximum(count, 1.0)), HIDDEN)


def fused(
    seqs,
    heads,
    seg1,
    features,
    off_hbm,
    q_hbm,
    k_hbm,
    v_hbm,
    c_hbm,
    gain_hbm,
    dq_ref,
    dk_ref,
    dv_ref,
    off_ref,
    gain_ref,
    xin,
    wide,
    mats,
    grads,
    weights,
    far_weights,
    bias,
    far_bias,
    late_score,
    picker,
    placer,
    kvsel,
    qsel,
    dosel,
    kvbuf,
    qbuf,
    dobuf,
    hsend,
    hbuf,
    rows_ref,
    outwide,
    in_sem,
    kv_send,
    kv_recv,
    q_send,
    q_recv,
    do_send,
    do_recv,
    h_send,
    h_recv,
):
    me = lax.axis_index("seq")
    mine = lax.axis_index("head")
    both, tok = mats.shape[1], mats.shape[2]
    size = mats.shape[3]
    far = seqs * ROWS
    half = ROWS // 2
    quad = RATE3 * seg1 // tok
    scale = size ** (-0.5)
    scale2 = scale * LOG2E

    loads = []
    for at, (source, target) in enumerate(
        (
            (off_hbm, off_ref),
            (k_hbm, xin.at[0]),
            (v_hbm, xin.at[1]),
            (q_hbm, xin.at[2]),
            (c_hbm, xin.at[3]),
            (gain_hbm, gain_ref),
        )
    ):
        copy = pltpu.make_async_copy(source, target, in_sem.at[at])
        copy.start()
        loads.append(copy)
    kvbuf[...] = jnp.zeros_like(kvbuf)
    qbuf[...] = jnp.zeros_like(qbuf)
    dobuf[...] = jnp.zeros_like(dobuf)
    hbuf[...] = jnp.zeros_like(hbuf)

    barrier = pltpu.get_barrier_semaphore()
    for step in range(1, seqs):
        pl.semaphore_signal(
            barrier, inc=1, device_id=(lax.rem(me + step, seqs), mine), device_id_type=MESH
        )
    for step in range(1, heads):
        pl.semaphore_signal(
            barrier, inc=1, device_id=(me, lax.rem(mine + step, heads)), device_id_type=MESH
        )
    rows_ref[...] = jnp.zeros_like(rows_ref)

    def remote(source, target, send, recv, step, owner):
        return pltpu.make_async_remote_copy(
            src_ref=source,
            dst_ref=target,
            send_sem=send.at[step - 1],
            recv_sem=recv.at[step - 1],
            device_id=owner,
            device_id_type=MESH,
        )

    def peer(step):
        owner = me
        for bit in range(step.bit_length()):
            if (step >> bit) & 1:
                owner = owner + 2**bit * (1 - 2 * ((me // 2**bit) % 2))
        return (owner, mine)

    kv_copies, q_copies, do_copies = {}, {}, {}
    for step in range(1, seqs):
        count = 2 * ROWS if step < quad else ROWS
        top = pl.ds(0, count)
        kv_copies[step] = remote(
            kvsel.at[:, top], kvbuf.at[:, me, top], kv_send, kv_recv, step, peer(step)
        )
        q_copies[step] = remote(qsel.at[top], qbuf.at[me, top], q_send, q_recv, step, peer(step))
        top = pl.ds(0, count + ROWS)
        do_copies[step] = remote(
            dosel.at[top], dobuf.at[me, top], do_send, do_recv, step, peer(step)
        )
    h_copies = [
        remote(hsend, hbuf.at[mine], h_send, h_recv, step, (me, lax.rem(mine + step, heads)))
        for step in range(1, heads)
    ]

    def each(side, copies, action):
        width = seqs // 2
        while width:
            @pl.when((me // width) % 2 == side)
            def _(width=width):
                for step in range(width, 2 * width):
                    getattr(copies[step], action)()

            width //= 2

    def per_head(mixed, h):
        groups = mixed.astype(jnp.float32).reshape(seqs, 2, both, half, size)
        return groups[:, :, h].reshape(far, size).astype(jnp.bfloat16)

    def select(at, g):
        rows = []
        for h in range(both):
            start = both * ((wanted[h] & (RATE4 - 1)) ^ (RATE3 * g)) + h
            rows.append(wide[at, pl.ds(start, half, stride=both * RATE4), :])
        return jnp.concatenate(rows, axis=0).astype(jnp.bfloat16)

    loads[0].wait()
    wanted = [off_ref[h] for h in range(both)]

    lane = iota((tok, 128), 1)
    token = iota((tok, 128), 0)
    causal = iota((tok, tok), 0) <= iota((tok, tok), 1)
    for h in range(both):
        off = wanted[h]
        marks = (token // seg1) == lane
        marks = marks | ((lane == 64) & ((token & (RATE2 - 1)) == (off & (RATE2 - 1))))
        marks = marks | ((lane == 65) & ((token & (RATE3 - 1)) == (off & (RATE3 - 1))))
        marks = marks | ((lane == 66) & ((token & (RATE4 - 1)) == (off & (RATE4 - 1))))
        marked = jnp.where(marks, 1.0, 0.0).astype(jnp.bfloat16)
        count = dot_nt(marked, marked)
        bias[h] = bias_of(jnp.where(causal, count, 0.0))

    for h in range(both):
        off = wanted[h]
        slot = iota((far, tok), 0) // ROWS
        query = iota((far, tok), 1)
        sel3 = (query & (RATE3 - 1)) == (off & (RATE3 - 1))
        sel4 = (query & (RATE4 - 1)) == (off & (RATE4 - 1))
        key4 = (iota((far, tok), 0) & half) == 0
        near = (slot // quad) == (me // quad)
        count = jnp.where(near & sel3, 1.0, 0.0) + jnp.where(key4 & sel4, 1.0, 0.0)
        far_bias[h] = bias_of(jnp.where(slot < me, count, 0.0))

    for at in range(2):
        loads[1 + at].wait()
        wide[at] = xin[at].astype(jnp.float32)
        for g in range(2):
            kvsel[at, pl.ds(g * ROWS, ROWS), :] = select(at, g)
    pl.semaphore_wait(barrier, seqs + heads - 2)
    each(0, kv_copies, "start")

    for at in range(3, 6):
        loads[at].wait()
    wide[2] = xin[2].astype(jnp.float32)
    for g in range(2):
        qsel[pl.ds(g * ROWS, ROWS), :] = select(2, g)

    for at in range(3):
        for h in range(both):
            mats[at, h] = wide[at, pl.ds(h, tok, stride=both), :].astype(jnp.bfloat16)

    wide[3] = xin[3].astype(jnp.float32)
    for h in range(both):
        grad = wide[3, pl.ds(h, tok, stride=both), :] * gain_ref[h : h + 1, :]
        grads[h] = grad.T

    first_stats = []
    for h in range(both):
        score = dot_nt(mats[0, h], mats[2, h]) * scale2 + bias[h]
        peak = jnp.max(score, axis=0, keepdims=True)
        held = jnp.exp2(score - peak)
        weights[h] = held
        total = jnp.sum(held, axis=0, keepdims=True)
        out = dot_tn(mats[1, h], held.astype(jnp.bfloat16))
        first_stats.append((peak, total, out))

    each(1, kv_copies, "wait_recv")

    sums = [jnp.zeros((1, tok), jnp.float32) for _ in range(4)]
    stats = []
    far_keys = [per_head(kvbuf[0], h) for h in range(both)]
    far_values = [per_head(kvbuf[1], h) for h in range(both)]
    for h in range(both):
        peak, total, out = first_stats[h]
        score = dot_nt(far_keys[h], mats[2, h]) * scale2 + far_bias[h]
        top = jnp.maximum(peak, jnp.max(score, axis=0, keepdims=True))
        shrink = jnp.exp2(peak - top)
        held = jnp.exp2(score - top)
        total = total * shrink + jnp.sum(held, axis=0, keepdims=True)
        ratio = 1.0 / total
        far_weights[h] = held * ratio
        out = (out * shrink + dot_tn(far_values[h], held.astype(jnp.bfloat16))) * ratio
        grad = grads[h]
        sums[0] = sums[0] + jnp.sum(out, axis=0, keepdims=True)
        sums[1] = sums[1] + jnp.sum(out * out, axis=0, keepdims=True)
        sums[2] = sums[2] + jnp.sum(grad, axis=0, keepdims=True)
        sums[3] = sums[3] + jnp.sum(grad * out, axis=0, keepdims=True)
        stats.append((out, shrink * ratio, top + jnp.log2(total)))
    for at in range(4):
        hsend[at : at + 1, :] = sums[at]
    for copy in h_copies:
        copy.start()
    each(1, q_copies, "start")

    for h in range(both):
        weights[h] = weights[h] * stats[h][1]
    row = iota((2 * ROWS, both * tok), 0)
    column = iota((2 * ROWS, both * tok), 1)
    head_of = (row // half) & 1
    start = jnp.where(head_of == 0, wanted[0], wanted[1]) & (RATE4 - 1)
    place = (start ^ (RATE3 * (row // ROWS))) + RATE4 * (row & (half - 1)) + tok * head_of
    picker[...] = jnp.where(column == place, 1.0, 0.0).astype(jnp.bfloat16)
    for h in range(both):
        token = iota((tok, far), 0)
        column = iota((tok, far), 1)
        start = (wanted[h] & (RATE4 - 1)) ^ (2 * (column & half))
        hit = (token == start + RATE4 * (column & (half - 1))) & (column // ROWS == me)
        placer[:, pl.ds(h * far, far)] = jnp.where(hit, 1.0, 0.0).astype(jnp.bfloat16)

    def put_pieces(h, at, rest):
        for piece in range(3):
            part = rest.astype(jnp.bfloat16).astype(jnp.float32)
            rest = rest - part
            line = 8 * h + 2 * piece + at
            rows_ref[line : line + 1, :] = part

    for h in range(both):
        put_pieces(h, 0, stats[h][2])

    for copy in h_copies:
        copy.wait_recv()
    full = hsend[...]
    for at in range(heads):
        full = full + hbuf[at]
    full = full * (1.0 / features)
    centre = full[0:1]
    inverse = lax.rsqrt(full[1:2] - centre * centre + epsilon)
    first = full[2:3]
    second = inverse * (full[3:4] - centre * first)

    douts = []
    for h in range(both):
        out = stats[h][0]
        normed = (out - centre) * inverse
        dout = (inverse * (grads[h] - first - normed * second)).astype(jnp.bfloat16)
        delta = jnp.sum(dout.astype(jnp.float32) * out, axis=0, keepdims=True)
        put_pieces(h, 1, delta)
        douts.append((dout, delta))
    chosen = dot_nt(picker[...], jnp.concatenate([item[0] for item in douts], axis=1))
    moved = dot_nn(rows_ref[...].astype(jnp.bfloat16), placer[...])
    moved = jnp.concatenate([moved[0:8, 0:far], moved[8:16, far : 2 * far]], axis=0)
    dosel[0:ROWS, :] = chosen[0:ROWS].astype(jnp.bfloat16)
    dosel[ROWS : 2 * ROWS, :] = moved.astype(jnp.bfloat16)
    dosel[2 * ROWS : 3 * ROWS, :] = chosen[ROWS : 2 * ROWS].astype(jnp.bfloat16)
    each(1, do_copies, "start")

    key_parts = []
    for h in range(both):
        dout, delta = douts[h]
        weight = weights[h]
        weight_grad = dot_nn(mats[1, h], dout)
        score_grad = (weight * (weight_grad - delta)).astype(jnp.bfloat16)
        value_part = dot_nt(weight.astype(jnp.bfloat16), dout)
        key_part = dot_nn(score_grad, mats[2, h])
        far_grad = dot_nn(far_values[h], dout)
        far_score = (far_weights[h] * (far_grad - delta)).astype(jnp.bfloat16)
        query_part = dot_tn(mats[0, h], score_grad) + dot_tn(far_keys[h], far_score)
        outwide[0, pl.ds(h, tok, stride=both), :] = (query_part * scale).T
        key_parts.append((key_part, value_part))
    dq_ref[...] = outwide[0].astype(jnp.bfloat16)

    each(0, q_copies, "wait_recv")
    late_queries = [per_head(qbuf[...], h) for h in range(both)]
    for h in range(both):
        off = wanted[h]
        slot = iota((tok, far), 1) // ROWS
        key = iota((tok, far), 0)
        sel3 = (key & (RATE3 - 1)) == (off & (RATE3 - 1))
        sel4 = (key & (RATE4 - 1)) == (off & (RATE4 - 1))
        query4 = (iota((tok, far), 1) & half) == 0
        near = (slot // quad) == (me // quad)
        count = jnp.where(near & sel3, 1.0, 0.0) + jnp.where(query4 & sel4, 1.0, 0.0)
        late_bias = bias_of(jnp.where(slot > me, count, 0.0))
        late_score[h] = dot_nt(mats[0, h], late_queries[h]) * scale2 + late_bias

    each(0, do_copies, "wait_recv")

    arrived = dobuf[...].astype(jnp.float32)
    mixed = jnp.stack([arrived[:, 0:ROWS], arrived[:, 2 * ROWS : 3 * ROWS]], axis=1)
    lines = arrived[0, ROWS : 2 * ROWS]
    for at in range(1, seqs):
        lines = lines + arrived[at, ROWS : 2 * ROWS]
    for h in range(both):
        key_part, value_part = key_parts[h]
        late_douts = per_head(mixed, h)
        at = 8 * h
        lse = lines[at : at + 1] + lines[at + 2 : at + 3] + lines[at + 4 : at + 5]
        delta = lines[at + 1 : at + 2] + lines[at + 3 : at + 4] + lines[at + 5 : at + 6]
        weight = jnp.exp2(late_score[h] - lse)
        weight_grad = dot_nt(mats[1, h], late_douts)
        score_grad = (weight * (weight_grad - delta)).astype(jnp.bfloat16)
        value_part = value_part + dot_nn(weight.astype(jnp.bfloat16), late_douts)
        key_part = key_part + dot_nn(score_grad, late_queries[h])
        outwide[1, pl.ds(h, tok, stride=both), :] = key_part * scale
        outwide[2, pl.ds(h, tok, stride=both), :] = value_part
    dk_ref[...] = outwide[1].astype(jnp.bfloat16)
    dv_ref[...] = outwide[2].astype(jnp.bfloat16)

    each(0, kv_copies, "wait_send")
    each(1, q_copies, "wait_send")
    each(1, do_copies, "wait_send")
    for copy in h_copies:
        copy.wait_send()


def place_outputs(dq_ref, dk_ref, dv_ref, dq_hbm, dk_hbm, dv_hbm, sem):
    copies = [
        pltpu.make_async_copy(source, target, sem.at[at])
        for at, (source, target) in enumerate(
            ((dq_ref, dq_hbm), (dk_ref, dk_hbm), (dv_ref, dv_hbm))
        )
    ]
    for copy in copies:
        copy.start()
    for copy in copies:
        copy.wait()


def fused_shards(query_rows, key_rows, value_rows, cotangent, norm_gain, offsets):
    tok, both, size = query_rows.shape
    seqs = lax.axis_size("seq")
    heads = lax.axis_size("head")
    seg1 = tok * seqs // RATE4
    far = seqs * ROWS
    flat = (both * tok, size)
    low, full = jnp.bfloat16, jnp.float32
    vmem = pl.BlockSpec(memory_space=pltpu.VMEM)
    hbm = pl.BlockSpec(memory_space=pltpu.HBM)
    outs = pl.pallas_call(
        functools.partial(fused, seqs, heads, seg1, both * size * heads),
        out_shape=[jax.ShapeDtypeStruct(flat, low)] * 3,
        in_specs=[hbm] * 6,
        out_specs=[vmem] * 3,
        scratch_shapes=[
            pltpu.SMEM((both,), jnp.int32),
            pltpu.VMEM((both, size), full),
            pltpu.VMEM((4,) + flat, low),
            pltpu.VMEM((4,) + flat, full),
            pltpu.VMEM((3, both, tok, size), low),
            pltpu.VMEM((both, size, tok), full),
            pltpu.VMEM((both, tok, tok), full),
            pltpu.VMEM((both, far, tok), full),
            pltpu.VMEM((both, tok, tok), full),
            pltpu.VMEM((both, far, tok), full),
            pltpu.VMEM((both, tok, far), full),
            pltpu.VMEM((2 * ROWS, both * tok), low),
            pltpu.VMEM((tok, both * far), low),
            pltpu.VMEM((2, 2 * ROWS, size), low),
            pltpu.VMEM((2 * ROWS, size), low),
            pltpu.VMEM((3 * ROWS, size), low),
            pltpu.VMEM((2, seqs, 2 * ROWS, size), low),
            pltpu.VMEM((seqs, 2 * ROWS, size), low),
            pltpu.VMEM((seqs, 3 * ROWS, size), low),
            pltpu.VMEM((4, tok), full),
            pltpu.VMEM((heads, 4, tok), full),
            pltpu.VMEM((8 * both, tok), full),
            pltpu.VMEM((3,) + flat, full),
            pltpu.SemaphoreType.DMA((6,)),
        ]
        + [pltpu.SemaphoreType.DMA((seqs - 1,))] * 6
        + [pltpu.SemaphoreType.DMA((heads - 1,))] * 2,
        compiler_params=pltpu.CompilerParams(
            collective_id=0, has_side_effects=True, vmem_limit_bytes=VMEM_BYTES
        ),
        name="fused_backward",
    )(
        offsets,
        query_rows.reshape(flat),
        key_rows.reshape(flat),
        value_rows.reshape(flat),
        cotangent.reshape(flat),
        norm_gain,
    )
    outs = pl.pallas_call(
        place_outputs,
        out_shape=[jax.ShapeDtypeStruct(flat, low)] * 3,
        in_specs=[vmem] * 3,
        out_specs=[hbm] * 3,
        scratch_shapes=[pltpu.SemaphoreType.DMA((3,))],
        compiler_params=pltpu.CompilerParams(vmem_limit_bytes=1024 * 1024),
        name="place_outputs",
    )(*outs)
    return tuple(out.reshape(query_rows.shape) for out in outs)


def fits(mesh, tok, both, size):
    seqs = mesh.shape["seq"]
    seg1 = tok * seqs // RATE4
    return (
        tok == ROWS * RATE3
        and size == 128
        and both == 2
        and seqs * ROWS == 128
        and (RATE3 * seg1 // tok) & (RATE3 * seg1 // tok - 1) == 0
        and tok % (RATE2 * seg1) == 0
        and (RATE3 * seg1) % tok == 0
        and tok // seg1 <= 64
    )


def solution(mesh):
    placed = (
        P("seq", "head", None),
        P("seq", "head", None),
        P("seq", "head", None),
        P("seq", "head", None),
        P("head", None),
        P("head"),
    )

    def run(query_rows, key_rows, value_rows, cotangent, norm_gain, offsets):
        tokens, heads, size = query_rows.shape
        small = fits(mesh, tokens // mesh.shape["seq"], heads // mesh.shape["head"], size)
        return jax.shard_map(
            fused_shards if small else shards,
            mesh=mesh,
            in_specs=placed,
            out_specs=(P("seq", "head", None), P("seq", "head", None), P("seq", "head", None)),
            check_vma=False,
        )(query_rows, key_rows, value_rows, cotangent, norm_gain, offsets)

    return run
```
